128 devices in a mesh: grp: 2 (over y_hi), row: 4 (over y_lo, core), col: 16 (over x, z).
Axes of the slice: x: 4, y: 4 (y_hi: 2, y_lo: 2; y = y_hi * 2 + y_lo), z: 4, core: 2. Of those that a mesh axis runs over, the one named last changes fastest.
Arguments:
- members: float32 [2, 2048, 2048], P('grp', 'row', 'col'), may hold values from -6 to 6
- control: float32 [2, 2048, 2048], P('grp', 'row', 'col'), may hold values from -6 to 6
- loc_spectrum: float32 [12], replicated, may hold values from 0.2 to 3
- pattern: int32 [48, 2], replicated, may hold values from 0 to 11
- shell_index: int32 [16, 16], replicated, may hold values from 0 to 11, as said below
Outputs:
- increment: float32 [2048, 2048], P('row', 'col')
The draws below stay inside these ranges and needn't reach their ends.
Inputs may be any that keep to these rules, and one draw needn't show every extreme that they name: `shell_index`: tile (0, 0) lies in block 0, and tile (8, 8) in block 11; blocks grow with the tile's distance from wavenumber zero, give or take one.
All inputs are finite; a program needn't handle non-finite values.
Results may differ from the reference program's by a relative error of at most 0.0003.
Values sent between devices are 32-bit elements; how exact they have to be, the bound alone decides.
No kernel may reach another device: no remote copies, remote signals or barrier semaphores. Data moves between devices by JAX's collectives and lax.ppermute only.
A program may use at most 64 MiB of HBM per device.

```python
import math
import jax
import jax.numpy as jnp
from jax import lax

N = 2048
TILE_K = 128
NBAND = 2
NPAIR = 48
MEMBERS = 2
NTILE = 16
NSHELL = 12


def draw_shell_index(key, part):
    key = jax.random.fold_in(key, 7)
    tiles = jnp.arange(NTILE, dtype=jnp.int32)
    doubled = 2 * tiles * TILE_K + TILE_K
    signed = jnp.where(doubled < N, doubled, doubled - 2 * N)
    radius_sq = signed[:, None] * signed[None, :] * 0 + signed[:, None] ** 2 + signed[None, :] ** 2
    levels = jnp.arange(1, NSHELL, dtype=jnp.int32)
    bounds = (2 * levels * TILE_K) ** 2
    base = jnp.sum((radius_sq[:, :, None] >= bounds[None, None, :]).astype(jnp.int32), axis=2)
    jitter = jax.random.randint(key, (NTILE, NTILE), -1, 2, dtype=jnp.int32)
    shells = jnp.clip(base + jitter, 0, NSHELL - 1)
    shells = shells.at[0, 0].set(0)
    shells = shells.at[NTILE // 2, NTILE // 2].set(NSHELL - 1)
    return shells.astype(jnp.int32)


def set_ends(values, rng, least, largest):
    dims = values.shape
    index_at = [jax.random.randint(jax.random.fold_in(rng, axis), (), 0, dims[axis]) for axis in range(len(dims))]
    values = values.at[tuple(index_at)].set(least)
    longest = dims.index(max(dims))
    index_at[longest] = (index_at[longest] + 1) % dims[longest]
    return values.at[tuple(index_at)].set(largest)


def block_scale(own_key, dims, pieces, least, top_value):
    def one(axis_at, blocks):
        steps = jax.random.uniform(jax.random.fold_in(jax.random.fold_in(own_key, 6), axis_at), (blocks,), jnp.float32, least / len(pieces), top_value / len(pieces))
        return jnp.repeat(jnp.exp(steps), dims[axis_at] // blocks).reshape((-1,) + (1,) * (len(dims) - axis_at - 1))

    gain = one(*pieces[0])
    for cut in pieces[1:]:
        gain = gain * one(*cut)
    return gain


def scatter_about(rng, extent, deviation, bound, shards=(), kind=jnp.bfloat16):
    factor_of = block_scale(rng, extent, shards, -0.22, 0.18) if shards else 1.0
    array = jax.random.normal(rng, extent, jnp.float32) * deviation * factor_of
    return jnp.minimum(jnp.maximum(array, -bound), bound).astype(kind)


def setup_inputs(seed: int = 0) -> dict:
    seeds = jax.random.split(jax.random.key(seed), 6)
    return {
        "members": scatter_about(seeds[0], (MEMBERS, N, N), 1.0, 6.0, ((0, 2), (1, 4), (2, 16)), jnp.float32),
        "control": scatter_about(seeds[1], (MEMBERS, N, N), 1.0, 6.0, ((0, 2), (1, 4), (2, 16)), jnp.float32),
        "loc_spectrum": jnp.clip(jnp.exp(jax.random.uniform(seeds[2], (NSHELL,), jnp.float32, math.log(0.2), math.log(3.0))), 0.2, 3.0),
        "pattern": set_ends(jax.random.randint(seeds[3], (NPAIR, 2), 0, NSHELL), jax.random.fold_in(seeds[3], 1), 0, NSHELL - 1).astype(jnp.int32),
        "shell_index": draw_shell_index(jax.random.fold_in(seeds[5], 71), 0),
    }


def band_tables(loc_spectrum, pattern):
    shells = jnp.arange(NSHELL, dtype=jnp.int32)
    band_of = shells * NBAND // NSHELL
    first_onehot = (band_of[pattern[:, 0]][:, None] == jnp.arange(NBAND, dtype=jnp.int32)[None, :]).astype(loc_spectrum.dtype)
    second_onehot = (pattern[:, 1][:, None] == shells[None, :]).astype(loc_spectrum.dtype)
    counts = jnp.dot(first_onehot.T, second_onehot, precision=lax.Precision.HIGHEST)
    return (counts * loc_spectrum[None, :], band_of)

def reference(members, control, loc_spectrum, pattern, shell_index):
    gain_tab, band_of = band_tables(loc_spectrum, pattern)
    cells = jnp.repeat(jnp.repeat(shell_index, TILE_K, axis=0), TILE_K, axis=1)
    gains = gain_tab[:, cells]
    bands = (band_of[cells][None] == jnp.arange(NBAND, dtype=jnp.int32)[:, None, None]).astype(members.dtype)

    def member_step(total, operands):
        member_field, control_field = operands
        member_hat = jnp.fft.fft2(member_field)
        control_hat = jnp.fft.fft2(control_field)
        for band in range(NBAND):
            member_band = jnp.real(jnp.fft.ifft2(bands[band] * member_hat))
            control_band = jnp.real(jnp.fft.ifft2(gains[band] * control_hat))
            total = total + member_band * control_band
        return (total, None)
    total, _ = lax.scan(member_step, jnp.zeros((N, N), members.dtype), (members, control))
    return total * (1.0 / math.sqrt(MEMBERS - 1))
```

```python
import math

import jax
import jax.numpy as jnp
import ml_dtypes
import numpy as np
from jax import lax
from jax.experimental import pallas as pl
from jax.experimental.pallas import tpu as pltpu
from jax.sharding import PartitionSpec as P

NBAND = 2
NSHELL = 12
F32 = jnp.float32
BF16 = jnp.bfloat16
C1, C2, C3 = math.cos(math.pi / 8), math.cos(math.pi / 4), math.cos(3 * math.pi / 8)
LIMIT = 48 * 1024 * 1024


def split_table(table):
    high = table.astype(ml_dtypes.bfloat16)
    low = (table - high.astype(np.float64)).astype(ml_dtypes.bfloat16)
    return high, low


def rows_tables():
    j = np.arange(128)
    full_f, full_i, half_f, half_i = [], [], [], []
    scale = 1.0 / (2048.0 * 2048.0)

    def interleave(real_part, imag_part):
        chunks = real_part.shape[0] // 16
        stacked = np.stack([real_part.reshape(chunks, 16, -1), imag_part.reshape(chunks, 16, -1)], axis=1)
        return stacked.reshape(chunks * 32, -1)

    for s in range(1, 8):
        t = np.arange(128)
        theta = 2 * np.pi * (((s + 16 * t)[:, None] * j[None, :]) % 2048) / 2048
        cos, sin = np.cos(theta), np.sin(theta)
        full_f.append(interleave(np.concatenate([cos, sin], 1), np.concatenate([-sin, cos], 1)))
        full_i.append(2 * scale * interleave(np.concatenate([cos, sin], 1), np.concatenate([-sin, cos], 1)).T)
    for s in (0, 8):
        t = np.arange(64)
        theta = 2 * np.pi * (((s + 16 * t)[:, None] * j[None, :]) % 2048) / 2048
        cos, sin = np.cos(theta), -np.sin(theta)
        weight = np.full((64, 1), 2.0)
        if s == 0:
            sin[0] = 1.0 - 2.0 * (j % 2)
            weight[0] = 1.0
        half_f.append(interleave(cos, sin))
        half_i.append(scale * interleave(weight * cos, weight * sin).T)
    return np.stack(full_f), np.stack(half_f), np.stack(full_i), np.stack(half_i)


def cols_tables():
    j = np.arange(128)
    theta = 2 * np.pi * ((j[:, None] * j[None, :]) % 128) / 128
    cos, sin = np.cos(theta), np.sin(theta)
    forward = np.block([[cos, -sin], [sin, cos]])
    inverse = np.block([[cos, sin], [-sin, cos]])
    angle = 2 * np.pi * (np.arange(16)[:, None] * j[None, :]) / 2048
    twiddle = np.stack([np.cos(angle), -np.sin(angle)], axis=1).astype(np.float32)
    return forward, inverse, twiddle


def split_value(value):
    high = value.astype(BF16)
    return high, (value - high.astype(F32)).astype(BF16)


def mxu(a, b):
    return jnp.dot(a, b, preferred_element_type=F32)


def table_times(high, low, value):
    v_high, v_low = split_value(value)
    wide = mxu(high, jnp.concatenate([v_high, v_low], axis=1))
    return wide[:, :128] + wide[:, 128:] + mxu(low, v_high)


def times_table(value, high, low):
    v_high, v_low = split_value(value)
    return mxu(v_high, high) + (mxu(v_low, high) + mxu(v_high, low))


def fft4(a, b, c, d, sign):
    s0r, s0i = a[0] + c[0], a[1] + c[1]
    s1r, s1i = a[0] - c[0], a[1] - c[1]
    s2r, s2i = b[0] + d[0], b[1] + d[1]
    s3r, s3i = b[0] - d[0], b[1] - d[1]
    rr, ri = -sign * s3i, sign * s3r
    return (
        (s0r + s2r, s0i + s2i),
        (s1r + rr, s1i + ri),
        (s0r - s2r, s0i - s2i),
        (s1r - rr, s1i - ri),
    )


def turn(z, k, sign):
    re, im = z
    k = (k * sign) % 16
    if k == 0:
        return z
    if k == 4:
        return (-im, re)
    if k == 2:
        return ((re - im) * C2, (re + im) * C2)
    if k == 14:
        return ((re + im) * C2, (im - re) * C2)
    if k == 6:
        return ((re + im) * -C2, (re - im) * C2)
    if k == 10:
        return ((im - re) * C2, (re + im) * -C2)
    cos, sin = math.cos(2 * math.pi * k / 16), math.sin(2 * math.pi * k / 16)
    return (re * cos - im * sin, re * sin + im * cos)


def fft16(z, sign):
    out = [None] * 16
    inner = [fft4(z[p], z[p + 4], z[p + 8], z[p + 12], sign) for p in range(4)]
    for k in range(4):
        outer = fft4(*[turn(inner[p][k], p * k, sign) for p in range(4)], sign)
        for q in range(4):
            out[k + 4 * q] = outer[q]
    return out


def swap_blocks(values, lane):
    low64 = lane < 64
    low32 = (lane & 32) == 0
    a0, a1, a2, a3 = values
    b0 = jnp.where(low64, a0, pltpu.roll(a2, 64, 1))
    b2 = jnp.where(low64, pltpu.roll(a0, 64, 1), a2)
    b1 = jnp.where(low64, a1, pltpu.roll(a3, 64, 1))
    b3 = jnp.where(low64, pltpu.roll(a1, 64, 1), a3)
    c0 = jnp.where(low32, b0, pltpu.roll(b1, 32, 1))
    c1 = jnp.where(low32, pltpu.roll(b0, 96, 1), b1)
    c2 = jnp.where(low32, b2, pltpu.roll(b3, 32, 1))
    c3 = jnp.where(low32, pltpu.roll(b2, 96, 1), b3)
    return c0, c1, c2, c3


def rows_forward(place, members, control, received, full_h, full_l, half_h, half_l, out, z_full, z_half):
    row = place[0]
    first = (row & 1) == 0
    flip = jnp.where((row >> 1) == 0, 1.0, -1.0).astype(F32)
    for slab in range(16):
        x = []
        for m in range(8):
            at = pl.ds((m % 4) * 128 + slab * 8, 8)
            own = jnp.where(first, members[at, :], control[at, :])
            own_here = first if m < 4 else jnp.logical_not(first)
            x.append(jnp.where(own_here, own, received[at, :]))
        e = [x[m] + x[m + 4] for m in range(4)]
        d = [x[m] - x[m + 4] for m in range(4)]
        e02, e13 = e[0] + e[2], e[1] + e[3]
        minus, plus = (d[1] - d[3]) * C2, (d[1] + d[3]) * C2
        a = [None] + [(x[m] - x[8 - m]) * flip for m in range(1, 4)]
        b = [None] + [(x[m] + x[8 - m]) * flip for m in range(1, 4)]
        x0, x4 = x[0] * flip, x[4] * flip
        even, odd = x0 + a[2] * C2, x0 - a[2] * C2
        p1, p3 = a[1] * C1 + a[3] * C3, a[1] * C3 - a[3] * C1
        i_even, i_odd = x4 + b[2] * C2, b[2] * C2 - x4
        q1, q3 = b[1] * C3 + b[3] * C1, b[1] * C1 - b[3] * C3
        rows = pl.ds(slab * 8, 8)
        shifted = pl.ds(128 + slab * 8, 8)
        z_half[0, rows, :] = e02 + e13
        z_half[1, rows, :] = e02 - e13
        values = {
            1: (even + p1, -(i_even + q1)),
            2: (d[0] + minus, -(d[2] + plus)),
            3: (odd + p3, -(i_odd + q3)),
            4: (e[0] - e[2], e[3] - e[1]),
            5: (odd - p3, i_odd - q3),
            6: (d[0] - minus, d[2] - plus),
            7: (even - p1, i_even - q1),
        }
        for s, (re, im) in values.items():
            z_full[s - 1, rows, :] = re
            z_full[s - 1, shifted, :] = im
    for s in range(7):
        out[pl.ds(256 * s, 256), :] = table_times(full_h[s], full_l[s], z_full[s])
    for s in range(2):
        out[pl.ds(1792 + 128 * s, 128), :] = table_times(half_h[s], half_l[s], z_half[s])


def gain_tables(place, pattern, loc, shell_index, straight, mirrored):
    chunk = place[1]
    general = chunk < 56
    s = jnp.where(general, (chunk >> 3) + 1, jnp.where(chunk < 60, 0, 8))
    u = jnp.where(general, chunk & 7, (chunk - 56) & 3)
    special = chunk == 56
    pairs = pattern[...]
    shell_lane = lax.broadcasted_iota(jnp.int32, (pairs.shape[0], NSHELL), 1)
    hits = pairs[:, 1:2] == shell_lane
    second = pairs[:, 0:1] * NBAND >= NSHELL
    shells = shell_index[...]
    loc_row = loc[...]
    filters = []
    in_second = shells * NBAND >= NSHELL
    filters.append(jnp.where(in_second, 0.0, 1.0).astype(F32))
    filters.append(jnp.where(in_second, 1.0, 0.0).astype(F32))
    for band in range(NBAND):
        chosen = second if band else jnp.logical_not(second)
        counts = jnp.sum(jnp.where(jnp.logical_and(hits, chosen), 1.0, 0.0).astype(F32), axis=0, keepdims=True)
        tab = counts * loc_row
        gain = jnp.zeros(shells.shape, F32)
        for shell in range(NSHELL):
            gain = jnp.where(shells == shell, tab[:, shell : shell + 1], gain)
        filters.append(gain)
    i = lax.broadcasted_iota(jnp.int32, (16, 16), 0)
    a = lax.broadcasted_iota(jnp.int32, (16, 16), 1)
    t = 16 * u + i
    tile = t >> 3
    negated = jnp.where(s == 0, ((128 - t) & 127) >> 3, 15 - tile)
    pick = (a == tile, a == negated)
    swap_row = jnp.logical_and(special, i == 0)
    partner = tuple(a == jnp.where(swap_row, 8, chosen) for chosen in (tile, negated))
    lane = lax.broadcasted_iota(jnp.int32, (16, 128), 1)
    tile_row = lax.broadcasted_iota(jnp.int32, (16, 128), 0)
    spread = tile_row == (lane >> 3)
    spread_neg = (tile_row == (((128 - lane) & 127) >> 3), tile_row == 15 - (lane >> 3))

    def as_f32(mask):
        return jnp.where(mask, 1.0, 0.0).astype(F32)

    def dot(x, y):
        return jnp.dot(x, y, preferred_element_type=F32, precision=lax.Precision.HIGHEST)

    choose = jnp.concatenate([as_f32(m) for m in pick + partner], axis=0)
    widen = jnp.concatenate([as_f32(m) for m in (spread,) + spread_neg], axis=1)
    for f in range(2 * NBAND):
        wide = dot(dot(choose, filters[f]), widen)
        for kind in range(2):
            at = slice(128 + 128 * kind, 256 + 128 * kind)
            here = 0.5 * (wide[0:16, :128] + wide[16:32, at])
            other = 0.5 * (wide[32:48, :128] + wide[48:64, at])
            straight[kind, f] = 0.5 * (here + other)
            mirrored[kind, f] = (0.5 * (here - other))[0:8]


def cols_filter(received, straight, mirrored, twiddle, fwd_h, fwd_l, inv_h, inv_l, out, z, y, v):
    tw = [(twiddle[s, 0:1, :], twiddle[s, 1:2, :]) for s in range(16)]

    def put(s, field, at, zr, zi):
        wr, wi = tw[s]
        z[s, field, at, 0:128] = zr * wr - zi * wi
        z[s, field, at, 128:256] = zr * wi + zi * wr

    for field in range(2):
        for half in range(2):
            re_at, im_at = pl.ds(8 * half, 8), pl.ds(16 + 8 * half, 8)
            values = []
            for c in range(16):
                one, two = field * 16 + c, (field + 2) * 16 + c
                values.append(
                    (received[one, re_at, :] + received[two, re_at, :], received[one, im_at, :] + received[two, im_at, :])
                )
            values = fft16(values, -1)
            for s in range(16):
                put(s, field, re_at, *values[s])
                if half == 0:
                    mr, mi = values[(16 - s) % 16]
                    put(s, field, pl.ds(16, 8), mr, -mi)
    for group in range(4):
        spectrum = times_table(z[pl.ds(4 * group, 4)].reshape(4 * 2 * 24, 256), fwd_h[...], fwd_l[...])
        spectrum = spectrum.reshape(4, 2, 24, 256)
        filtered = []
        for step in range(4):
            kind = 0 if group == 0 and step == 0 else 1
            for f in range(4):
                tile = spectrum[step, f // 2]
                gain = straight[kind, f]
                mirror = mirrored[kind, f]
                gain = jnp.concatenate([gain, gain], axis=1)
                mirror = jnp.concatenate([mirror, mirror], axis=1)
                top = gain[0:8] * tile[0:8] + mirror * tile[16:24]
                filtered.append(jnp.concatenate([top, gain[8:16] * tile[8:16]], axis=0))
        filtered = jnp.concatenate(filtered, axis=0)
        back = times_table(filtered, inv_h[...], inv_l[...])
        y[pl.ds(4 * group, 4)] = back.reshape(4, 4, 16, 256)
    lane = lax.broadcasted_iota(jnp.int32, (8, 128), 1)
    for half in range(2):
        at = pl.ds(8 * half, 8)
        for f in range(4):
            values = []
            for s in range(16):
                re, im = y[s, f, at, 0:128], y[s, f, at, 128:256]
                wr, wi = tw[s]
                values.append((re * wr + im * wi, im * wr - re * wi))
            values = fft16(values, 1)
            for c in range(16):
                v[f, c, 0] = values[c][0]
                v[f, c, 1] = values[c][1]
        for c in range(16):
            for part in range(2):
                moved = swap_blocks([v[f, c, part] for f in range(4)], lane)
                for r in range(4):
                    out[r * 16 + c, pl.ds(16 * part + 8 * half, 8), :] = moved[r]


def rows_inverse(received, full_h, full_l, half_h, half_l, out, z_full, z_half):
    for s in range(7):
        z_full[s] = table_times(full_h[s], full_l[s], received[pl.ds(256 * s, 256), :])
    for s in range(2):
        z_half[s] = table_times(half_h[s], half_l[s], received[pl.ds(1792 + 128 * s, 128), :])
    lane = lax.broadcasted_iota(jnp.int32, (8, 128), 1)
    block = lane >> 5
    for slab in range(16):
        rows, shifted = pl.ds(slab * 8, 8), pl.ds(128 + slab * 8, 8)
        y0, y8 = z_half[0, rows, :], z_half[1, rows, :]
        a = [None] + [z_full[s, rows, :] for s in range(7)]
        b = [None] + [z_full[s, shifted, :] for s in range(7)]
        plus, minus = y0 + y8, y0 - y8
        a26, turned = a[2] + a[6], (a[2] - a[6]) * C2
        c_even = [plus + a26 + a[4], minus + turned, plus - a[4], minus - turned, plus - a26 + a[4]]
        p, q, r, t = a[1] - a[7], a[3] - a[5], a[1] + a[7], a[3] + a[5]
        c_odd = [r + t, p * C1 + q * C3, (r - t) * C2, p * C3 - q * C1, None]
        b17, b35, b26 = b[1] + b[7], b[3] + b[5], (b[2] + b[6]) * C2
        d17, d35 = b[1] - b[7], b[3] - b[5]
        s_odd = [None, b17 * C3 + b35 * C1, (d17 + d35) * C2, b17 * C1 - b35 * C3, d17 - d35]
        s_even = [None, b26 + b[4], b[2] - b[6], b26 - b[4], None]
        x = [None] * 16
        for m in range(5):
            if m == 0:
                x[0], x[8] = c_even[0] + c_odd[0], c_even[0] - c_odd[0]
            elif m == 4:
                x[4], x[12] = c_even[4] - s_odd[4], c_even[4] + s_odd[4]
            else:
                c_near, c_far = c_even[m] + c_odd[m], c_even[m] - c_odd[m]
                s_near, s_far = s_odd[m] + s_even[m], s_odd[m] - s_even[m]
                x[m], x[16 - m] = c_near - s_near, c_near + s_near
                x[8 - m], x[8 + m] = c_far - s_far, c_far + s_far
        total = []
        for m in range(16):
            product = x[m] * pltpu.roll(x[m], 64, 1)
            total.append(product + pltpu.roll(product, 32, 1))
        for dest in range(4):
            packed = total[4 * dest]
            for k in range(1, 4):
                packed = jnp.where(block == k, total[4 * dest + k], packed)
            out[dest, rows, :] = packed
            out[4 + dest, rows, :] = packed


def assemble(received, out):
    lane = lax.broadcasted_iota(jnp.int32, (8, 128), 1)
    for slab in range(16):
        rows = pl.ds(slab * 8, 8)
        moved = swap_blocks([received[r, rows, :] + received[4 + r, rows, :] for r in range(4)], lane)
        for m in range(4):
            out[pl.ds(128 * m + slab * 8, 8), :] = moved[m]


def in_vmem(count):
    return [pl.BlockSpec(memory_space=pltpu.VMEM)] * count


def in_smem():
    return [pl.BlockSpec(memory_space=pltpu.SMEM)]


def params():
    return pltpu.CompilerParams(vmem_limit_bytes=LIMIT)


def shape(*dims):
    return jax.ShapeDtypeStruct(dims, F32)


def on_device(members, control, loc_spectrum, pattern, shell_index):
    row, col = lax.axis_index("row"), lax.axis_index("col")
    place = jnp.stack([row, row * 16 + col]).astype(jnp.int32)
    full_f, half_f, full_i, half_i = [split_table(t) for t in rows_tables()]
    fwd, inv, twiddle = cols_tables()
    fwd, inv = split_table(fwd), split_table(inv)
    members = members.reshape(512, 128)
    control = control.reshape(512, 128)
    send = jnp.where((row & 1) == 0, control, members)
    received = lax.ppermute(send, "row", [(0, 1), (1, 0), (2, 3), (3, 2)])
    straight, mirrored = pl.pallas_call(
        gain_tables,
        out_shape=(shape(2, 4, 16, 128), shape(2, 4, 8, 128)),
        in_specs=in_smem() + in_vmem(3),
        out_specs=tuple(in_vmem(2)),
        compiler_params=params(),
        name="gain_tables",
    )(place, pattern, loc_spectrum.reshape(1, NSHELL), shell_index)
    spectra = pl.pallas_call(
        rows_forward,
        out_shape=shape(2048, 128),
        in_specs=in_smem() + in_vmem(7),
        out_specs=in_vmem(1)[0],
        scratch_shapes=[pltpu.VMEM((7, 256, 128), F32), pltpu.VMEM((2, 128, 128), F32)],
        compiler_params=params(),
        name="rows_forward",
    )(place, members, control, received, *full_f, *half_f)
    spectra = lax.all_to_all(spectra.reshape(64, 32, 128), ("row", "col"), split_axis=0, concat_axis=0, tiled=True)
    filtered = pl.pallas_call(
        cols_filter,
        out_shape=shape(64, 32, 128),
        in_specs=in_vmem(8),
        out_specs=in_vmem(1)[0],
        scratch_shapes=[
            pltpu.VMEM((16, 2, 24, 256), F32),
            pltpu.VMEM((16, 4, 16, 256), F32),
            pltpu.VMEM((4, 16, 2, 8, 128), F32),
        ],
        compiler_params=params(),
        name="cols_filter",
    )(spectra, straight, mirrored, twiddle, *fwd, *inv)
    filtered = lax.all_to_all(filtered, ("row", "col"), split_axis=0, concat_axis=0, tiled=True)
    products = pl.pallas_call(
        rows_inverse,
        out_shape=shape(8, 128, 128),
        in_specs=in_vmem(5),
        out_specs=in_vmem(1)[0],
        scratch_shapes=[pltpu.VMEM((7, 256, 128), F32), pltpu.VMEM((2, 128, 128), F32)],
        compiler_params=params(),
        name="rows_inverse",
    )(filtered.reshape(2048, 128), *full_i, *half_i)
    products = lax.all_to_all(products, ("grp", "row"), split_axis=0, concat_axis=0, tiled=True)
    return pl.pallas_call(
        assemble,
        out_shape=shape(512, 128),
        in_specs=in_vmem(1),
        out_specs=in_vmem(1)[0],
        compiler_params=params(),
        name="assemble",
    )(products)


def solution(mesh):
    placed = (P("grp", "row", "col"), P("grp", "row", "col"), P(), P(), P())
    return jax.shard_map(
        on_device, mesh=mesh, in_specs=placed, out_specs=P("row", "col"), check_vma=False
    )
```

```python
import math

import jax
import jax.numpy as jnp
import ml_dtypes
import numpy as np
from jax import lax
from jax.experimental import pallas as pl
from jax.experimental.pallas import tpu as pltpu
from jax.sharding import PartitionSpec as P

NBAND = 2
NSHELL = 12
F32 = jnp.float32
BF16 = jnp.bfloat16
C1, C2, C3 = math.cos(math.pi / 8), math.cos(math.pi / 4), math.cos(3 * math.pi / 8)
LIMIT = 48 * 1024 * 1024
SCALE = 1.0 / (2048.0 * 2048.0)


def split_table(table):
    high = table.astype(ml_dtypes.bfloat16)
    low = (table - high.astype(np.float64)).astype(ml_dtypes.bfloat16)
    return high, low


def rows_tables():
    j = np.arange(128)
    t = np.arange(64)
    forward, inverse = [], []

    def interleave(real_part, imag_part):
        stacked = np.stack([real_part.reshape(4, 16, 128), imag_part.reshape(4, 16, 128)], axis=1)
        return stacked.reshape(128, 128)

    for s in (0, 8):
        theta = 2 * np.pi * (((s + 16 * t)[:, None] * j[None, :]) % 2048) / 2048
        cos, sin = np.cos(theta), -np.sin(theta)
        weight = np.full((64, 1), 2.0)
        if s == 0:
            sin[0] = 1.0 - 2.0 * (j % 2)
            weight[0] = 1.0
        forward.append(interleave(cos, sin))
        inverse.append(SCALE * interleave(weight * cos, weight * sin).T)
    return np.stack(forward), np.stack(inverse)


def cols_tables():
    j = np.arange(128)
    theta = 2 * np.pi * ((j[:, None] * j[None, :]) % 128) / 128
    cos, sin = np.cos(theta), np.sin(theta)
    forward = np.block([[cos, -sin], [sin, cos]])
    inverse = np.block([[cos, sin], [-sin, cos]])
    angle = 2 * np.pi * (np.arange(16)[:, None] * j[None, :]) / 2048
    twiddle = np.stack([np.cos(angle), -np.sin(angle)], axis=1).astype(np.float32)
    column = np.concatenate([np.cos(angle[:8]), np.sin(angle[:8])], axis=0).T
    return forward, inverse, twiddle, column


def split_value(value):
    high = value.astype(BF16)
    return high, (value - high.astype(F32)).astype(BF16)


def mxu(a, b):
    return jnp.dot(a, b, preferred_element_type=F32)


def table_times(both, value):
    v_high, v_low = split_value(value)
    rows = both.shape[0] // 2
    first = mxu(both, v_high)
    return first[:rows] + (first[rows:] + mxu(both[:rows], v_low))


def times_table(value, both):
    v_high, v_low = split_value(value)
    high, low = both[:256], both[256:]
    return mxu(v_high, high) + (mxu(v_low, high) + mxu(v_high, low))


def fft4(a, b, c, d, sign):
    s0r, s0i = a[0] + c[0], a[1] + c[1]
    s1r, s1i = a[0] - c[0], a[1] - c[1]
    s2r, s2i = b[0] + d[0], b[1] + d[1]
    s3r, s3i = b[0] - d[0], b[1] - d[1]
    rr, ri = -sign * s3i, sign * s3r
    return (
        (s0r + s2r, s0i + s2i),
        (s1r + rr, s1i + ri),
        (s0r - s2r, s0i - s2i),
        (s1r - rr, s1i - ri),
    )


def turn(z, k, sign):
    re, im = z
    k = (k * sign) % 16
    if k == 0:
        return z
    if k == 4:
        return (-im, re)
    if k == 2:
        return ((re - im) * C2, (re + im) * C2)
    if k == 14:
        return ((re + im) * C2, (im - re) * C2)
    if k == 6:
        return ((re + im) * -C2, (re - im) * C2)
    if k == 10:
        return ((im - re) * C2, (re + im) * -C2)
    cos, sin = math.cos(2 * math.pi * k / 16), math.sin(2 * math.pi * k / 16)
    return (re * cos - im * sin, re * sin + im * cos)


def fft16(z, sign):
    out = [None] * 16
    inner = [fft4(z[p], z[p + 4], z[p + 8], z[p + 12], sign) for p in range(4)]
    for k in range(4):
        outer = fft4(*[turn(inner[p][k], p * k, sign) for p in range(4)], sign)
        for q in range(4):
            out[k + 4 * q] = outer[q]
    return out


def swap_blocks(values, lane):
    values = list(values)
    low = lane < 64
    for i in range(4):
        one, two = values[i], values[i + 4]
        moved = pltpu.roll(jnp.where(low, two, one), 64, 1)
        values[i], values[i + 4] = jnp.where(low, one, moved), jnp.where(low, moved, two)
    for d in (2, 1):
        low = (lane & (16 * d)) == 0
        for i in range(8):
            if i & d:
                continue
            one, two = values[i], values[i + d]
            values[i] = jnp.where(low, one, pltpu.roll(two, 16 * d, 1))
            values[i + d] = jnp.where(low, pltpu.roll(one, 128 - 16 * d, 1), two)
    return values


def rows_forward(own, got_members, got_control, tables, columns, out, z_full, z_half):
    row = lax.axis_index("row")
    first = (row & 1) == 0
    flip = jnp.where((row >> 1) == 0, 1.0, -1.0).astype(F32)
    for slab in range(16):
        x = []
        for m in range(8):
            at = pl.ds((m % 4) * 128 + slab * 8, 8)
            if m < 4:
                x.append(jnp.where(first, own[at, :], got_control[at, :]))
            else:
                x.append(jnp.where(first, got_members[at, :], own[at, :]))
        e = [x[m] + x[m + 4] for m in range(4)]
        d = [x[m] - x[m + 4] for m in range(4)]
        e02, e13 = e[0] + e[2], e[1] + e[3]
        minus, plus = (d[1] - d[3]) * C2, (d[1] + d[3]) * C2
        a = [None] + [(x[m] - x[8 - m]) * flip for m in range(1, 4)]
        b = [None] + [(x[m] + x[8 - m]) * flip for m in range(1, 4)]
        x0, x4 = x[0] * flip, x[4] * flip
        even, odd = x0 + a[2] * C2, x0 - a[2] * C2
        p1, p3 = a[1] * C1 + a[3] * C3, a[1] * C3 - a[3] * C1
        i_even, i_odd = x4 + b[2] * C2, b[2] * C2 - x4
        q1, q3 = b[1] * C3 + b[3] * C1, b[1] * C1 - b[3] * C3
        rows = pl.ds(slab * 8, 8)
        shifted = pl.ds(128 + slab * 8, 8)
        z_half[0, rows, :] = e02 + e13
        z_half[1, rows, :] = e02 - e13
        values = {
            1: (even + p1, -(i_even + q1)),
            2: (d[0] + minus, -(d[2] + plus)),
            3: (odd + p3, -(i_odd + q3)),
            4: (e[0] - e[2], e[3] - e[1]),
            5: (odd - p3, i_odd - q3),
            6: (d[0] - minus, d[2] - plus),
            7: (even - p1, i_even - q1),
        }
        turns = columns[rows, 0:16]
        for s, (re, im) in values.items():
            cos, sin = turns[:, s : s + 1], turns[:, 8 + s : 9 + s]
            lanes = pl.ds(128 * (s - 1), 128)
            z_full[rows, lanes] = re * cos + im * sin
            z_full[shifted, lanes] = im * cos - re * sin
    for pair in range(4):
        width = 256 if pair < 3 else 128
        result = table_times(tables[0:512, :], z_full[:, 256 * pair : 256 * pair + width])
        for k in range(width // 128):
            at = 256 * (2 * pair + k)
            lanes = slice(128 * k, 128 * k + 128)
            for u in range(8):
                out[pl.ds(at + 32 * u, 16), :] = result[16 * u : 16 * u + 16, lanes]
                out[pl.ds(at + 32 * u + 16, 16), :] = result[128 + 16 * u : 144 + 16 * u, lanes]
    for s in range(2):
        out[pl.ds(1792 + 128 * s, 128), :] = table_times(tables[1024:1280, 128 * s : 128 * s + 128], z_half[s])


def front(members, control, tables, columns, pattern, loc, shell_index, own, tables_v, columns_v, straight, mirrored,
          pairs_v, loc_v, shells_v, sems):
    row, col = lax.axis_index("row"), lax.axis_index("col")
    first = (row & 1) == 0
    field = pltpu.make_async_copy(members, own, sems.at[0])
    small = [
        pltpu.make_async_copy(pattern, pairs_v, sems.at[3]),
        pltpu.make_async_copy(loc, loc_v, sems.at[4]),
        pltpu.make_async_copy(shell_index, shells_v, sems.at[5]),
    ]
    large = [
        pltpu.make_async_copy(tables, tables_v, sems.at[1]),
        pltpu.make_async_copy(columns, columns_v, sems.at[2]),
    ]
    for copy in small:
        copy.start()

    @pl.when(first)
    def _():
        field.start()

    @pl.when(jnp.logical_not(first))
    def _():
        pltpu.make_async_copy(control, own, sems.at[0]).start()

    for copy in large:
        copy.start()
    for copy in small:
        copy.wait()
    chunk = row * 16 + col
    general = chunk < 56
    s = jnp.where(general, (chunk >> 3) + 1, jnp.where(chunk < 60, 0, 8))
    u = jnp.where(general, chunk & 7, (chunk - 56) & 3)
    special = chunk == 56
    from_shell, to_shell = pairs_v[0:1, :], pairs_v[1:2, :]
    hits = to_shell == lax.broadcasted_iota(jnp.int32, (NSHELL, to_shell.shape[1]), 0)
    second = from_shell * NBAND >= NSHELL
    shells = shells_v[...]
    in_second = shells * NBAND >= NSHELL
    filters = [jnp.where(in_second, 0.0, 1.0).astype(F32), jnp.where(in_second, 1.0, 0.0).astype(F32)]
    for band in range(NBAND):
        chosen = second if band else jnp.logical_not(second)
        counts = jnp.sum(jnp.where(jnp.logical_and(hits, chosen), 1.0, 0.0).astype(F32), axis=1, keepdims=True)
        gain = jnp.zeros(shells.shape, F32)
        for shell in range(NSHELL):
            gain = jnp.where(shells == shell, counts[shell : shell + 1, :] * loc_v[:, shell : shell + 1], gain)
        filters.append(gain)
    i = lax.broadcasted_iota(jnp.int32, (16, 16), 0)
    a = lax.broadcasted_iota(jnp.int32, (16, 16), 1)
    t = 16 * u + i
    tile = t >> 3
    negated = jnp.where(s == 0, ((128 - t) & 127) >> 3, 15 - tile)
    pick = (a == tile, a == negated)
    swap_row = jnp.logical_and(special, i == 0)
    partner = tuple(a == jnp.where(swap_row, 8, chosen) for chosen in (tile, negated))
    lane = lax.broadcasted_iota(jnp.int32, (16, 128), 1)
    tile_row = lax.broadcasted_iota(jnp.int32, (16, 128), 0)
    spread = tile_row == (lane >> 3)
    spread_neg = (tile_row == (((128 - lane) & 127) >> 3), tile_row == 15 - (lane >> 3))

    def as_f32(mask):
        return jnp.where(mask, 1.0, 0.0).astype(F32)

    def dot(x, y):
        return jnp.dot(x, y, preferred_element_type=F32, precision=lax.Precision.HIGHEST)

    choose = jnp.concatenate([as_f32(m) for m in pick + partner], axis=0)
    widen = jnp.concatenate([as_f32(m) for m in (spread,) + spread_neg], axis=1)
    for f in range(2 * NBAND):
        wide = dot(dot(choose, filters[f]), widen)
        for kind in range(2):
            at = slice(128 + 128 * kind, 256 + 128 * kind)
            here = 0.5 * (wide[0:16, :128] + wide[16:32, at])
            other = 0.5 * (wide[32:48, :128] + wide[48:64, at])
            straight[kind, f] = 0.5 * (here + other)
            mirrored[kind, f] = (0.5 * (here - other))[0:8]
    field.wait()
    for copy in large:
        copy.wait()


def cols_filter(received, straight, mirrored, tables, columns, out, z, y, v):
    tw = [(columns[128 + s : 129 + s, :], columns[144 + s : 145 + s, :]) for s in range(16)]

    def put(s, field, at, zr, zi):
        wr, wi = tw[s]
        z[s, field, at, 0:128] = zr * wr - zi * wi
        z[s, field, at, 128:256] = zr * wi + zi * wr

    for field in range(2):
        for half in range(2):
            re_at, im_at = pl.ds(8 * half, 8), pl.ds(16 + 8 * half, 8)
            values = []
            for c in range(16):
                one, two = field * 16 + c, (field + 2) * 16 + c
                values.append(
                    (received[one, re_at, :] + received[two, re_at, :], received[one, im_at, :] + received[two, im_at, :])
                )
            values = fft16(values, -1)
            for s in range(16):
                put(s, field, re_at, *values[s])
                if half == 0:
                    mr, mi = values[(16 - s) % 16]
                    put(s, field, pl.ds(16, 8), mr, -mi)
    for group in range(4):
        spectrum = times_table(z[pl.ds(4 * group, 4)].reshape(4 * 2 * 24, 256), tables[512:1024, :])
        spectrum = spectrum.reshape(4, 2, 24, 256)
        filtered = []
        for step in range(4):
            kind = 0 if group == 0 and step == 0 else 1
            for f in range(4):
                tile = spectrum[step, f // 2]
                gain = straight[kind, f]
                mirror = mirrored[kind, f]
                gain = jnp.concatenate([gain, gain], axis=1)
                mirror = jnp.concatenate([mirror, mirror], axis=1)
                top = gain[0:8] * tile[0:8] + mirror * tile[16:24]
                filtered.append(jnp.concatenate([top, gain[8:16] * tile[8:16]], axis=0))
        filtered = jnp.concatenate(filtered, axis=0)
        back = times_table(filtered, tables[0:512, :])
        y[pl.ds(4 * group, 4)] = back.reshape(4, 4, 16, 256)
    lane = lax.broadcasted_iota(jnp.int32, (8, 128), 1)
    for half in range(2):
        at = pl.ds(8 * half, 8)
        for f in range(4):
            values = []
            for s in range(16):
                re, im = y[s, f, at, 0:128], y[s, f, at, 128:256]
                wr, wi = tw[s]
                values.append((re * wr + im * wi, im * wr - re * wi))
            values = fft16(values, 1)
            for c in range(16):
                v[f, c, 0] = values[c][0]
                v[f, c, 1] = values[c][1]
        for c in range(16):
            moved = swap_blocks([v[f, c, part] for f in range(4) for part in range(2)], lane)
            for q in range(8):
                out[q * 16 + c, at, :] = moved[q]


def rows_inverse(received, tables, columns, out, z_full, z_half):
    row = lax.axis_index("row")
    lane16 = lax.broadcasted_iota(jnp.int32, (16, 128), 1)
    even = (lane16 & 16) == 0

    def chunk(d):
        one, two = received[d], received[64 + d]
        re = jnp.where(even, one, pltpu.roll(two, 16, 1))
        im = jnp.where(even, pltpu.roll(one, 112, 1), two)
        return re, im

    for pair in range(4):
        spectra = []
        for s in range(2 * pair, min(2 * pair + 2, 7)):
            parts = [chunk(8 * s + u) for u in range(8)]
            spectra.append(jnp.concatenate([p[0] for p in parts] + [p[1] for p in parts], axis=0))
        result = table_times(tables[512:1024, :], jnp.concatenate(spectra, axis=1) if len(spectra) > 1 else spectra[0])
        for k in range(len(spectra)):
            z_full[2 * pair + k] = result[:, 128 * k : 128 * k + 128]
    for s in range(2):
        parts = [chunk(56 + 4 * s + u) for u in range(4)]
        z_half[s] = table_times(tables[1280:1536, 128 * s : 128 * s + 128], jnp.concatenate([p[k] for p in parts for k in range(2)], axis=0))
    lane = lax.broadcasted_iota(jnp.int32, (8, 128), 1)
    low64, low32, low16 = lane < 64, (lane & 32) == 0, (lane & 16) == 0

    def fold(one, two, low, shift):
        other = jnp.where(low, two, one)
        return jnp.where(low, one, two) + jnp.where(low, pltpu.roll(other, 128 - shift, 1), pltpu.roll(other, shift, 1))

    for slab in range(8):
        x = [fields_of(slab + 8 * h, z_full, z_half, columns) for h in range(2)]
        for dest in range(4):
            u = []
            for m in range(4 * dest, 4 * dest + 4):
                one, two = x[0][m], x[1][m]
                u.append(jnp.where(low64, one, two) * pltpu.roll(jnp.where(low64, two, one), 64, 1))
            packed = fold(fold(u[0], u[2], low32, 32), fold(u[1], u[3], low32, 32), low16, 16)
            slot = dest ^ row
            out[((slot & 1) << 1) | (slot >> 1), pl.ds(slab * 8, 8), :] = packed


def fields_of(slab, z_full, z_half, columns):
    rows, shifted = pl.ds(slab * 8, 8), pl.ds(128 + slab * 8, 8)
    y0, y8 = z_half[0, rows, :], z_half[1, rows, :]
    turns = columns[rows, 16:32]
    a, b = [None], [None]
    for s in range(1, 8):
        cos, sin = turns[:, s : s + 1], turns[:, 8 + s : 9 + s]
        re, im = z_full[s - 1, rows, :], z_full[s - 1, shifted, :]
        a.append(re * cos - im * sin)
        b.append(re * sin + im * cos)
    plus, minus = y0 + y8, y0 - y8
    a26, turned = a[2] + a[6], (a[2] - a[6]) * C2
    c_even = [plus + a26 + a[4], minus + turned, plus - a[4], minus - turned, plus - a26 + a[4]]
    p, q, r, t = a[1] - a[7], a[3] - a[5], a[1] + a[7], a[3] + a[5]
    c_odd = [r + t, p * C1 + q * C3, (r - t) * C2, p * C3 - q * C1, None]
    b17, b35, b26 = b[1] + b[7], b[3] + b[5], (b[2] + b[6]) * C2
    d17, d35 = b[1] - b[7], b[3] - b[5]
    s_odd = [None, b17 * C3 + b35 * C1, (d17 + d35) * C2, b17 * C1 - b35 * C3, d17 - d35]
    s_even = [None, b26 + b[4], b[2] - b[6], b26 - b[4], None]
    x = [None] * 16
    x[0], x[8] = c_even[0] + c_odd[0], c_even[0] - c_odd[0]
    x[4], x[12] = c_even[4] - s_odd[4], c_even[4] + s_odd[4]
    for m in range(1, 4):
        c_near, c_far = c_even[m] + c_odd[m], c_even[m] - c_odd[m]
        s_near, s_far = s_odd[m] + s_even[m], s_odd[m] - s_even[m]
        x[m], x[16 - m] = c_near - s_near, c_near + s_near
        x[8 - m], x[8 + m] = c_far - s_far, c_far + s_far
    return x


def assemble(own, by_row, by_grp, by_both, out, pieces):
    mine = lax.axis_index("grp") * 4 + lax.axis_index("row")
    for k, ref in enumerate((own, by_row, by_grp, by_both)):
        pieces[pl.ds(2 * k, 2)] = ref[...]
    lane = lax.broadcasted_iota(jnp.int32, (8, 128), 1)
    for slab in range(8):
        rows = pl.ds(slab * 8, 8)
        moved = swap_blocks([pieces[q ^ mine, rows, :] for q in range(8)], lane)
        for e in range(8):
            out[pl.ds(128 * (e & 3) + 64 * (e >> 2) + slab * 8, 8), :] = moved[e]


def in_vmem(count):
    return [pl.BlockSpec(memory_space=pltpu.VMEM)] * count


def in_hbm(*arrays):
    return [pltpu.with_memory_space_constraint(jnp.asarray(x), pltpu.HBM) for x in arrays]


def params():
    return pltpu.CompilerParams(vmem_limit_bytes=LIMIT)


def shape(*dims):
    return jax.ShapeDtypeStruct(dims, F32)


def constant_tables():
    half_f, half_i = [np.concatenate(split_table(t), axis=1) for t in rows_tables()]
    fwd, inv, twiddle, column = cols_tables()
    halves = [np.concatenate([h[0], h[1]], axis=1) for h in (half_f, half_i)]
    tables = np.concatenate([*split_table(inv), *split_table(fwd), *halves], axis=0)
    columns = np.zeros((160, 128), np.float32)
    columns[:128, 0:16] = column
    columns[:128, 16:32] = 2 * SCALE * column
    columns[128:144] = twiddle[:, 0]
    columns[144:160] = twiddle[:, 1]
    return tables, columns


def on_device(members, control, loc_spectrum, pattern, shell_index):
    tables, columns = constant_tables()
    members = members.reshape(512, 128)
    control = control.reshape(512, 128)
    swap_cores = [(0, 1), (1, 0), (2, 3), (3, 2)]
    got_members = lax.ppermute(members, "row", swap_cores)
    got_control = lax.ppermute(control, "row", swap_cores)
    own, tables, columns, straight, mirrored = pl.pallas_call(
        front,
        out_shape=(
            shape(512, 128),
            jax.ShapeDtypeStruct(tables.shape, BF16),
            shape(*columns.shape),
            shape(2, 4, 16, 128),
            shape(2, 4, 8, 128),
        ),
        in_specs=[pl.BlockSpec(memory_space=pltpu.HBM)] * 7,
        out_specs=tuple(in_vmem(5)),
        scratch_shapes=[
            pltpu.VMEM((2, pattern.shape[0]), jnp.int32),
            pltpu.VMEM((1, NSHELL), F32),
            pltpu.VMEM(shell_index.shape, jnp.int32),
            pltpu.SemaphoreType.DMA((6,)),
        ],
        compiler_params=params(),
        name="front",
    )(*in_hbm(members, control, tables, columns, pattern.T, loc_spectrum.reshape(1, NSHELL), shell_index))
    spectra = pl.pallas_call(
        rows_forward,
        out_shape=shape(2048, 128),
        in_specs=in_vmem(5),
        out_specs=in_vmem(1)[0],
        scratch_shapes=[pltpu.VMEM((256, 896), F32), pltpu.VMEM((2, 128, 128), F32)],
        compiler_params=params(),
        name="rows_forward",
    )(own, got_members, got_control, tables, columns)
    spectra = lax.all_to_all(spectra.reshape(64, 32, 128), ("row", "col"), split_axis=0, concat_axis=0, tiled=True)
    filtered = pl.pallas_call(
        cols_filter,
        out_shape=shape(128, 16, 128),
        in_specs=in_vmem(5),
        out_specs=in_vmem(1)[0],
        scratch_shapes=[
            pltpu.VMEM((16, 2, 24, 256), F32),
            pltpu.VMEM((16, 4, 16, 256), F32),
            pltpu.VMEM((4, 16, 2, 8, 128), F32),
        ],
        compiler_params=params(),
        name="cols_filter",
    )(spectra, straight, mirrored, tables, columns)
    filtered = lax.all_to_all(filtered, ("grp", "row", "col"), split_axis=0, concat_axis=0, tiled=True)
    products = pl.pallas_call(
        rows_inverse,
        out_shape=shape(4, 64, 128),
        in_specs=in_vmem(3),
        out_specs=in_vmem(1)[0],
        scratch_shapes=[pltpu.VMEM((7, 256, 128), F32), pltpu.VMEM((2, 128, 128), F32)],
        compiler_params=params(),
        name="rows_inverse",
    )(filtered, tables, columns)
    got = lax.ppermute(products[2:4], "row", swap_cores)
    near = jnp.stack([products[0], got[0]])
    far = jnp.stack([products[1], got[1]])

    def exchange(value, step):
        return lax.ppermute(value, ("grp", "row"), [(i, i ^ step) for i in range(8)])

    by_grp, by_both, by_row = exchange(near, 4), exchange(far, 6), exchange(far, 2)
    return pl.pallas_call(
        assemble,
        out_shape=shape(512, 128),
        in_specs=in_vmem(4),
        out_specs=in_vmem(1)[0],
        scratch_shapes=[pltpu.VMEM((8, 64, 128), F32)],
        compiler_params=params(),
        name="assemble",
    )(near, by_row, by_grp, by_both)


def solution(mesh):
    placed = (P("grp", "row", "col"), P("grp", "row", "col"), P(), P(), P())
    return jax.shard_map(
        on_device, mesh=mesh, in_specs=placed, out_specs=P("row", "col"), check_vma=False
    )
```

```python
import math

import jax
import jax.numpy as jnp
import ml_dtypes
import numpy as np
from jax import lax
from jax.experimental import pallas as pl
from jax.experimental.pallas import tpu as pltpu
from jax.sharding import Mesh
from jax.sharding import PartitionSpec as P

NBAND = 2
NSHELL = 12
F32 = jnp.float32
BF16 = jnp.bfloat16
C1, C2, C3 = math.cos(math.pi / 8), math.cos(math.pi / 4), math.cos(3 * math.pi / 8)
LIMIT = 48 * 1024 * 1024
SCALE = 1.0 / (2048.0 * 2048.0)


def split_table(table):
    high = table.astype(ml_dtypes.bfloat16)
    low = (table - high.astype(np.float64)).astype(ml_dtypes.bfloat16)
    return high, low


def rows_tables():
    j = np.arange(128)
    t = np.arange(64)
    forward, inverse = [], []

    def interleave(real_part, imag_part):
        stacked = np.stack([real_part.reshape(4, 16, 128), imag_part.reshape(4, 16, 128)], axis=1)
        return stacked.reshape(128, 128)

    for s in (0, 8):
        theta = 2 * np.pi * (((s + 16 * t)[:, None] * j[None, :]) % 2048) / 2048
        cos, sin = np.cos(theta), -np.sin(theta)
        weight = np.full((64, 1), 2.0)
        if s == 0:
            sin[0] = 1.0 - 2.0 * (j % 2)
            weight[0] = 1.0
        forward.append(interleave(cos, sin))
        inverse.append(SCALE * interleave(weight * cos, weight * sin).T)
    return np.stack(forward), np.stack(inverse)


def cols_tables():
    j = np.arange(128)
    theta = 2 * np.pi * ((j[:, None] * j[None, :]) % 128) / 128
    cos, sin = np.cos(theta), np.sin(theta)
    forward = np.block([[cos, -sin], [sin, cos]])
    inverse = np.block([[cos, sin], [-sin, cos]])
    angle = 2 * np.pi * (np.arange(16)[:, None] * j[None, :]) / 2048
    twiddle = np.stack([np.cos(angle), -np.sin(angle)], axis=1).astype(np.float32)
    column = np.concatenate([np.cos(angle[:8]), np.sin(angle[:8])], axis=0).T
    return forward, inverse, twiddle, column


AXES = ("grp", "ylo", "core", "x1", "x0", "z1", "z0")
FIRST = ("x1", "x0", "core", "z1", "ylo", "z0")
SECOND = ("core", "z1", "z0", "x1", "x0", "grp", "ylo")


def place_of(order, at):
    place = 0
    for axis in order:
        place = place * 2 + at[axis]
    return place


def block_at(block):
    return {"x1": block >> 3, "x0": (block >> 2) & 1, "z1": (block >> 1) & 1, "z0": block & 1}


def of_group(grp, chunk):
    at = {"grp": grp}
    for axis in reversed(FIRST):
        at[axis] = chunk & 1
        chunk >>= 1
    return place_of(SECOND, at)


def split_value(value):
    high = value.astype(BF16)
    return high, (value - high.astype(F32)).astype(BF16)


def mxu(a, b):
    return jnp.dot(a, b, preferred_element_type=F32)


def table_times(both, value):
    v_high, v_low = split_value(value)
    rows = both.shape[0] // 2
    first = mxu(both, v_high)
    return first[:rows] + (first[rows:] + mxu(both[:rows], v_low))


def times_table(value, both):
    v_high, v_low = split_value(value)
    high, low = both[:256], both[256:]
    return mxu(v_high, high) + (mxu(v_low, high) + mxu(v_high, low))


def fft4(a, b, c, d, sign):
    s0r, s0i = a[0] + c[0], a[1] + c[1]
    s1r, s1i = a[0] - c[0], a[1] - c[1]
    s2r, s2i = b[0] + d[0], b[1] + d[1]
    s3r, s3i = b[0] - d[0], b[1] - d[1]
    rr, ri = -sign * s3i, sign * s3r
    return (
        (s0r + s2r, s0i + s2i),
        (s1r + rr, s1i + ri),
        (s0r - s2r, s0i - s2i),
        (s1r - rr, s1i - ri),
    )


def turn(z, k, sign):
    re, im = z
    k = (k * sign) % 16
    if k == 0:
        return z
    if k == 4:
        return (-im, re)
    if k == 2:
        return ((re - im) * C2, (re + im) * C2)
    if k == 14:
        return ((re + im) * C2, (im - re) * C2)
    if k == 6:
        return ((re + im) * -C2, (re - im) * C2)
    if k == 10:
        return ((im - re) * C2, (re + im) * -C2)
    cos, sin = math.cos(2 * math.pi * k / 16), math.sin(2 * math.pi * k / 16)
    return (re * cos - im * sin, re * sin + im * cos)


def fft16(z, sign):
    out = [None] * 16
    inner = [fft4(z[p], z[p + 4], z[p + 8], z[p + 12], sign) for p in range(4)]
    for k in range(4):
        outer = fft4(*[turn(inner[p][k], p * k, sign) for p in range(4)], sign)
        for q in range(4):
            out[k + 4 * q] = outer[q]
    return out


def swap_blocks(values, lane):
    values = list(values)
    low = lane < 64
    for i in range(4):
        one, two = values[i], values[i + 4]
        moved = pltpu.roll(jnp.where(low, two, one), 64, 1)
        values[i], values[i + 4] = jnp.where(low, one, moved), jnp.where(low, moved, two)
    for d in (2, 1):
        low = (lane & (16 * d)) == 0
        for i in range(8):
            if i & d:
                continue
            one, two = values[i], values[i + d]
            values[i] = jnp.where(low, one, pltpu.roll(two, 16 * d, 1))
            values[i + d] = jnp.where(low, pltpu.roll(one, 128 - 16 * d, 1), two)
    return values


def rows_forward(own, got_members, got_control, tables, columns, out, z_full, z_half):
    first = lax.axis_index("core") == 0
    flip = jnp.where(lax.axis_index("ylo") == 0, 1.0, -1.0).astype(F32)
    for slab in range(16):
        x = []
        for m in range(8):
            at = pl.ds((m % 4) * 128 + slab * 8, 8)
            if m < 4:
                x.append(jnp.where(first, own[at, :], got_control[at, :]))
            else:
                x.append(jnp.where(first, got_members[at, :], own[at, :]))
        e = [x[m] + x[m + 4] for m in range(4)]
        d = [x[m] - x[m + 4] for m in range(4)]
        e02, e13 = e[0] + e[2], e[1] + e[3]
        minus, plus = (d[1] - d[3]) * C2, (d[1] + d[3]) * C2
        a = [None] + [(x[m] - x[8 - m]) * flip for m in range(1, 4)]
        b = [None] + [(x[m] + x[8 - m]) * flip for m in range(1, 4)]
        x0, x4 = x[0] * flip, x[4] * flip
        even, odd = x0 + a[2] * C2, x0 - a[2] * C2
        p1, p3 = a[1] * C1 + a[3] * C3, a[1] * C3 - a[3] * C1
        i_even, i_odd = x4 + b[2] * C2, b[2] * C2 - x4
        q1, q3 = b[1] * C3 + b[3] * C1, b[1] * C1 - b[3] * C3
        rows = pl.ds(slab * 8, 8)
        shifted = pl.ds(128 + slab * 8, 8)
        z_half[0, rows, :] = e02 + e13
        z_half[1, rows, :] = e02 - e13
        values = {
            1: (even + p1, -(i_even + q1)),
            2: (d[0] + minus, -(d[2] + plus)),
            3: (odd + p3, -(i_odd + q3)),
            4: (e[0] - e[2], e[3] - e[1]),
            5: (odd - p3, i_odd - q3),
            6: (d[0] - minus, d[2] - plus),
            7: (even - p1, i_even - q1),
        }
        turns = columns[rows, 0:16]
        for s, (re, im) in values.items():
            cos, sin = turns[:, s : s + 1], turns[:, 8 + s : 9 + s]
            lanes = pl.ds(128 * (s - 1), 128)
            z_full[rows, lanes] = re * cos + im * sin
            z_full[shifted, lanes] = im * cos - re * sin
    for pair in range(4):
        width = 256 if pair < 3 else 128
        result = table_times(tables[0:512, :], z_full[:, 256 * pair : 256 * pair + width])
        for k in range(width // 128):
            at = 256 * (2 * pair + k)
            lanes = slice(128 * k, 128 * k + 128)
            for u in range(8):
                out[pl.ds(at + 32 * u, 16), :] = result[16 * u : 16 * u + 16, lanes]
                out[pl.ds(at + 32 * u + 16, 16), :] = result[128 + 16 * u : 144 + 16 * u, lanes]
    for s in range(2):
        out[pl.ds(1792 + 128 * s, 128), :] = table_times(tables[1024:1280, 128 * s : 128 * s + 128], z_half[s])


def front(members, control, tables, columns, pattern, loc, shell_index, own, tables_v, columns_v, straight, mirrored,
          pairs_v, loc_v, shells_v, sems):
    core = lax.axis_index("core")
    first = core == 0
    field = pltpu.make_async_copy(members, own, sems.at[0])
    small = [
        pltpu.make_async_copy(pattern, pairs_v, sems.at[3]),
        pltpu.make_async_copy(loc, loc_v, sems.at[4]),
        pltpu.make_async_copy(shell_index, shells_v, sems.at[5]),
    ]
    large = [
        pltpu.make_async_copy(tables, tables_v, sems.at[1]),
        pltpu.make_async_copy(columns, columns_v, sems.at[2]),
    ]
    for copy in small:
        copy.start()

    @pl.when(first)
    def _():
        field.start()

    @pl.when(jnp.logical_not(first))
    def _():
        pltpu.make_async_copy(control, own, sems.at[0]).start()

    for copy in large:
        copy.start()
    for copy in small:
        copy.wait()
    chunk = place_of(FIRST, {axis: lax.axis_index(axis) for axis in FIRST})
    general = chunk < 56
    s = jnp.where(general, (chunk >> 3) + 1, jnp.where(chunk < 60, 0, 8))
    u = jnp.where(general, chunk & 7, (chunk - 56) & 3)
    special = chunk == 56
    from_shell, to_shell = pairs_v[0:1, :], pairs_v[1:2, :]
    hits = to_shell == lax.broadcasted_iota(jnp.int32, (NSHELL, to_shell.shape[1]), 0)
    second = from_shell * NBAND >= NSHELL
    shells = shells_v[...]
    in_second = shells * NBAND >= NSHELL
    filters = [jnp.where(in_second, 0.0, 1.0).astype(F32), jnp.where(in_second, 1.0, 0.0).astype(F32)]
    for band in range(NBAND):
        chosen = second if band else jnp.logical_not(second)
        counts = jnp.sum(jnp.where(jnp.logical_and(hits, chosen), 1.0, 0.0).astype(F32), axis=1, keepdims=True)
        gain = jnp.zeros(shells.shape, F32)
        for shell in range(NSHELL):
            gain = jnp.where(shells == shell, counts[shell : shell + 1, :] * loc_v[:, shell : shell + 1], gain)
        filters.append(gain)
    i = lax.broadcasted_iota(jnp.int32, (16, 16), 0)
    a = lax.broadcasted_iota(jnp.int32, (16, 16), 1)
    t = 16 * u + i
    tile = t >> 3
    negated = jnp.where(s == 0, ((128 - t) & 127) >> 3, 15 - tile)
    pick = (a == tile, a == negated)
    swap_row = jnp.logical_and(special, i == 0)
    partner = tuple(a == jnp.where(swap_row, 8, chosen) for chosen in (tile, negated))
    lane = lax.broadcasted_iota(jnp.int32, (16, 128), 1)
    tile_row = lax.broadcasted_iota(jnp.int32, (16, 128), 0)
    spread = tile_row == (lane >> 3)
    spread_neg = (tile_row == (((128 - lane) & 127) >> 3), tile_row == 15 - (lane >> 3))

    def as_f32(mask):
        return jnp.where(mask, 1.0, 0.0).astype(F32)

    def dot(x, y):
        return jnp.dot(x, y, preferred_element_type=F32, precision=lax.Precision.HIGHEST)

    choose = jnp.concatenate([as_f32(m) for m in pick + partner], axis=0)
    widen = jnp.concatenate([as_f32(m) for m in (spread,) + spread_neg], axis=1)
    for f in range(2 * NBAND):
        wide = dot(dot(choose, filters[f]), widen)
        for kind in range(2):
            at = slice(128 + 128 * kind, 256 + 128 * kind)
            here = 0.5 * (wide[0:16, :128] + wide[16:32, at])
            other = 0.5 * (wide[32:48, :128] + wide[48:64, at])
            straight[kind, f] = 0.5 * (here + other)
            mirrored[kind, f] = (0.5 * (here - other))[0:8]
    field.wait()
    for copy in large:
        copy.wait()


def cols_filter(received, straight, mirrored, tables, columns, out, z, y, v):
    tw = [(columns[128 + s : 129 + s, :], columns[144 + s : 145 + s, :]) for s in range(16)]

    def put(s, field, at, zr, zi):
        wr, wi = tw[s]
        z[s, field, at, 0:128] = zr * wr - zi * wi
        z[s, field, at, 128:256] = zr * wi + zi * wr

    for field in range(2):
        for half in range(2):
            re_at, im_at = pl.ds(8 * half, 8), pl.ds(16 + 8 * half, 8)
            values = []
            for c in range(16):
                one, two = [place_of(FIRST, {"ylo": ylo, "core": field, **block_at(c)}) for ylo in range(2)]
                values.append(
                    (received[one, re_at, :] + received[two, re_at, :], received[one, im_at, :] + received[two, im_at, :])
                )
            values = fft16(values, -1)
            for s in range(16):
                put(s, field, re_at, *values[s])
                if half == 0:
                    mr, mi = values[(16 - s) % 16]
                    put(s, field, pl.ds(16, 8), mr, -mi)
    for group in range(4):
        spectrum = times_table(z[pl.ds(4 * group, 4)].reshape(4 * 2 * 24, 256), tables[512:1024, :])
        spectrum = spectrum.reshape(4, 2, 24, 256)
        filtered = []
        for step in range(4):
            kind = 0 if group == 0 and step == 0 else 1
            for f in range(4):
                tile = spectrum[step, f // 2]
                gain = straight[kind, f]
                mirror = mirrored[kind, f]
                gain = jnp.concatenate([gain, gain], axis=1)
                mirror = jnp.concatenate([mirror, mirror], axis=1)
                top = gain[0:8] * tile[0:8] + mirror * tile[16:24]
                filtered.append(jnp.concatenate([top, gain[8:16] * tile[8:16]], axis=0))
        filtered = jnp.concatenate(filtered, axis=0)
        back = times_table(filtered, tables[0:512, :])
        y[pl.ds(4 * group, 4)] = back.reshape(4, 4, 16, 256)
    lane = lax.broadcasted_iota(jnp.int32, (8, 128), 1)
    for half in range(2):
        at = pl.ds(8 * half, 8)
        for f in range(4):
            values = []
            for s in range(16):
                re, im = y[s, f, at, 0:128], y[s, f, at, 128:256]
                wr, wi = tw[s]
                values.append((re * wr + im * wi, im * wr - re * wi))
            values = fft16(values, 1)
            for c in range(16):
                v[f, c, 0] = values[c][0]
                v[f, c, 1] = values[c][1]
        for c in range(16):
            moved = swap_blocks([v[f, c, part] for f in range(4) for part in range(2)], lane)
            for q in range(8):
                target = {"grp": q >> 2, "ylo": (q >> 1) & 1, "core": q & 1, **block_at(c)}
                out[place_of(SECOND, target), at, :] = moved[q]


def rows_inverse(received, tables, columns, out, z_full, z_half):
    row = lax.axis_index("ylo") * 2 + lax.axis_index("core")
    lane16 = lax.broadcasted_iota(jnp.int32, (16, 128), 1)
    even = (lane16 & 16) == 0

    def chunk(d):
        one, two = received[of_group(0, d)], received[of_group(1, d)]
        re = jnp.where(even, one, pltpu.roll(two, 16, 1))
        im = jnp.where(even, pltpu.roll(one, 112, 1), two)
        return re, im

    for pair in range(4):
        spectra = []
        for s in range(2 * pair, min(2 * pair + 2, 7)):
            parts = [chunk(8 * s + u) for u in range(8)]
            spectra.append(jnp.concatenate([p[0] for p in parts] + [p[1] for p in parts], axis=0))
        result = table_times(tables[512:1024, :], jnp.concatenate(spectra, axis=1) if len(spectra) > 1 else spectra[0])
        for k in range(len(spectra)):
            z_full[2 * pair + k] = result[:, 128 * k : 128 * k + 128]
    for s in range(2):
        parts = [chunk(56 + 4 * s + u) for u in range(4)]
        z_half[s] = table_times(tables[1280:1536, 128 * s : 128 * s + 128], jnp.concatenate([p[k] for p in parts for k in range(2)], axis=0))
    lane = lax.broadcasted_iota(jnp.int32, (8, 128), 1)
    low64, low32, low16 = lane < 64, (lane & 32) == 0, (lane & 16) == 0

    def fold(one, two, low, shift):
        other = jnp.where(low, two, one)
        return jnp.where(low, one, two) + jnp.where(low, pltpu.roll(other, 128 - shift, 1), pltpu.roll(other, shift, 1))

    for slab in range(8):
        x = [fields_of(slab + 8 * h, z_full, z_half, columns) for h in range(2)]
        for dest in range(4):
            u = []
            for m in range(4 * dest, 4 * dest + 4):
                one, two = x[0][m], x[1][m]
                u.append(jnp.where(low64, one, two) * pltpu.roll(jnp.where(low64, two, one), 64, 1))
            packed = fold(fold(u[0], u[2], low32, 32), fold(u[1], u[3], low32, 32), low16, 16)
            slot = dest ^ row
            out[((slot & 1) << 1) | (slot >> 1), pl.ds(slab * 8, 8), :] = packed


def fields_of(slab, z_full, z_half, columns):
    rows, shifted = pl.ds(slab * 8, 8), pl.ds(128 + slab * 8, 8)
    y0, y8 = z_half[0, rows, :], z_half[1, rows, :]
    turns = columns[rows, 16:32]
    a, b = [None], [None]
    for s in range(1, 8):
        cos, sin = turns[:, s : s + 1], turns[:, 8 + s : 9 + s]
        re, im = z_full[s - 1, rows, :], z_full[s - 1, shifted, :]
        a.append(re * cos - im * sin)
        b.append(re * sin + im * cos)
    plus, minus = y0 + y8, y0 - y8
    a26, turned = a[2] + a[6], (a[2] - a[6]) * C2
    c_even = [plus + a26 + a[4], minus + turned, plus - a[4], minus - turned, plus - a26 + a[4]]
    p, q, r, t = a[1] - a[7], a[3] - a[5], a[1] + a[7], a[3] + a[5]
    c_odd = [r + t, p * C1 + q * C3, (r - t) * C2, p * C3 - q * C1, None]
    b17, b35, b26 = b[1] + b[7], b[3] + b[5], (b[2] + b[6]) * C2
    d17, d35 = b[1] - b[7], b[3] - b[5]
    s_odd = [None, b17 * C3 + b35 * C1, (d17 + d35) * C2, b17 * C1 - b35 * C3, d17 - d35]
    s_even = [None, b26 + b[4], b[2] - b[6], b26 - b[4], None]
    x = [None] * 16
    x[0], x[8] = c_even[0] + c_odd[0], c_even[0] - c_odd[0]
    x[4], x[12] = c_even[4] - s_odd[4], c_even[4] + s_odd[4]
    for m in range(1, 4):
        c_near, c_far = c_even[m] + c_odd[m], c_even[m] - c_odd[m]
        s_near, s_far = s_odd[m] + s_even[m], s_odd[m] - s_even[m]
        x[m], x[16 - m] = c_near - s_near, c_near + s_near
        x[8 - m], x[8 + m] = c_far - s_far, c_far + s_far
    return x


def assemble(own, by_row, by_grp, by_both, out, pieces):
    mine = (lax.axis_index("grp") * 2 + lax.axis_index("ylo")) * 2 + lax.axis_index("core")
    for k, ref in enumerate((own, by_row, by_grp, by_both)):
        pieces[pl.ds(2 * k, 2)] = ref[...]
    lane = lax.broadcasted_iota(jnp.int32, (8, 128), 1)
    for slab in range(8):
        rows = pl.ds(slab * 8, 8)
        moved = swap_blocks([pieces[q ^ mine, rows, :] for q in range(8)], lane)
        for e in range(8):
            out[pl.ds(128 * (e & 3) + 64 * (e >> 2) + slab * 8, 8), :] = moved[e]


def in_vmem(count):
    return [pl.BlockSpec(memory_space=pltpu.VMEM)] * count


def in_hbm(*arrays):
    return [pltpu.with_memory_space_constraint(jnp.asarray(x), pltpu.HBM) for x in arrays]


def params():
    return pltpu.CompilerParams(vmem_limit_bytes=LIMIT)


def shape(*dims):
    return jax.ShapeDtypeStruct(dims, F32)


def constant_tables():
    half_f, half_i = [np.concatenate(split_table(t), axis=1) for t in rows_tables()]
    fwd, inv, twiddle, column = cols_tables()
    halves = [np.concatenate([h[0], h[1]], axis=1) for h in (half_f, half_i)]
    tables = np.concatenate([*split_table(inv), *split_table(fwd), *halves], axis=0)
    columns = np.zeros((160, 128), np.float32)
    columns[:128, 0:16] = column
    columns[:128, 16:32] = 2 * SCALE * column
    columns[128:144] = twiddle[:, 0]
    columns[144:160] = twiddle[:, 1]
    return tables, columns


def call_rows_forward(own, got_members, got_control, tables, columns):
    return pl.pallas_call(
        rows_forward,
        out_shape=shape(2048, 128),
        in_specs=in_vmem(5),
        out_specs=in_vmem(1)[0],
        scratch_shapes=[pltpu.VMEM((256, 896), F32), pltpu.VMEM((2, 128, 128), F32)],
        compiler_params=params(),
        name="rows_forward",
    )(own, got_members, got_control, tables, columns)


def call_cols_filter(spectra, straight, mirrored, tables, columns):
    return pl.pallas_call(
        cols_filter,
        out_shape=shape(128, 16, 128),
        in_specs=in_vmem(5),
        out_specs=in_vmem(1)[0],
        scratch_shapes=[
            pltpu.VMEM((16, 2, 24, 256), F32),
            pltpu.VMEM((16, 4, 16, 256), F32),
            pltpu.VMEM((4, 16, 2, 8, 128), F32),
        ],
        compiler_params=params(),
        name="cols_filter",
    )(spectra, straight, mirrored, tables, columns)


def call_rows_inverse(filtered, tables, columns):
    return pl.pallas_call(
        rows_inverse,
        out_shape=shape(4, 64, 128),
        in_specs=in_vmem(3),
        out_specs=in_vmem(1)[0],
        scratch_shapes=[pltpu.VMEM((7, 256, 128), F32), pltpu.VMEM((2, 128, 128), F32)],
        compiler_params=params(),
        name="rows_inverse",
    )(filtered, tables, columns)


def call_assemble(near, by_row, by_grp, by_both):
    return pl.pallas_call(
        assemble,
        out_shape=shape(512, 128),
        in_specs=in_vmem(4),
        out_specs=in_vmem(1)[0],
        scratch_shapes=[pltpu.VMEM((8, 64, 128), F32)],
        compiler_params=params(),
        name="assemble",
    )(near, by_row, by_grp, by_both)


def on_device(members, control, loc_spectrum, pattern, shell_index):
    tables, columns = constant_tables()
    members = members.reshape(512, 128)
    control = control.reshape(512, 128)
    swap_cores = [(0, 1), (1, 0)]
    got_members = lax.ppermute(members, "core", swap_cores)
    got_control = lax.ppermute(control, "core", swap_cores)
    own, tables, columns, straight, mirrored = pl.pallas_call(
        front,
        out_shape=(
            shape(512, 128),
            jax.ShapeDtypeStruct(tables.shape, BF16),
            shape(*columns.shape),
            shape(2, 4, 16, 128),
            shape(2, 4, 8, 128),
        ),
        in_specs=[pl.BlockSpec(memory_space=pltpu.HBM)] * 7,
        out_specs=tuple(in_vmem(5)),
        scratch_shapes=[
            pltpu.VMEM((2, pattern.shape[0]), jnp.int32),
            pltpu.VMEM((1, NSHELL), F32),
            pltpu.VMEM(shell_index.shape, jnp.int32),
            pltpu.SemaphoreType.DMA((6,)),
        ],
        compiler_params=params(),
        name="front",
    )(*in_hbm(members, control, tables, columns, pattern.T, loc_spectrum.reshape(1, NSHELL), shell_index))
    spectra = call_rows_forward(own, got_members, got_control, tables, columns)
    spectra = lax.all_to_all(spectra.reshape(64, 32, 128), FIRST, split_axis=0, concat_axis=0, tiled=True)
    filtered = call_cols_filter(spectra, straight, mirrored, tables, columns)
    filtered = lax.all_to_all(filtered, SECOND, split_axis=0, concat_axis=0, tiled=True)
    products = call_rows_inverse(filtered, tables, columns)
    got = lax.ppermute(products[2:4], "core", swap_cores)
    near = jnp.stack([products[0], got[0]])
    far = jnp.stack([products[1], got[1]])

    def exchange(value, step):
        return lax.ppermute(value, ("grp", "ylo"), [(i, i ^ step) for i in range(4)])

    by_grp, by_both, by_row = exchange(near, 2), exchange(far, 3), exchange(far, 1)
    return call_assemble(near, by_row, by_grp, by_both)


def solution(mesh):
    fine = Mesh(mesh.devices.reshape((2,) * len(AXES)), AXES)
    rows, cols = AXES[1:3], AXES[3:]
    placed = (P("grp", rows, cols), P("grp", rows, cols), P(), P(), P())
    return jax.shard_map(on_device, mesh=fine, in_specs=placed, out_specs=P(rows, cols), check_vma=False)
```

```python
import math

import jax
import jax.numpy as jnp
import ml_dtypes
import numpy as np
from jax import lax
from jax.experimental import pallas as pl
from jax.experimental.pallas import tpu as pltpu
from jax.sharding import Mesh
from jax.sharding import PartitionSpec as P

NBAND = 2
NSHELL = 12
F32 = jnp.float32
BF16 = jnp.bfloat16
C1, C2, C3 = math.cos(math.pi / 8), math.cos(math.pi / 4), math.cos(3 * math.pi / 8)
LIMIT = 48 * 1024 * 1024
GROUP = 8
SCALE = 1.0 / (2048.0 * 2048.0)


def split_table(table):
    high = table.astype(ml_dtypes.bfloat16)
    low = (table - high.astype(np.float64)).astype(ml_dtypes.bfloat16)
    return high, low


def rows_tables():
    j = np.arange(128)
    t = np.arange(64)
    forward, inverse = [], []

    def interleave(real_part, imag_part):
        stacked = np.stack([real_part.reshape(4, 16, 128), imag_part.reshape(4, 16, 128)], axis=1)
        return stacked.reshape(128, 128)

    for s in (0, 8):
        theta = 2 * np.pi * (((s + 16 * t)[:, None] * j[None, :]) % 2048) / 2048
        cos, sin = np.cos(theta), -np.sin(theta)
        weight = np.full((64, 1), 2.0)
        if s == 0:
            sin[0] = 1.0 - 2.0 * (j % 2)
            weight[0] = 1.0
        forward.append(interleave(cos, sin))
        inverse.append(SCALE * interleave(weight * cos, weight * sin).T)
    return np.stack(forward), np.stack(inverse)


def cols_tables():
    j = np.arange(128)
    theta = 2 * np.pi * ((j[:, None] * j[None, :]) % 128) / 128
    cos, sin = np.cos(theta), np.sin(theta)
    forward = np.block([[cos, -sin], [sin, cos]])
    inverse = np.block([[cos, sin], [-sin, cos]])
    angle = 2 * np.pi * (np.arange(16)[:, None] * j[None, :]) / 2048
    twiddle = np.stack([np.cos(angle), -np.sin(angle)], axis=1).astype(np.float32)
    column = np.concatenate([np.cos(angle[:8]), np.sin(angle[:8])], axis=0).T
    return forward, inverse, twiddle, column


AXES = ("grp", "ylo", "core", "x1", "x0", "z1", "z0")
FIRST = ("x1", "x0", "core", "z1", "ylo", "z0")
SECOND = ("core", "z1", "z0", "x1", "x0", "grp", "ylo")


def place_of(order, at):
    place = 0
    for axis in order:
        place = place * 2 + at[axis]
    return place


def block_at(block):
    return {"x1": block >> 3, "x0": (block >> 2) & 1, "z1": (block >> 1) & 1, "z0": block & 1}


def of_group(grp, chunk):
    at = {"grp": grp}
    for axis in reversed(FIRST):
        at[axis] = chunk & 1
        chunk >>= 1
    return place_of(SECOND, at)


def split_value(value):
    high = value.astype(BF16)
    return high, (value - high.astype(F32)).astype(BF16)


def mxu(a, b):
    return jnp.dot(a, b, preferred_element_type=F32)


def table_times(both, value):
    v_high, v_low = split_value(value)
    rows = both.shape[0] // 2
    high, low = both[:rows], both[rows:]
    return mxu(jnp.concatenate([high, high, low], axis=1), jnp.concatenate([v_high, v_low, v_high], axis=0))


def times_table(value, both):
    v_high, v_low = split_value(value)
    high, low = both[:256], both[256:]
    return mxu(jnp.concatenate([v_high, v_low, v_high], axis=1), jnp.concatenate([high, high, low], axis=0))


def fft4(a, b, c, d, sign):
    s0r, s0i = a[0] + c[0], a[1] + c[1]
    s1r, s1i = a[0] - c[0], a[1] - c[1]
    s2r, s2i = b[0] + d[0], b[1] + d[1]
    s3r, s3i = b[0] - d[0], b[1] - d[1]
    rr, ri = -sign * s3i, sign * s3r
    return (
        (s0r + s2r, s0i + s2i),
        (s1r + rr, s1i + ri),
        (s0r - s2r, s0i - s2i),
        (s1r - rr, s1i - ri),
    )


def turn(z, k, sign):
    re, im = z
    k = (k * sign) % 16
    if k == 0:
        return z
    if k == 4:
        return (-im, re)
    if k == 2:
        return ((re - im) * C2, (re + im) * C2)
    if k == 14:
        return ((re + im) * C2, (im - re) * C2)
    if k == 6:
        return ((re + im) * -C2, (re - im) * C2)
    if k == 10:
        return ((im - re) * C2, (re + im) * -C2)
    cos, sin = math.cos(2 * math.pi * k / 16), math.sin(2 * math.pi * k / 16)
    return (re * cos - im * sin, re * sin + im * cos)


def fft16(z, sign):
    out = [None] * 16
    inner = [fft4(z[p], z[p + 4], z[p + 8], z[p + 12], sign) for p in range(4)]
    for k in range(4):
        outer = fft4(*[turn(inner[p][k], p * k, sign) for p in range(4)], sign)
        for q in range(4):
            out[k + 4 * q] = outer[q]
    return out


def diagonals(values, lane):
    for d in (1, 2, 4):
        chosen = (lane & (16 * d)) != 0
        values = [jnp.where(chosen, values[(i + d) % 8], values[i]) for i in range(8)]
    return values


def rows_forward(own, got_members, got_control, tables, columns, out, z_full, z_half):
    first = lax.axis_index("core") == 0
    flip = jnp.where(lax.axis_index("ylo") == 0, 1.0, -1.0).astype(F32)
    for slab in range(16):
        x = []
        for m in range(8):
            at = pl.ds((m % 4) * 128 + slab * 8, 8)
            if m < 4:
                x.append(jnp.where(first, own[at, :], got_control[at, :]))
            else:
                x.append(jnp.where(first, got_members[at, :], own[at, :]))
        e = [x[m] + x[m + 4] for m in range(4)]
        d = [x[m] - x[m + 4] for m in range(4)]
        e02, e13 = e[0] + e[2], e[1] + e[3]
        minus, plus = (d[1] - d[3]) * C2, (d[1] + d[3]) * C2
        a = [None] + [(x[m] - x[8 - m]) * flip for m in range(1, 4)]
        b = [None] + [(x[m] + x[8 - m]) * flip for m in range(1, 4)]
        x0, x4 = x[0] * flip, x[4] * flip
        even, odd = x0 + a[2] * C2, x0 - a[2] * C2
        p1, p3 = a[1] * C1 + a[3] * C3, a[1] * C3 - a[3] * C1
        i_even, i_odd = x4 + b[2] * C2, b[2] * C2 - x4
        q1, q3 = b[1] * C3 + b[3] * C1, b[1] * C1 - b[3] * C3
        rows = pl.ds(slab * 8, 8)
        shifted = pl.ds(128 + slab * 8, 8)
        z_half[0, rows, :] = e02 + e13
        z_half[1, rows, :] = e02 - e13
        values = {
            1: (even + p1, -(i_even + q1)),
            2: (d[0] + minus, -(d[2] + plus)),
            3: (odd + p3, -(i_odd + q3)),
            4: (e[0] - e[2], e[3] - e[1]),
            5: (odd - p3, i_odd - q3),
            6: (d[0] - minus, d[2] - plus),
            7: (even - p1, i_even - q1),
        }
        turns = columns[rows, 0:16]
        for s, (re, im) in values.items():
            cos, sin = turns[:, s : s + 1], turns[:, 8 + s : 9 + s]
            lanes = pl.ds(128 * (s - 1), 128)
            z_full[rows, lanes] = re * cos + im * sin
            z_full[shifted, lanes] = im * cos - re * sin
    for members in ((0,), (1, 2), (3, 4), (5, 6)):
        lanes = pl.ds(128 * members[0], 128 * len(members))
        result = table_times(tables[0:512, :], z_full[:, lanes])
        for k, s in enumerate(members):
            at = 256 * s
            lanes = slice(128 * k, 128 * k + 128)
            for u in range(8):
                out[pl.ds(at + 32 * u, 16), :] = result[16 * u : 16 * u + 16, lanes]
                out[pl.ds(at + 32 * u + 16, 16), :] = result[128 + 16 * u : 144 + 16 * u, lanes]
    for s in range(2):
        out[pl.ds(1792 + 128 * s, 128), :] = table_times(tables[1024:1280, 128 * s : 128 * s + 128], z_half[s])


def front(members, control, tables, columns, pattern, loc, shell_index, own, tables_v, columns_v, straight, mirrored,
          pairs_v, loc_v, shells_v, filters_v, sems):
    core = lax.axis_index("core")
    first = core == 0
    field = pltpu.make_async_copy(members, own, sems.at[0])
    small = [
        pltpu.make_async_copy(pattern, pairs_v, sems.at[3]),
        pltpu.make_async_copy(loc, loc_v, sems.at[4]),
        pltpu.make_async_copy(shell_index, shells_v, sems.at[5]),
    ]
    large = [
        pltpu.make_async_copy(tables, tables_v, sems.at[1]),
        pltpu.make_async_copy(columns, columns_v, sems.at[2]),
    ]
    for copy in small:
        copy.start()

    @pl.when(first)
    def _():
        field.start()

    @pl.when(jnp.logical_not(first))
    def _():
        pltpu.make_async_copy(control, own, sems.at[0]).start()

    for copy in large:
        copy.start()
    for copy in small:
        copy.wait()
    chunk = place_of(FIRST, {axis: lax.axis_index(axis) for axis in FIRST})
    general = chunk < 56
    s = jnp.where(general, (chunk >> 3) + 1, jnp.where(chunk < 60, 0, 8))
    u = jnp.where(general, chunk & 7, (chunk - 56) & 3)
    special = chunk == 56
    from_shell, to_shell = pairs_v[0:1, :], pairs_v[1:2, :]
    hits = to_shell == lax.broadcasted_iota(jnp.int32, (NSHELL, to_shell.shape[1]), 0)
    second = from_shell * NBAND >= NSHELL
    shells = shells_v[...]
    in_second = shells * NBAND >= NSHELL
    filters = [jnp.where(in_second, 0.0, 1.0).astype(F32), jnp.where(in_second, 1.0, 0.0).astype(F32)]
    for band in range(NBAND):
        chosen = second if band else jnp.logical_not(second)
        counts = jnp.sum(jnp.where(jnp.logical_and(hits, chosen), 1.0, 0.0).astype(F32), axis=1, keepdims=True)
        gain = jnp.zeros(shells.shape, F32)
        for shell in range(NSHELL):
            gain = jnp.where(shells == shell, counts[shell : shell + 1, :] * loc_v[:, shell : shell + 1], gain)
        filters.append(gain)
    for f in range(2 * NBAND):
        filters_v[f] = filters[f]
    i = lax.broadcasted_iota(jnp.int32, (16, 16), 0)
    picked = []
    for f in range(2 * NBAND):

        def tile_row(tile):
            return filters_v[f, pl.ds(tile, 1), :]

        here = jnp.where(i < 8, tile_row(2 * u), tile_row(2 * u + 1))
        negated = jnp.where(i < jnp.where(s == 0, 9, 8), tile_row(15 - 2 * u), tile_row(14 - 2 * u))
        negated = jnp.where(jnp.logical_and(i == 0, s == 0), tile_row((16 - 2 * u) & 15), negated)
        picked += [here, negated, jnp.broadcast_to(tile_row(8), (8, 16))]
    picked = jnp.concatenate(picked, axis=0)
    high, rest = split_value(picked)
    middle = (picked - high.astype(F32) - rest.astype(F32)).astype(BF16)
    tile = lax.broadcasted_iota(jnp.int32, (48, 128), 0) & 15
    lane = lax.broadcasted_iota(jnp.int32, (48, 128), 1)
    spread = [tile == (lane >> 3), tile == (((128 - lane) & 127) >> 3), tile == 15 - (lane >> 3)]
    widen = jnp.concatenate([jnp.where(mask, 1.0, 0.0).astype(BF16) for mask in spread], axis=1)
    wide = mxu(jnp.concatenate([high, rest, middle], axis=1), widen)
    first_row = jnp.logical_and(special, lax.broadcasted_iota(jnp.int32, (8, 128), 0) == 0)
    for f in range(2 * NBAND):
        for kind in range(2):
            at = slice(128 + 128 * kind, 256 + 128 * kind)
            top = 40 * f
            gain = 0.5 * (wide[top : top + 16, :128] + wide[top + 16 : top + 32, at])
            other = 0.5 * (wide[top + 32 : top + 40, :128] + wide[top + 32 : top + 40, at])
            straight[kind, f, 0:8] = jnp.where(first_row, 0.5 * (gain[0:8] + other), gain[0:8])
            straight[kind, f, 8:16] = gain[8:16]
            mirrored[kind, f] = jnp.where(first_row, 0.5 * (gain[0:8] - other), 0.0)
    field.wait()
    for copy in large:
        copy.wait()


def cols_filter(received, straight, mirrored, tables, columns, out, z, y, v):
    tw = [(columns[128 + s : 129 + s, :], columns[144 + s : 145 + s, :]) for s in range(16)]

    def put(s, field, at, zr, zi):
        wr, wi = tw[s]
        z[s, field, at, 0:128] = zr * wr - zi * wi
        z[s, field, at, 128:256] = zr * wi + zi * wr

    lane = lax.broadcasted_iota(jnp.int32, (8, 128), 1)
    grp = lax.axis_index("grp")
    shifts = [(16 * (e + grp)) & 127 for e in range(8)]

    def forward(field, half):
        re_at, im_at = pl.ds(8 * half, 8), pl.ds(16 + 8 * half, 8)
        values = []
        for c in range(16):
            one, two = [place_of(FIRST, {"ylo": ylo, "core": field, **block_at(c)}) for ylo in range(2)]
            values.append(
                (received[one, re_at, :] + received[two, re_at, :], received[one, im_at, :] + received[two, im_at, :])
            )
        values = fft16(values, -1)
        for s in range(16):
            put(s, field, re_at, *values[s])
            if half == 0:
                mr, mi = values[(16 - s) % 16]
                put(s, field, pl.ds(16, 8), mr, -mi)

    def spectral(field, group):
        steps = range(GROUP * group, GROUP * group + GROUP)
        spectrum = times_table(z[pl.ds(steps[0], GROUP), field].reshape(GROUP * 24, 256), tables[512:1024, :])
        spectrum = spectrum.reshape(GROUP, 24, 256)
        filtered = []
        for step in range(GROUP):
            kind = 0 if steps[step] == 0 else 1
            tile = spectrum[step]
            for f in (2 * field, 2 * field + 1):
                gain = straight[kind, f]
                mirror = mirrored[kind, f]
                gain = jnp.concatenate([gain, gain], axis=1)
                mirror = jnp.concatenate([mirror, mirror], axis=1)
                top = gain[0:8] * tile[0:8] + mirror * tile[16:24]
                filtered.append(jnp.concatenate([top, gain[8:16] * tile[8:16]], axis=0))
        back = times_table(jnp.concatenate(filtered, axis=0), tables[0:512, :])
        y[pl.ds(steps[0], GROUP), pl.ds(2 * field, 2)] = back.reshape(GROUP, 2, 16, 256)

    def inverse(f, half):
        at = pl.ds(8 * half, 8)
        values = []
        for s in range(16):
            re, im = y[s, f, at, 0:128], y[s, f, at, 128:256]
            wr, wi = tw[s]
            values.append((re * wr + im * wi, im * wr - re * wi))
        values = fft16(values, 1)
        for c in range(16):
            v[f, c, 0, at] = values[c][0]
            v[f, c, 1, at] = values[c][1]

    def send(half, c):
        at = pl.ds(8 * half, 8)
        turned = [pltpu.roll(v[e >> 1, c, e & 1, at], shifts[e], 1) for e in range(8)]
        for i, moved in enumerate(diagonals(turned, lane)):
            q = (-i - grp) & 7
            target = {"grp": q >> 2, "ylo": (q >> 1) & 1, "core": q & 1, **block_at(c)}
            out[place_of(SECOND, target), at, :] = moved

    forward(0, 0)
    forward(0, 1)
    for group in range(16 // GROUP):
        spectral(0, group)
    forward(1, 0)
    forward(1, 1)
    for group in range(16 // GROUP):
        spectral(1, group)
    for f, half in ((0, 0), (1, 0), (0, 1), (1, 1), (2, 0), (3, 0)):
        inverse(f, half)
    for c in range(16):
        send(0, c)
    inverse(2, 1)
    inverse(3, 1)
    for c in range(16):
        send(1, c)


def rows_inverse(received, tables, columns, out, z_full, z_half):
    row = lax.axis_index("ylo") * 2 + lax.axis_index("core")
    mine = lax.axis_index("grp") * 4 + row
    even = ((lax.broadcasted_iota(jnp.int32, (16, 128), 1) - 16 * mine) & 16) == 0

    def chunk(d):
        one, two = received[of_group(0, d)], received[of_group(1, d)]
        return jnp.where(even, one, two), pltpu.roll(jnp.where(even, two, one), 112, 1)

    for members in ((0,), (1, 2), (3, 4), (5, 6)):
        spectra = []
        for s in members:
            parts = [chunk(8 * s + u) for u in range(8)]
            spectra.append(jnp.concatenate([p[0] for p in parts] + [p[1] for p in parts], axis=0))
        result = table_times(tables[512:1024, :], jnp.concatenate(spectra, axis=1))
        for k, s in enumerate(members):
            z_full[s] = result[:, 128 * k : 128 * k + 128]
    for s in range(2):
        parts = [chunk(56 + 4 * s + u) for u in range(4)]
        z_half[s] = table_times(tables[1280:1536, 128 * s : 128 * s + 128], jnp.concatenate([p[k] for p in parts for k in range(2)], axis=0))
    lane = lax.broadcasted_iota(jnp.int32, (8, 128), 1) - 16 * mine
    low64, low32, low16 = (lane & 64) == 0, (lane & 32) == 0, (lane & 16) == 0

    def fold(one, two, low, shift):
        other = jnp.where(low, two, one)
        return jnp.where(low, one, two) + jnp.where(low, pltpu.roll(other, 128 - shift, 1), pltpu.roll(other, shift, 1))

    for slab in range(8):
        x = [fields_of(slab + 8 * h, z_full, z_half, columns) for h in range(2)]
        for dest in range(4):
            u = []
            for m in range(4 * dest, 4 * dest + 4):
                one, two = x[0][m], x[1][m]
                u.append(jnp.where(low64, one, two) * pltpu.roll(jnp.where(low64, two, one), 64, 1))
            packed = fold(fold(u[0], u[2], low32, 32), fold(u[1], u[3], low32, 32), low16, 16)
            slot = dest ^ row
            out[((slot & 1) << 1) | (slot >> 1), pl.ds(slab * 8, 8), :] = packed


def fields_of(slab, z_full, z_half, columns):
    rows, shifted = pl.ds(slab * 8, 8), pl.ds(128 + slab * 8, 8)
    y0, y8 = z_half[0, rows, :], z_half[1, rows, :]
    turns = columns[rows, 16:32]
    a, b = [None], [None]
    for s in range(1, 8):
        cos, sin = turns[:, s : s + 1], turns[:, 8 + s : 9 + s]
        re, im = z_full[s - 1, rows, :], z_full[s - 1, shifted, :]
        a.append(re * cos - im * sin)
        b.append(re * sin + im * cos)
    plus, minus = y0 + y8, y0 - y8
    a26, turned = a[2] + a[6], (a[2] - a[6]) * C2
    c_even = [plus + a26 + a[4], minus + turned, plus - a[4], minus - turned, plus - a26 + a[4]]
    p, q, r, t = a[1] - a[7], a[3] - a[5], a[1] + a[7], a[3] + a[5]
    c_odd = [r + t, p * C1 + q * C3, (r - t) * C2, p * C3 - q * C1, None]
    b17, b35, b26 = b[1] + b[7], b[3] + b[5], (b[2] + b[6]) * C2
    d17, d35 = b[1] - b[7], b[3] - b[5]
    s_odd = [None, b17 * C3 + b35 * C1, (d17 + d35) * C2, b17 * C1 - b35 * C3, d17 - d35]
    s_even = [None, b26 + b[4], b[2] - b[6], b26 - b[4], None]
    x = [None] * 16
    x[0], x[8] = c_even[0] + c_odd[0], c_even[0] - c_odd[0]
    x[4], x[12] = c_even[4] - s_odd[4], c_even[4] + s_odd[4]
    for m in range(1, 4):
        c_near, c_far = c_even[m] + c_odd[m], c_even[m] - c_odd[m]
        s_near, s_far = s_odd[m] + s_even[m], s_odd[m] - s_even[m]
        x[m], x[16 - m] = c_near - s_near, c_near + s_near
        x[8 - m], x[8 + m] = c_far - s_far, c_far + s_far
    return x


def assemble(own, by_row, by_grp, by_both, out, pieces, whole, sems):
    mine = (lax.axis_index("grp") * 2 + lax.axis_index("ylo")) * 2 + lax.axis_index("core")
    for k, ref in enumerate((own, by_row, by_grp, by_both)):
        pieces[pl.ds(2 * k, 2)] = ref[...]
    lane = lax.broadcasted_iota(jnp.int32, (8, 128), 1)
    copies = []
    for part in range(2):
        for slab in range(4 * part, 4 * part + 4):
            rows = pl.ds(slab * 8, 8)
            for i, moved in enumerate(diagonals([pieces[q ^ mine, rows, :] for q in range(8)], lane)):
                e = -i % 8
                whole[e & 3, e >> 2, rows, :] = pltpu.roll(moved, 16 * i, 1) if i else moved
        rows = pl.ds(32 * part, 32)
        copy = pltpu.make_async_copy(whole.at[:, :, rows, :], out.at[:, :, rows, :], sems.at[part])
        copy.start()
        copies.append(copy)
    for copy in copies:
        copy.wait()


def in_vmem(count):
    return [pl.BlockSpec(memory_space=pltpu.VMEM)] * count


def in_hbm(*arrays):
    return [pltpu.with_memory_space_constraint(jnp.asarray(x), pltpu.HBM) for x in arrays]


def params():
    return pltpu.CompilerParams(vmem_limit_bytes=LIMIT)


def shape(*dims):
    return jax.ShapeDtypeStruct(dims, F32)


def constant_tables():
    half_f, half_i = [np.concatenate(split_table(t), axis=1) for t in rows_tables()]
    fwd, inv, twiddle, column = cols_tables()
    halves = [np.concatenate([h[0], h[1]], axis=1) for h in (half_f, half_i)]
    tables = np.concatenate([*split_table(inv), *split_table(fwd), *halves], axis=0)
    columns = np.zeros((160, 128), np.float32)
    columns[:128, 0:16] = column
    columns[:128, 16:32] = 2 * SCALE * column
    columns[128:144] = twiddle[:, 0]
    columns[144:160] = twiddle[:, 1]
    return tables, columns


def call_rows_forward(own, got_members, got_control, tables, columns):
    return pl.pallas_call(
        rows_forward,
        out_shape=shape(2048, 128),
        in_specs=in_vmem(5),
        out_specs=in_vmem(1)[0],
        scratch_shapes=[pltpu.VMEM((256, 896), F32), pltpu.VMEM((2, 128, 128), F32)],
        compiler_params=params(),
        name="rows_forward",
    )(own, got_members, got_control, tables, columns)


def call_cols_filter(spectra, straight, mirrored, tables, columns):
    return pl.pallas_call(
        cols_filter,
        out_shape=shape(128, 16, 128),
        in_specs=in_vmem(5),
        out_specs=in_vmem(1)[0],
        scratch_shapes=[
            pltpu.VMEM((16, 2, 24, 256), F32),
            pltpu.VMEM((16, 4, 16, 256), F32),
            pltpu.VMEM((4, 16, 2, 16, 128), F32),
        ],
        compiler_params=params(),
        name="cols_filter",
    )(spectra, straight, mirrored, tables, columns)


def call_rows_inverse(filtered, tables, columns):
    return pl.pallas_call(
        rows_inverse,
        out_shape=shape(4, 64, 128),
        in_specs=in_vmem(3),
        out_specs=in_vmem(1)[0],
        scratch_shapes=[pltpu.VMEM((7, 256, 128), F32), pltpu.VMEM((2, 128, 128), F32)],
        compiler_params=params(),
        name="rows_inverse",
    )(filtered, tables, columns)


def call_assemble(near, by_row, by_grp, by_both):
    return pl.pallas_call(
        assemble,
        out_shape=shape(4, 2, 64, 128),
        in_specs=in_vmem(4),
        out_specs=pl.BlockSpec(memory_space=pltpu.HBM),
        scratch_shapes=[
            pltpu.VMEM((8, 64, 128), F32),
            pltpu.VMEM((4, 2, 64, 128), F32),
            pltpu.SemaphoreType.DMA((2,)),
        ],
        compiler_params=params(),
        name="assemble",
    )(near, by_row, by_grp, by_both).reshape(512, 128)


def call_front(members, control, tables, columns, pattern, loc_spectrum, shell_index):
    return pl.pallas_call(
        front,
        out_shape=(
            shape(512, 128),
            jax.ShapeDtypeStruct(tables.shape, BF16),
            shape(*columns.shape),
            shape(2, 4, 16, 128),
            shape(2, 4, 8, 128),
        ),
        in_specs=[pl.BlockSpec(memory_space=pltpu.HBM)] * 7,
        out_specs=tuple(in_vmem(5)),
        scratch_shapes=[
            pltpu.VMEM((2, pattern.shape[0]), jnp.int32),
            pltpu.VMEM((1, NSHELL), F32),
            pltpu.VMEM(shell_index.shape, jnp.int32),
            pltpu.VMEM((2 * NBAND, *shell_index.shape), F32),
            pltpu.SemaphoreType.DMA((6,)),
        ],
        compiler_params=params(),
        name="front",
    )(*in_hbm(members, control, tables, columns, pattern.T, loc_spectrum.reshape(1, NSHELL), shell_index))


def on_device(members, control, loc_spectrum, pattern, shell_index):
    tables, columns = constant_tables()
    members = members.reshape(512, 128)
    control = control.reshape(512, 128)
    swap_cores = [(0, 1), (1, 0)]
    got_members = lax.ppermute(members, "core", swap_cores)
    got_control = lax.ppermute(control, "core", swap_cores)
    own, tables, columns, straight, mirrored = call_front(
        members, control, tables, columns, pattern, loc_spectrum, shell_index
    )
    spectra = call_rows_forward(own, got_members, got_control, tables, columns)
    spectra = lax.all_to_all(spectra.reshape(64, 32, 128), FIRST, split_axis=0, concat_axis=0, tiled=True)
    filtered = call_cols_filter(spectra, straight, mirrored, tables, columns)
    filtered = lax.all_to_all(filtered, SECOND, split_axis=0, concat_axis=0, tiled=True)
    products = call_rows_inverse(filtered, tables, columns)
    got = lax.ppermute(products[2:4], "core", swap_cores)
    near = jnp.stack([products[0], got[0]])
    far = jnp.stack([products[1], got[1]])

    def exchange(value, step):
        return lax.ppermute(value, ("grp", "ylo"), [(i, i ^ step) for i in range(4)])

    by_grp, by_both, by_row = exchange(near, 2), exchange(far, 3), exchange(far, 1)
    return call_assemble(near, by_row, by_grp, by_both)


def solution(mesh):
    fine = Mesh(mesh.devices.reshape((2,) * len(AXES)), AXES)
    rows, cols = AXES[1:3], AXES[3:]
    placed = (P("grp", rows, cols), P("grp", rows, cols), P(), P(), P())
    return jax.shard_map(on_device, mesh=fine, in_specs=placed, out_specs=P(rows, cols), check_vma=False)
```

```python
import math

import jax
import jax.numpy as jnp
import ml_dtypes
import numpy as np
from jax import lax
from jax.experimental import pallas as pl
from jax.experimental.pallas import tpu as pltpu
from jax.sharding import Mesh
from jax.sharding import PartitionSpec as P

NBAND = 2
NSHELL = 12
F32 = jnp.float32
BF16 = jnp.bfloat16
C1, C2, C3 = math.cos(math.pi / 8), math.cos(math.pi / 4), math.cos(3 * math.pi / 8)
LIMIT = 48 * 1024 * 1024
GROUP = 16
SCALE = 1.0 / (2048.0 * 2048.0)


def split_table(table):
    high = table.astype(ml_dtypes.bfloat16)
    low = (table - high.astype(np.float64)).astype(ml_dtypes.bfloat16)
    return high, low


def rows_tables():
    j = np.arange(128)
    t = np.arange(64)
    forward, inverse = [], []

    def interleave(real_part, imag_part):
        stacked = np.stack([real_part.reshape(4, 16, 128), imag_part.reshape(4, 16, 128)], axis=1)
        return stacked.reshape(128, 128)

    for s in (0, 8):
        theta = 2 * np.pi * (((s + 16 * t)[:, None] * j[None, :]) % 2048) / 2048
        cos, sin = np.cos(theta), -np.sin(theta)
        weight = np.full((64, 1), 2.0)
        if s == 0:
            sin[0] = 1.0 - 2.0 * (j % 2)
            weight[0] = 1.0
        forward.append(interleave(cos, sin))
        inverse.append(SCALE * interleave(weight * cos, weight * sin).T)
    return np.stack(forward), np.stack(inverse)


def cols_tables():
    j = np.arange(128)
    theta = 2 * np.pi * ((j[:, None] * j[None, :]) % 128) / 128
    cos, sin = np.cos(theta), np.sin(theta)
    forward = np.block([[cos, -sin], [sin, cos]])
    inverse = np.block([[cos, sin], [-sin, cos]])
    angle = 2 * np.pi * (np.arange(16)[:, None] * j[None, :]) / 2048
    twiddle = np.stack([np.cos(angle), -np.sin(angle)], axis=1).astype(np.float32)
    column = np.concatenate([np.cos(angle[:8]), np.sin(angle[:8])], axis=0).T
    return forward, inverse, twiddle, column


AXES = ("grp", "ylo", "core", "x1", "x0", "z1", "z0")
FIRST = ("x1", "x0", "core", "z1", "ylo", "z0")
SECOND = ("core", "z1", "z0", "x1", "x0", "grp", "ylo")


def place_of(order, at):
    place = 0
    for axis in order:
        place = place * 2 + at[axis]
    return place


def block_at(block):
    return {"x1": block >> 3, "x0": (block >> 2) & 1, "z1": (block >> 1) & 1, "z0": block & 1}


def of_group(grp, chunk):
    at = {"grp": grp}
    for axis in reversed(FIRST):
        at[axis] = chunk & 1
        chunk >>= 1
    return place_of(SECOND, at)


def split_value(value):
    high = value.astype(BF16)
    return high, (value - high.astype(F32)).astype(BF16)


def mxu(a, b):
    return jnp.dot(a, b, preferred_element_type=F32)


def table_times(both, value):
    v_high, v_low = split_value(value)
    rows = both.shape[0] // 2
    high, low = both[:rows], both[rows:]
    return mxu(jnp.concatenate([high, high, low], axis=1), jnp.concatenate([v_high, v_low, v_high], axis=0))


def times_table(value, both):
    v_high, v_low = split_value(value)
    high, low = both[:256], both[256:]
    return mxu(jnp.concatenate([v_high, v_low, v_high], axis=1), jnp.concatenate([high, high, low], axis=0))


def fft4(a, b, c, d, sign):
    s0r, s0i = a[0] + c[0], a[1] + c[1]
    s1r, s1i = a[0] - c[0], a[1] - c[1]
    s2r, s2i = b[0] + d[0], b[1] + d[1]
    s3r, s3i = b[0] - d[0], b[1] - d[1]
    rr, ri = -sign * s3i, sign * s3r
    return (
        (s0r + s2r, s0i + s2i),
        (s1r + rr, s1i + ri),
        (s0r - s2r, s0i - s2i),
        (s1r - rr, s1i - ri),
    )


def turn(z, k, sign):
    re, im = z
    k = (k * sign) % 16
    if k == 0:
        return z
    if k == 4:
        return (-im, re)
    if k == 2:
        return ((re - im) * C2, (re + im) * C2)
    if k == 14:
        return ((re + im) * C2, (im - re) * C2)
    if k == 6:
        return ((re + im) * -C2, (re - im) * C2)
    if k == 10:
        return ((im - re) * C2, (re + im) * -C2)
    cos, sin = math.cos(2 * math.pi * k / 16), math.sin(2 * math.pi * k / 16)
    return (re * cos - im * sin, re * sin + im * cos)


def fft16(z, sign):
    out = [None] * 16
    inner = [fft4(z[p], z[p + 4], z[p + 8], z[p + 12], sign) for p in range(4)]
    for k in range(4):
        outer = fft4(*[turn(inner[p][k], p * k, sign) for p in range(4)], sign)
        for q in range(4):
            out[k + 4 * q] = outer[q]
    return out


def diagonals(values, lane):
    for d in (1, 2, 4):
        chosen = (lane & (16 * d)) != 0
        values = [jnp.where(chosen, values[(i + d) % 8], values[i]) for i in range(8)]
    return values


def rows_forward(own, got_members, got_control, tables, columns, out, z_full, z_half):
    first = lax.axis_index("core") == 0
    flip = jnp.where(lax.axis_index("ylo") == 0, 1.0, -1.0).astype(F32)
    for slab in range(16):
        x = []
        for m in range(8):
            at = pl.ds((m % 4) * 128 + slab * 8, 8)
            if m < 4:
                x.append(jnp.where(first, own[at, :], got_control[at, :]))
            else:
                x.append(jnp.where(first, got_members[at, :], own[at, :]))
        e = [x[m] + x[m + 4] for m in range(4)]
        d = [x[m] - x[m + 4] for m in range(4)]
        e02, e13 = e[0] + e[2], e[1] + e[3]
        minus, plus = (d[1] - d[3]) * C2, (d[1] + d[3]) * C2
        a = [None] + [(x[m] - x[8 - m]) * flip for m in range(1, 4)]
        b = [None] + [(x[m] + x[8 - m]) * flip for m in range(1, 4)]
        x0, x4 = x[0] * flip, x[4] * flip
        even, odd = x0 + a[2] * C2, x0 - a[2] * C2
        p1, p3 = a[1] * C1 + a[3] * C3, a[1] * C3 - a[3] * C1
        i_even, i_odd = x4 + b[2] * C2, b[2] * C2 - x4
        q1, q3 = b[1] * C3 + b[3] * C1, b[1] * C1 - b[3] * C3
        rows = pl.ds(slab * 8, 8)
        shifted = pl.ds(128 + slab * 8, 8)
        z_half[0, rows, :] = e02 + e13
        z_half[1, rows, :] = e02 - e13
        values = {
            1: (even + p1, -(i_even + q1)),
            2: (d[0] + minus, -(d[2] + plus)),
            3: (odd + p3, -(i_odd + q3)),
            4: (e[0] - e[2], e[3] - e[1]),
            5: (odd - p3, i_odd - q3),
            6: (d[0] - minus, d[2] - plus),
            7: (even - p1, i_even - q1),
        }
        turns = columns[rows, 0:16]
        for s, (re, im) in values.items():
            cos, sin = turns[:, s : s + 1], turns[:, 8 + s : 9 + s]
            lanes = pl.ds(128 * (s - 1), 128)
            z_full[rows, lanes] = re * cos + im * sin
            z_full[shifted, lanes] = im * cos - re * sin
    for members in ((0,), (1, 2), (3, 4), (5, 6)):
        lanes = pl.ds(128 * members[0], 128 * len(members))
        result = table_times(tables[0:512, :], z_full[:, lanes])
        for k, s in enumerate(members):
            at = 256 * s
            lanes = slice(128 * k, 128 * k + 128)
            for u in range(8):
                out[pl.ds(at + 32 * u, 16), :] = result[16 * u : 16 * u + 16, lanes]
                out[pl.ds(at + 32 * u + 16, 16), :] = result[128 + 16 * u : 144 + 16 * u, lanes]
    for s in range(2):
        out[pl.ds(1792 + 128 * s, 128), :] = table_times(tables[1024:1280, 128 * s : 128 * s + 128], z_half[s])


def front(members, control, tables, columns, pattern, loc, shell_index, own, tables_v, columns_v, straight, mirrored,
          pairs_v, loc_v, shells_v, filters_v, sems):
    core = lax.axis_index("core")
    first = core == 0
    field = pltpu.make_async_copy(members, own, sems.at[0])
    small = [
        pltpu.make_async_copy(pattern, pairs_v, sems.at[3]),
        pltpu.make_async_copy(loc, loc_v, sems.at[4]),
        pltpu.make_async_copy(shell_index, shells_v, sems.at[5]),
    ]
    large = [
        pltpu.make_async_copy(tables, tables_v, sems.at[1]),
        pltpu.make_async_copy(columns, columns_v, sems.at[2]),
    ]
    for copy in small:
        copy.start()

    @pl.when(first)
    def _():
        field.start()

    @pl.when(jnp.logical_not(first))
    def _():
        pltpu.make_async_copy(control, own, sems.at[0]).start()

    for copy in large:
        copy.start()
    for copy in small:
        copy.wait()
    chunk = place_of(FIRST, {axis: lax.axis_index(axis) for axis in FIRST})
    general = chunk < 56
    s = jnp.where(general, (chunk >> 3) + 1, jnp.where(chunk < 60, 0, 8))
    u = jnp.where(general, chunk & 7, (chunk - 56) & 3)
    special = chunk == 56
    from_shell, to_shell = pairs_v[0:1, :], pairs_v[1:2, :]
    hits = to_shell == lax.broadcasted_iota(jnp.int32, (NSHELL, to_shell.shape[1]), 0)
    second = from_shell * NBAND >= NSHELL
    shells = shells_v[...]
    in_second = shells * NBAND >= NSHELL
    filters = [jnp.where(in_second, 0.0, 1.0).astype(F32), jnp.where(in_second, 1.0, 0.0).astype(F32)]
    for band in range(NBAND):
        chosen = second if band else jnp.logical_not(second)
        counts = jnp.sum(jnp.where(jnp.logical_and(hits, chosen), 1.0, 0.0).astype(F32), axis=1, keepdims=True)
        gain = jnp.zeros(shells.shape, F32)
        for shell in range(NSHELL):
            gain = jnp.where(shells == shell, counts[shell : shell + 1, :] * loc_v[:, shell : shell + 1], gain)
        filters.append(gain)
    for f in range(2 * NBAND):
        filters_v[f] = filters[f]
    i = lax.broadcasted_iota(jnp.int32, (16, 16), 0)
    picked = []
    for f in range(2 * NBAND):

        def tile_row(tile):
            return filters_v[f, pl.ds(tile, 1), :]

        here = jnp.where(i < 8, tile_row(2 * u), tile_row(2 * u + 1))
        negated = jnp.where(i < jnp.where(s == 0, 9, 8), tile_row(15 - 2 * u), tile_row(14 - 2 * u))
        negated = jnp.where(jnp.logical_and(i == 0, s == 0), tile_row((16 - 2 * u) & 15), negated)
        picked += [here, negated, jnp.broadcast_to(tile_row(8), (8, 16))]
    picked = jnp.concatenate(picked, axis=0)
    high, rest = split_value(picked)
    middle = (picked - high.astype(F32) - rest.astype(F32)).astype(BF16)
    tile = lax.broadcasted_iota(jnp.int32, (48, 128), 0) & 15
    lane = lax.broadcasted_iota(jnp.int32, (48, 128), 1)
    spread = [tile == (lane >> 3), tile == (((128 - lane) & 127) >> 3), tile == 15 - (lane >> 3)]
    widen = jnp.concatenate([jnp.where(mask, 1.0, 0.0).astype(BF16) for mask in spread], axis=1)
    wide = mxu(jnp.concatenate([high, rest, middle], axis=1), widen)
    first_row = jnp.logical_and(special, lax.broadcasted_iota(jnp.int32, (8, 128), 0) == 0)
    for f in range(2 * NBAND):
        for kind in range(2):
            at = slice(128 + 128 * kind, 256 + 128 * kind)
            top = 40 * f
            gain = 0.5 * (wide[top : top + 16, :128] + wide[top + 16 : top + 32, at])
            other = 0.5 * (wide[top + 32 : top + 40, :128] + wide[top + 32 : top + 40, at])
            straight[kind, f, 0:8] = jnp.where(first_row, 0.5 * (gain[0:8] + other), gain[0:8])
            straight[kind, f, 8:16] = gain[8:16]
            mirrored[kind, f] = jnp.where(first_row, 0.5 * (gain[0:8] - other), 0.0)
    field.wait()
    for copy in large:
        copy.wait()


def cols_filter(received, straight, mirrored, tables, columns, out, z, y, v):
    tw = [(columns[128 + s : 129 + s, :], columns[144 + s : 145 + s, :]) for s in range(16)]

    def put(s, field, at, zr, zi):
        wr, wi = tw[s]
        z[s, field, at, 0:128] = zr * wr - zi * wi
        z[s, field, at, 128:256] = zr * wi + zi * wr

    lane = lax.broadcasted_iota(jnp.int32, (8, 128), 1)
    grp = lax.axis_index("grp")
    shifts = [(16 * (e + grp)) & 127 for e in range(8)]

    def forward(field, half):
        re_at, im_at = pl.ds(8 * half, 8), pl.ds(16 + 8 * half, 8)
        values = []
        for c in range(16):
            one, two = [place_of(FIRST, {"ylo": ylo, "core": field, **block_at(c)}) for ylo in range(2)]
            values.append(
                (received[one, re_at, :] + received[two, re_at, :], received[one, im_at, :] + received[two, im_at, :])
            )
        values = fft16(values, -1)
        for s in range(16):
            put(s, field, re_at, *values[s])
            if half == 0:
                mr, mi = values[(16 - s) % 16]
                put(s, field, pl.ds(16, 8), mr, -mi)

    def spectral(field, group):
        steps = range(16 * group, 16 * group + 16)
        spectrum = times_table(z[pl.ds(steps[0], 16), field].reshape(16 * 24, 256), tables[512:1024, :])
        spectrum = spectrum.reshape(16, 24, 256)
        for f in (2 * field, 2 * field + 1):
            filtered = []
            for step in range(16):
                kind = 0 if steps[step] == 0 else 1
                tile = spectrum[step]
                gain = straight[kind, f]
                mirror = mirrored[kind, f]
                gain = jnp.concatenate([gain, gain], axis=1)
                mirror = jnp.concatenate([mirror, mirror], axis=1)
                top = gain[0:8] * tile[0:8] + mirror * tile[16:24]
                filtered.append(jnp.concatenate([top, gain[8:16] * tile[8:16]], axis=0))
            back = times_table(jnp.concatenate(filtered, axis=0), tables[0:512, :])
            y[pl.ds(steps[0], 16), f] = back.reshape(16, 16, 256)

    def inverse(f, half):
        at = pl.ds(8 * half, 8)
        values = []
        for s in range(16):
            re, im = y[s, f, at, 0:128], y[s, f, at, 128:256]
            wr, wi = tw[s]
            values.append((re * wr + im * wi, im * wr - re * wi))
        values = fft16(values, 1)
        for c in range(16):
            v[f, c, 0, at] = values[c][0]
            v[f, c, 1, at] = values[c][1]

    def send(half, c):
        at = pl.ds(8 * half, 8)
        turned = [pltpu.roll(v[e >> 1, c, e & 1, at], shifts[e], 1) for e in range(8)]
        for i, moved in enumerate(diagonals(turned, lane)):
            q = (-i - grp) & 7
            target = {"grp": q >> 2, "ylo": (q >> 1) & 1, "core": q & 1, **block_at(c)}
            out[place_of(SECOND, target), at, :] = moved

    forward(0, 0)
    forward(0, 1)
    for group in range(16 // GROUP):
        spectral(0, group)
    forward(1, 0)
    forward(1, 1)
    for group in range(16 // GROUP):
        spectral(1, group)
    for f, half in ((0, 0), (1, 0), (0, 1), (1, 1), (2, 0), (3, 0)):
        inverse(f, half)
    for c in range(16):
        send(0, c)
    inverse(2, 1)
    inverse(3, 1)
    for c in range(16):
        send(1, c)


def rows_inverse(received, tables, columns, out, z_full, z_half):
    row = lax.axis_index("ylo") * 2 + lax.axis_index("core")
    mine = lax.axis_index("grp") * 4 + row
    even = ((lax.broadcasted_iota(jnp.int32, (16, 128), 1) - 16 * mine) & 16) == 0

    def chunk(d):
        one, two = received[of_group(0, d)], received[of_group(1, d)]
        return jnp.where(even, one, two), pltpu.roll(jnp.where(even, two, one), 112, 1)

    for members in ((0,), (1, 2), (3, 4), (5, 6)):
        spectra = []
        for s in members:
            parts = [chunk(8 * s + u) for u in range(8)]
            spectra.append(jnp.concatenate([p[0] for p in parts] + [p[1] for p in parts], axis=0))
        result = table_times(tables[512:1024, :], jnp.concatenate(spectra, axis=1))
        for k, s in enumerate(members):
            z_full[s] = result[:, 128 * k : 128 * k + 128]
    for s in range(2):
        parts = [chunk(56 + 4 * s + u) for u in range(4)]
        z_half[s] = table_times(tables[1280:1536, 128 * s : 128 * s + 128], jnp.concatenate([p[k] for p in parts for k in range(2)], axis=0))
    lane = lax.broadcasted_iota(jnp.int32, (8, 128), 1) - 16 * mine
    low64, low32, low16 = (lane & 64) == 0, (lane & 32) == 0, (lane & 16) == 0

    def fold(one, two, low, shift):
        other = jnp.where(low, two, one)
        return jnp.where(low, one, two) + jnp.where(low, pltpu.roll(other, 128 - shift, 1), pltpu.roll(other, shift, 1))

    for slab in range(8):
        x = [fields_of(slab + 8 * h, z_full, z_half, columns) for h in range(2)]
        for dest in range(4):
            u = []
            for m in range(4 * dest, 4 * dest + 4):
                one, two = x[0][m], x[1][m]
                u.append(jnp.where(low64, one, two) * pltpu.roll(jnp.where(low64, two, one), 64, 1))
            packed = fold(fold(u[0], u[2], low32, 32), fold(u[1], u[3], low32, 32), low16, 16)
            slot = dest ^ row
            out[((slot & 1) << 1) | (slot >> 1), pl.ds(slab * 8, 8), :] = packed


def fields_of(slab, z_full, z_half, columns):
    rows, shifted = pl.ds(slab * 8, 8), pl.ds(128 + slab * 8, 8)
    y0, y8 = z_half[0, rows, :], z_half[1, rows, :]
    turns = columns[rows, 16:32]
    a, b = [None], [None]
    for s in range(1, 8):
        cos, sin = turns[:, s : s + 1], turns[:, 8 + s : 9 + s]
        re, im = z_full[s - 1, rows, :], z_full[s - 1, shifted, :]
        a.append(re * cos - im * sin)
        b.append(re * sin + im * cos)
    plus, minus = y0 + y8, y0 - y8
    a26, turned = a[2] + a[6], (a[2] - a[6]) * C2
    c_even = [plus + a26 + a[4], minus + turned, plus - a[4], minus - turned, plus - a26 + a[4]]
    p, q, r, t = a[1] - a[7], a[3] - a[5], a[1] + a[7], a[3] + a[5]
    c_odd = [r + t, p * C1 + q * C3, (r - t) * C2, p * C3 - q * C1, None]
    b17, b35, b26 = b[1] + b[7], b[3] + b[5], (b[2] + b[6]) * C2
    d17, d35 = b[1] - b[7], b[3] - b[5]
    s_odd = [None, b17 * C3 + b35 * C1, (d17 + d35) * C2, b17 * C1 - b35 * C3, d17 - d35]
    s_even = [None, b26 + b[4], b[2] - b[6], b26 - b[4], None]
    x = [None] * 16
    x[0], x[8] = c_even[0] + c_odd[0], c_even[0] - c_odd[0]
    x[4], x[12] = c_even[4] - s_odd[4], c_even[4] + s_odd[4]
    for m in range(1, 4):
        c_near, c_far = c_even[m] + c_odd[m], c_even[m] - c_odd[m]
        s_near, s_far = s_odd[m] + s_even[m], s_odd[m] - s_even[m]
        x[m], x[16 - m] = c_near - s_near, c_near + s_near
        x[8 - m], x[8 + m] = c_far - s_far, c_far + s_far
    return x


def assemble(own, by_row, by_grp, by_both, out, pieces, whole, sems):
    mine = (lax.axis_index("grp") * 2 + lax.axis_index("ylo")) * 2 + lax.axis_index("core")
    for k, ref in enumerate((own, by_row, by_grp, by_both)):
        pieces[pl.ds(2 * k, 2)] = ref[...]
    lane = lax.broadcasted_iota(jnp.int32, (8, 128), 1)
    copies = []
    for part in range(2):
        for slab in range(4 * part, 4 * part + 4):
            rows = pl.ds(slab * 8, 8)
            for i, moved in enumerate(diagonals([pieces[q ^ mine, rows, :] for q in range(8)], lane)):
                e = -i % 8
                whole[e & 3, e >> 2, rows, :] = pltpu.roll(moved, 16 * i, 1) if i else moved
        rows = pl.ds(32 * part, 32)
        copy = pltpu.make_async_copy(whole.at[:, :, rows, :], out.at[:, :, rows, :], sems.at[part])
        copy.start()
        copies.append(copy)
    for copy in copies:
        copy.wait()


def in_vmem(count):
    return [pl.BlockSpec(memory_space=pltpu.VMEM)] * count


def in_hbm(*arrays):
    return [pltpu.with_memory_space_constraint(jnp.asarray(x), pltpu.HBM) for x in arrays]


def params():
    return pltpu.CompilerParams(vmem_limit_bytes=LIMIT)


def shape(*dims):
    return jax.ShapeDtypeStruct(dims, F32)


def constant_tables():
    half_f, half_i = [np.concatenate(split_table(t), axis=1) for t in rows_tables()]
    fwd, inv, twiddle, column = cols_tables()
    halves = [np.concatenate([h[0], h[1]], axis=1) for h in (half_f, half_i)]
    tables = np.concatenate([*split_table(inv), *split_table(fwd), *halves], axis=0)
    columns = np.zeros((160, 128), np.float32)
    columns[:128, 0:16] = column
    columns[:128, 16:32] = 2 * SCALE * column
    columns[128:144] = twiddle[:, 0]
    columns[144:160] = twiddle[:, 1]
    return tables, columns


def call_rows_forward(own, got_members, got_control, tables, columns):
    return pl.pallas_call(
        rows_forward,
        out_shape=shape(2048, 128),
        in_specs=in_vmem(5),
        out_specs=in_vmem(1)[0],
        scratch_shapes=[pltpu.VMEM((256, 896), F32), pltpu.VMEM((2, 128, 128), F32)],
        compiler_params=params(),
        name="rows_forward",
    )(own, got_members, got_control, tables, columns)


def call_cols_filter(spectra, straight, mirrored, tables, columns):
    return pl.pallas_call(
        cols_filter,
        out_shape=shape(128, 16, 128),
        in_specs=in_vmem(5),
        out_specs=in_vmem(1)[0],
        scratch_shapes=[
            pltpu.VMEM((16, 2, 24, 256), F32),
            pltpu.VMEM((16, 4, 16, 256), F32),
            pltpu.VMEM((4, 16, 2, 16, 128), F32),
        ],
        compiler_params=params(),
        name="cols_filter",
    )(spectra, straight, mirrored, tables, columns)


def call_rows_inverse(filtered, tables, columns):
    return pl.pallas_call(
        rows_inverse,
        out_shape=shape(4, 64, 128),
        in_specs=in_vmem(3),
        out_specs=in_vmem(1)[0],
        scratch_shapes=[pltpu.VMEM((7, 256, 128), F32), pltpu.VMEM((2, 128, 128), F32)],
        compiler_params=params(),
        name="rows_inverse",
    )(filtered, tables, columns)


def call_assemble(near, by_row, by_grp, by_both):
    return pl.pallas_call(
        assemble,
        out_shape=shape(4, 2, 64, 128),
        in_specs=in_vmem(4),
        out_specs=pl.BlockSpec(memory_space=pltpu.HBM),
        scratch_shapes=[
            pltpu.VMEM((8, 64, 128), F32),
            pltpu.VMEM((4, 2, 64, 128), F32),
            pltpu.SemaphoreType.DMA((2,)),
        ],
        compiler_params=params(),
        name="assemble",
    )(near, by_row, by_grp, by_both).reshape(512, 128)


def call_front(members, control, tables, columns, pattern, loc_spectrum, shell_index):
    return pl.pallas_call(
        front,
        out_shape=(
            shape(512, 128),
            jax.ShapeDtypeStruct(tables.shape, BF16),
            shape(*columns.shape),
            shape(2, 4, 16, 128),
            shape(2, 4, 8, 128),
        ),
        in_specs=[pl.BlockSpec(memory_space=pltpu.HBM)] * 7,
        out_specs=tuple(in_vmem(5)),
        scratch_shapes=[
            pltpu.VMEM((2, pattern.shape[0]), jnp.int32),
            pltpu.VMEM((1, NSHELL), F32),
            pltpu.VMEM(shell_index.shape, jnp.int32),
            pltpu.VMEM((2 * NBAND, *shell_index.shape), F32),
            pltpu.SemaphoreType.DMA((6,)),
        ],
        compiler_params=params(),
        name="front",
    )(*in_hbm(members, control, tables, columns, pattern.T, loc_spectrum.reshape(1, NSHELL), shell_index))


def on_device(members, control, loc_spectrum, pattern, shell_index):
    tables, columns = constant_tables()
    members = members.reshape(512, 128)
    control = control.reshape(512, 128)
    swap_cores = [(0, 1), (1, 0)]
    got_members = lax.ppermute(members, "core", swap_cores)
    got_control = lax.ppermute(control, "core", swap_cores)
    own, tables, columns, straight, mirrored = call_front(
        members, control, tables, columns, pattern, loc_spectrum, shell_index
    )
    spectra = call_rows_forward(own, got_members, got_control, tables, columns)
    spectra = lax.all_to_all(spectra.reshape(64, 32, 128), FIRST, split_axis=0, concat_axis=0, tiled=True)
    filtered = call_cols_filter(spectra, straight, mirrored, tables, columns)
    filtered = lax.all_to_all(filtered, SECOND, split_axis=0, concat_axis=0, tiled=True)
    products = call_rows_inverse(filtered, tables, columns)
    got = lax.ppermute(products[2:4], "core", swap_cores)
    near = jnp.stack([products[0], got[0]])
    far = jnp.stack([products[1], got[1]])

    def exchange(value, step):
        return lax.ppermute(value, ("grp", "ylo"), [(i, i ^ step) for i in range(4)])

    by_grp, by_both, by_row = exchange(near, 2), exchange(far, 3), exchange(far, 1)
    return call_assemble(near, by_row, by_grp, by_both)


def solution(mesh):
    fine = Mesh(mesh.devices.reshape((2,) * len(AXES)), AXES)
    rows, cols = AXES[1:3], AXES[3:]
    placed = (P("grp", rows, cols), P("grp", rows, cols), P(), P(), P())
    return jax.shard_map(on_device, mesh=fine, in_specs=placed, out_specs=P(rows, cols), check_vma=False)
```

```python
import math

import jax
import jax.numpy as jnp
import ml_dtypes
import numpy as np
from jax import lax
from jax.experimental import pallas as pl
from jax.experimental.pallas import tpu as pltpu
from jax.sharding import Mesh
from jax.sharding import PartitionSpec as P

NBAND = 2
NSHELL = 12
F32 = jnp.float32
BF16 = jnp.bfloat16
C1, C2, C3 = math.cos(math.pi / 8), math.cos(math.pi / 4), math.cos(3 * math.pi / 8)
LIMIT = 48 * 1024 * 1024
GROUP = 16
SCALE = 1.0 / (2048.0 * 2048.0)


def split_table(table):
    high = table.astype(ml_dtypes.bfloat16)
    low = (table - high.astype(np.float64)).astype(ml_dtypes.bfloat16)
    return high, low


def rows_tables():
    j = np.arange(128)
    t = np.arange(64)
    forward, inverse = [], []

    def interleave(real_part, imag_part):
        stacked = np.stack([real_part.reshape(4, 16, 128), imag_part.reshape(4, 16, 128)], axis=1)
        return stacked.reshape(128, 128)

    for s in (0, 8):
        theta = 2 * np.pi * (((s + 16 * t)[:, None] * j[None, :]) % 2048) / 2048
        cos, sin = np.cos(theta), -np.sin(theta)
        weight = np.full((64, 1), 2.0)
        if s == 0:
            sin[0] = 1.0 - 2.0 * (j % 2)
            weight[0] = 1.0
        forward.append(interleave(cos, sin))
        inverse.append(SCALE * interleave(weight * cos, weight * sin).T)
    return np.stack(forward), np.stack(inverse)


def cols_tables():
    j = np.arange(128)
    theta = 2 * np.pi * ((j[:, None] * j[None, :]) % 128) / 128
    cos, sin = np.cos(theta), np.sin(theta)
    forward = np.block([[cos, -sin], [sin, cos]])
    inverse = np.block([[cos, sin], [-sin, cos]])
    angle = 2 * np.pi * (np.arange(16)[:, None] * j[None, :]) / 2048
    twiddle = np.stack([np.cos(angle), -np.sin(angle)], axis=1).astype(np.float32)
    column = np.concatenate([np.cos(angle[:8]), np.sin(angle[:8])], axis=0).T
    return forward, inverse, twiddle, column


AXES = ("grp", "ylo", "core", "x1", "x0", "z1", "z0")
FIRST = ("x1", "x0", "core", "z1", "ylo", "z0")
SECOND = ("core", "z1", "z0", "x1", "x0", "grp", "ylo")


def place_of(order, at):
    place = 0
    for axis in order:
        place = place * 2 + at[axis]
    return place


def block_at(block):
    return {"x1": block >> 3, "x0": (block >> 2) & 1, "z1": (block >> 1) & 1, "z0": block & 1}


def of_group(grp, chunk):
    at = {"grp": grp}
    for axis in reversed(FIRST):
        at[axis] = chunk & 1
        chunk >>= 1
    return place_of(SECOND, at)


def split_value(value):
    high = value.astype(BF16)
    return high, (value - high.astype(F32)).astype(BF16)


def mxu(a, b):
    return jnp.dot(a, b, preferred_element_type=F32)


def table_times(both, value):
    v_high, v_low = split_value(value)
    rows = both.shape[0] // 2
    high, low = both[:rows], both[rows:]
    return mxu(jnp.concatenate([high, high, low], axis=1), jnp.concatenate([v_high, v_low, v_high], axis=0))


def times_table(value, both):
    v_high, v_low = split_value(value)
    high, low = both[:256], both[256:]
    return mxu(jnp.concatenate([v_high, v_low, v_high], axis=1), jnp.concatenate([high, high, low], axis=0))


def fft4(a, b, c, d, sign):
    s0r, s0i = a[0] + c[0], a[1] + c[1]
    s1r, s1i = a[0] - c[0], a[1] - c[1]
    s2r, s2i = b[0] + d[0], b[1] + d[1]
    s3r, s3i = b[0] - d[0], b[1] - d[1]
    rr, ri = -sign * s3i, sign * s3r
    return (
        (s0r + s2r, s0i + s2i),
        (s1r + rr, s1i + ri),
        (s0r - s2r, s0i - s2i),
        (s1r - rr, s1i - ri),
    )


def turn(z, k, sign):
    re, im = z
    k = (k * sign) % 16
    if k == 0:
        return z
    if k == 4:
        return (-im, re)
    if k == 2:
        return ((re - im) * C2, (re + im) * C2)
    if k == 14:
        return ((re + im) * C2, (im - re) * C2)
    if k == 6:
        return ((re + im) * -C2, (re - im) * C2)
    if k == 10:
        return ((im - re) * C2, (re + im) * -C2)
    cos, sin = math.cos(2 * math.pi * k / 16), math.sin(2 * math.pi * k / 16)
    return (re * cos - im * sin, re * sin + im * cos)


def fft16(z, sign):
    out = [None] * 16
    inner = [fft4(z[p], z[p + 4], z[p + 8], z[p + 12], sign) for p in range(4)]
    for k in range(4):
        outer = fft4(*[turn(inner[p][k], p * k, sign) for p in range(4)], sign)
        for q in range(4):
            out[k + 4 * q] = outer[q]
    return out


def diagonals(values, lane):
    for d in (1, 2, 4):
        chosen = (lane & (16 * d)) != 0
        values = [jnp.where(chosen, values[(i + d) % 8], values[i]) for i in range(8)]
    return values


def rows_forward(own, got_members, got_control, tables, columns, out, z_full, z_half):
    first = lax.axis_index("core") == 0
    flip = jnp.where(lax.axis_index("ylo") == 0, 1.0, -1.0).astype(F32)
    for slab in range(16):
        x = []
        for m in range(8):
            at = pl.ds((m % 4) * 128 + slab * 8, 8)
            if m < 4:
                x.append(jnp.where(first, own[at, :], got_control[at, :]))
            else:
                x.append(jnp.where(first, got_members[at, :], own[at, :]))
        e = [x[m] + x[m + 4] for m in range(4)]
        d = [x[m] - x[m + 4] for m in range(4)]
        e02, e13 = e[0] + e[2], e[1] + e[3]
        minus, plus = (d[1] - d[3]) * C2, (d[1] + d[3]) * C2
        a = [None] + [(x[m] - x[8 - m]) * flip for m in range(1, 4)]
        b = [None] + [(x[m] + x[8 - m]) * flip for m in range(1, 4)]
        x0, x4 = x[0] * flip, x[4] * flip
        even, odd = x0 + a[2] * C2, x0 - a[2] * C2
        p1, p3 = a[1] * C1 + a[3] * C3, a[1] * C3 - a[3] * C1
        i_even, i_odd = x4 + b[2] * C2, b[2] * C2 - x4
        q1, q3 = b[1] * C3 + b[3] * C1, b[1] * C1 - b[3] * C3
        rows = pl.ds(slab * 8, 8)
        shifted = pl.ds(128 + slab * 8, 8)
        z_half[0, rows, :] = e02 + e13
        z_half[1, rows, :] = e02 - e13
        values = {
            1: (even + p1, -(i_even + q1)),
            2: (d[0] + minus, -(d[2] + plus)),
            3: (odd + p3, -(i_odd + q3)),
            4: (e[0] - e[2], e[3] - e[1]),
            5: (odd - p3, i_odd - q3),
            6: (d[0] - minus, d[2] - plus),
            7: (even - p1, i_even - q1),
        }
        turns = columns[rows, 0:16]
        for s, (re, im) in values.items():
            cos, sin = turns[:, s : s + 1], turns[:, 8 + s : 9 + s]
            lanes = pl.ds(128 * (s - 1), 128)
            z_full[rows, lanes] = re * cos + im * sin
            z_full[shifted, lanes] = im * cos - re * sin
    for members in ((0,), (1, 2), (3, 4), (5, 6)):
        lanes = pl.ds(128 * members[0], 128 * len(members))
        result = table_times(tables[0:512, :], z_full[:, lanes])
        for k, s in enumerate(members):
            at = 256 * s
            lanes = slice(128 * k, 128 * k + 128)
            for u in range(8):
                out[pl.ds(at + 32 * u, 16), :] = result[16 * u : 16 * u + 16, lanes]
                out[pl.ds(at + 32 * u + 16, 16), :] = result[128 + 16 * u : 144 + 16 * u, lanes]
    for s in range(2):
        out[pl.ds(1792 + 128 * s, 128), :] = table_times(tables[1024:1280, 128 * s : 128 * s + 128], z_half[s])


def front(members, control, tables, columns, pattern, loc, shell_index, own, tables_v, columns_v, straight, mirrored,
          pairs_v, loc_v, shells_v, filters_v, sems):
    core = lax.axis_index("core")
    first = core == 0
    field = pltpu.make_async_copy(members, own, sems.at[0])
    small = [
        pltpu.make_async_copy(pattern, pairs_v, sems.at[3]),
        pltpu.make_async_copy(loc, loc_v, sems.at[4]),
        pltpu.make_async_copy(shell_index, shells_v, sems.at[5]),
    ]
    large = [
        pltpu.make_async_copy(tables, tables_v, sems.at[1]),
        pltpu.make_async_copy(columns, columns_v, sems.at[2]),
    ]
    for copy in small:
        copy.start()

    @pl.when(first)
    def _():
        field.start()

    @pl.when(jnp.logical_not(first))
    def _():
        pltpu.make_async_copy(control, own, sems.at[0]).start()

    for copy in large:
        copy.start()
    for copy in small:
        copy.wait()
    chunk = place_of(FIRST, {axis: lax.axis_index(axis) for axis in FIRST})
    general = chunk < 56
    s = jnp.where(general, (chunk >> 3) + 1, jnp.where(chunk < 60, 0, 8))
    u = jnp.where(general, chunk & 7, (chunk - 56) & 3)
    special = chunk == 56
    from_shell, to_shell = pairs_v[0:1, :], pairs_v[1:2, :]
    hits = to_shell == lax.broadcasted_iota(jnp.int32, (NSHELL, to_shell.shape[1]), 0)
    second = from_shell * NBAND >= NSHELL
    shells = shells_v[...]
    in_second = shells * NBAND >= NSHELL
    filters = [jnp.where(in_second, 0.0, 1.0).astype(F32), jnp.where(in_second, 1.0, 0.0).astype(F32)]
    for band in range(NBAND):
        chosen = second if band else jnp.logical_not(second)
        counts = jnp.sum(jnp.where(jnp.logical_and(hits, chosen), 1.0, 0.0).astype(F32), axis=1, keepdims=True)
        gain = jnp.zeros(shells.shape, F32)
        for shell in range(NSHELL):
            gain = jnp.where(shells == shell, counts[shell : shell + 1, :] * loc_v[:, shell : shell + 1], gain)
        filters.append(gain)
    for f in range(2 * NBAND):
        filters_v[f] = filters[f]
    i = lax.broadcasted_iota(jnp.int32, (16, 16), 0)
    picked = []
    for f in range(2 * NBAND):

        def tile_row(tile):
            return filters_v[f, pl.ds(tile, 1), :]

        here = jnp.where(i < 8, tile_row(2 * u), tile_row(2 * u + 1))
        negated = jnp.where(i < jnp.where(s == 0, 9, 8), tile_row(15 - 2 * u), tile_row(14 - 2 * u))
        negated = jnp.where(jnp.logical_and(i == 0, s == 0), tile_row((16 - 2 * u) & 15), negated)
        picked += [here, negated, jnp.broadcast_to(tile_row(8), (8, 16))]
    picked = jnp.concatenate(picked, axis=0)
    high, rest = split_value(picked)
    middle = (picked - high.astype(F32) - rest.astype(F32)).astype(BF16)
    tile = lax.broadcasted_iota(jnp.int32, (48, 128), 0) & 15
    lane = lax.broadcasted_iota(jnp.int32, (48, 128), 1)
    spread = [tile == (lane >> 3), tile == (((128 - lane) & 127) >> 3), tile == 15 - (lane >> 3)]
    widen = jnp.concatenate([jnp.where(mask, 1.0, 0.0).astype(BF16) for mask in spread], axis=1)
    wide = mxu(jnp.concatenate([high, rest, middle], axis=1), widen)
    first_row = jnp.logical_and(special, lax.broadcasted_iota(jnp.int32, (8, 128), 0) == 0)
    for f in range(2 * NBAND):
        for kind in range(2):
            at = slice(128 + 128 * kind, 256 + 128 * kind)
            top = 40 * f
            gain = 0.5 * (wide[top : top + 16, :128] + wide[top + 16 : top + 32, at])
            other = 0.5 * (wide[top + 32 : top + 40, :128] + wide[top + 32 : top + 40, at])
            straight[kind, f, 0:8] = jnp.where(first_row, 0.5 * (gain[0:8] + other), gain[0:8])
            straight[kind, f, 8:16] = gain[8:16]
            mirrored[kind, f] = jnp.where(first_row, 0.5 * (gain[0:8] - other), 0.0)
    field.wait()
    for copy in large:
        copy.wait()


def cols_filter(received, straight, mirrored, tables, columns, out, z, y, v):
    tw = [(columns[128 + s : 129 + s, :], columns[144 + s : 145 + s, :]) for s in range(16)]

    def put(s, field, at, zr, zi):
        wr, wi = tw[s]
        z[s, field, at, 0:128] = zr * wr - zi * wi
        z[s, field, at, 128:256] = zr * wi + zi * wr

    lane = lax.broadcasted_iota(jnp.int32, (8, 128), 1)
    grp = lax.axis_index("grp")
    shifts = [(16 * (e + grp)) & 127 for e in range(8)]

    def forward(field, half):
        re_at, im_at = pl.ds(8 * half, 8), pl.ds(16 + 8 * half, 8)
        values = []
        for c in range(16):
            one, two = [place_of(FIRST, {"ylo": ylo, "core": field, **block_at(c)}) for ylo in range(2)]
            values.append(
                (received[one, re_at, :] + received[two, re_at, :], received[one, im_at, :] + received[two, im_at, :])
            )
        values = fft16(values, -1)
        for s in range(16):
            put(s, field, re_at, *values[s])
            if half == 0:
                mr, mi = values[(16 - s) % 16]
                put(s, field, pl.ds(16, 8), mr, -mi)

    def spectral(field, group):
        steps = range(16 * group, 16 * group + 16)
        spectrum = times_table(z[pl.ds(steps[0], 16), field].reshape(16 * 24, 256), tables[512:1024, :])
        spectrum = spectrum.reshape(16, 24, 256)
        for f in (2 * field, 2 * field + 1):
            filtered = []
            for step in range(16):
                kind = 0 if steps[step] == 0 else 1
                tile = spectrum[step]
                gain = straight[kind, f]
                mirror = mirrored[kind, f]
                gain = jnp.concatenate([gain, gain], axis=1)
                mirror = jnp.concatenate([mirror, mirror], axis=1)
                top = gain[0:8] * tile[0:8] + mirror * tile[16:24]
                filtered.append(jnp.concatenate([top, gain[8:16] * tile[8:16]], axis=0))
            back = times_table(jnp.concatenate(filtered, axis=0), tables[0:512, :])
            y[pl.ds(steps[0], 16), f] = back.reshape(16, 16, 256)

    def inverse(f, half):
        at = pl.ds(8 * half, 8)
        values = []
        for s in range(16):
            re, im = y[s, f, at, 0:128], y[s, f, at, 128:256]
            wr, wi = tw[s]
            values.append((re * wr + im * wi, im * wr - re * wi))
        values = fft16(values, 1)
        for c in range(16):
            v[f, c, 0, at] = values[c][0]
            v[f, c, 1, at] = values[c][1]

    def send(half, c):
        at = pl.ds(8 * half, 8)
        turned = [pltpu.roll(v[e >> 1, c, e & 1, at], shifts[e], 1) for e in range(8)]
        for i, moved in enumerate(diagonals(turned, lane)):
            q = (-i - grp) & 7
            target = {"grp": q >> 2, "ylo": (q >> 1) & 1, "core": q & 1, **block_at(c)}
            out[place_of(SECOND, target), at, :] = moved

    forward(0, 0)
    forward(0, 1)
    for group in range(16 // GROUP):
        spectral(0, group)
    forward(1, 0)
    forward(1, 1)
    for group in range(16 // GROUP):
        spectral(1, group)
    for f, half in ((0, 0), (1, 0), (0, 1), (1, 1), (2, 0), (3, 0)):
        inverse(f, half)
    for c in range(16):
        send(0, c)
    inverse(2, 1)
    inverse(3, 1)
    for c in range(16):
        send(1, c)


def rows_inverse(received, tables, columns, keep, send, z_full, z_half):
    row = lax.axis_index("ylo") * 2 + lax.axis_index("core")
    mine = lax.axis_index("grp") * 4 + row
    even = ((lax.broadcasted_iota(jnp.int32, (16, 128), 1) - 16 * mine) & 16) == 0

    def chunk(d):
        one, two = received[of_group(0, d)], received[of_group(1, d)]
        return jnp.where(even, one, two), pltpu.roll(jnp.where(even, two, one), 112, 1)

    for members in ((0,), (1, 2), (3, 4), (5, 6)):
        spectra = []
        for s in members:
            parts = [chunk(8 * s + u) for u in range(8)]
            spectra.append(jnp.concatenate([p[0] for p in parts] + [p[1] for p in parts], axis=0))
        result = table_times(tables[512:1024, :], jnp.concatenate(spectra, axis=1))
        for k, s in enumerate(members):
            z_full[s] = result[:, 128 * k : 128 * k + 128]
    for s in range(2):
        parts = [chunk(56 + 4 * s + u) for u in range(4)]
        z_half[s] = table_times(tables[1280:1536, 128 * s : 128 * s + 128], jnp.concatenate([p[k] for p in parts for k in range(2)], axis=0))
    lane = lax.broadcasted_iota(jnp.int32, (8, 128), 1) - 16 * mine
    on_even = (row & 1) == 0
    low64, low32, low16 = (lane & 64) == 0, (lane & 32) == 0, (lane & 16) == 0

    def fold(one, two, low, shift):
        other = jnp.where(low, two, one)
        return jnp.where(low, one, two) + jnp.where(low, pltpu.roll(other, 128 - shift, 1), pltpu.roll(other, shift, 1))

    for slab in range(8):
        x = [fields_of(slab + 8 * h, z_full, z_half, columns) for h in range(2)]
        pieces = []
        for dest in range(4):
            u = []
            for m in range(4 * dest, 4 * dest + 4):
                one, two = x[0][m], x[1][m]
                u.append(jnp.where(low64, one, two) * pltpu.roll(jnp.where(low64, two, one), 64, 1))
            packed = fold(fold(u[0], u[2], low32, 32), fold(u[1], u[3], low32, 32), low16, 16)
            pieces.append(packed)
        for ylo in range(2):
            even_core, odd_core = pieces[2 * ylo], pieces[2 * ylo + 1]
            keep[ylo ^ (row >> 1), pl.ds(slab * 8, 8), :] = jnp.where(on_even, even_core, odd_core)
            send[ylo ^ (row >> 1), pl.ds(slab * 8, 8), :] = jnp.where(on_even, odd_core, even_core)


def fields_of(slab, z_full, z_half, columns):
    rows, shifted = pl.ds(slab * 8, 8), pl.ds(128 + slab * 8, 8)
    y0, y8 = z_half[0, rows, :], z_half[1, rows, :]
    turns = columns[rows, 16:32]
    a, b = [None], [None]
    for s in range(1, 8):
        cos, sin = turns[:, s : s + 1], turns[:, 8 + s : 9 + s]
        re, im = z_full[s - 1, rows, :], z_full[s - 1, shifted, :]
        a.append(re * cos - im * sin)
        b.append(re * sin + im * cos)
    plus, minus = y0 + y8, y0 - y8
    a26, turned = a[2] + a[6], (a[2] - a[6]) * C2
    c_even = [plus + a26 + a[4], minus + turned, plus - a[4], minus - turned, plus - a26 + a[4]]
    p, q, r, t = a[1] - a[7], a[3] - a[5], a[1] + a[7], a[3] + a[5]
    c_odd = [r + t, p * C1 + q * C3, (r - t) * C2, p * C3 - q * C1, None]
    b17, b35, b26 = b[1] + b[7], b[3] + b[5], (b[2] + b[6]) * C2
    d17, d35 = b[1] - b[7], b[3] - b[5]
    s_odd = [None, b17 * C3 + b35 * C1, (d17 + d35) * C2, b17 * C1 - b35 * C3, d17 - d35]
    s_even = [None, b26 + b[4], b[2] - b[6], b26 - b[4], None]
    x = [None] * 16
    x[0], x[8] = c_even[0] + c_odd[0], c_even[0] - c_odd[0]
    x[4], x[12] = c_even[4] - s_odd[4], c_even[4] + s_odd[4]
    for m in range(1, 4):
        c_near, c_far = c_even[m] + c_odd[m], c_even[m] - c_odd[m]
        s_near, s_far = s_odd[m] + s_even[m], s_odd[m] - s_even[m]
        x[m], x[16 - m] = c_near - s_near, c_near + s_near
        x[8 - m], x[8 + m] = c_far - s_far, c_far + s_far
    return x


def assemble(own, by_row, by_grp, by_both, out, pieces, whole, sems):
    mine = (lax.axis_index("grp") * 2 + lax.axis_index("ylo")) * 2 + lax.axis_index("core")
    for k, ref in enumerate((own, by_row, by_grp, by_both)):
        pieces[pl.ds(2 * k, 2)] = ref[...]
    lane = lax.broadcasted_iota(jnp.int32, (8, 128), 1)
    copies = []
    for part in range(2):
        for slab in range(4 * part, 4 * part + 4):
            rows = pl.ds(slab * 8, 8)
            for i, moved in enumerate(diagonals([pieces[q ^ mine, rows, :] for q in range(8)], lane)):
                e = -i % 8
                whole[e & 3, e >> 2, rows, :] = pltpu.roll(moved, 16 * i, 1) if i else moved
        rows = pl.ds(32 * part, 32)
        copy = pltpu.make_async_copy(whole.at[:, :, rows, :], out.at[:, :, rows, :], sems.at[part])
        copy.start()
        copies.append(copy)
    for copy in copies:
        copy.wait()


def in_vmem(count):
    return [pl.BlockSpec(memory_space=pltpu.VMEM)] * count


def in_hbm(*arrays):
    return [pltpu.with_memory_space_constraint(jnp.asarray(x), pltpu.HBM) for x in arrays]


def params():
    return pltpu.CompilerParams(vmem_limit_bytes=LIMIT)


def shape(*dims):
    return jax.ShapeDtypeStruct(dims, F32)


def constant_tables():
    half_f, half_i = [np.concatenate(split_table(t), axis=1) for t in rows_tables()]
    fwd, inv, twiddle, column = cols_tables()
    halves = [np.concatenate([h[0], h[1]], axis=1) for h in (half_f, half_i)]
    tables = np.concatenate([*split_table(inv), *split_table(fwd), *halves], axis=0)
    columns = np.zeros((160, 128), np.float32)
    columns[:128, 0:16] = column
    columns[:128, 16:32] = 2 * SCALE * column
    columns[128:144] = twiddle[:, 0]
    columns[144:160] = twiddle[:, 1]
    return tables, columns


def call_rows_forward(own, got_members, got_control, tables, columns):
    return pl.pallas_call(
        rows_forward,
        out_shape=shape(2048, 128),
        in_specs=in_vmem(5),
        out_specs=in_vmem(1)[0],
        scratch_shapes=[pltpu.VMEM((256, 896), F32), pltpu.VMEM((2, 128, 128), F32)],
        compiler_params=params(),
        name="rows_forward",
    )(own, got_members, got_control, tables, columns)


def call_cols_filter(spectra, straight, mirrored, tables, columns):
    return pl.pallas_call(
        cols_filter,
        out_shape=shape(128, 16, 128),
        in_specs=in_vmem(5),
        out_specs=in_vmem(1)[0],
        scratch_shapes=[
            pltpu.VMEM((16, 2, 24, 256), F32),
            pltpu.VMEM((16, 4, 16, 256), F32),
            pltpu.VMEM((4, 16, 2, 16, 128), F32),
        ],
        compiler_params=params(),
        name="cols_filter",
    )(spectra, straight, mirrored, tables, columns)


def call_rows_inverse(filtered, tables, columns):
    return pl.pallas_call(
        rows_inverse,
        out_shape=(shape(2, 64, 128), shape(2, 64, 128)),
        in_specs=in_vmem(3),
        out_specs=tuple(in_vmem(2)),
        scratch_shapes=[pltpu.VMEM((7, 256, 128), F32), pltpu.VMEM((2, 128, 128), F32)],
        compiler_params=params(),
        name="rows_inverse",
    )(filtered, tables, columns)


def call_assemble(near, by_row, by_grp, by_both):
    return pl.pallas_call(
        assemble,
        out_shape=shape(4, 2, 64, 128),
        in_specs=in_vmem(4),
        out_specs=pl.BlockSpec(memory_space=pltpu.HBM),
        scratch_shapes=[
            pltpu.VMEM((8, 64, 128), F32),
            pltpu.VMEM((4, 2, 64, 128), F32),
            pltpu.SemaphoreType.DMA((2,)),
        ],
        compiler_params=params(),
        name="assemble",
    )(near, by_row, by_grp, by_both).reshape(512, 128)


def call_front(members, control, tables, columns, pattern, loc_spectrum, shell_index):
    return pl.pallas_call(
        front,
        out_shape=(
            shape(512, 128),
            jax.ShapeDtypeStruct(tables.shape, BF16),
            shape(*columns.shape),
            shape(2, 4, 16, 128),
            shape(2, 4, 8, 128),
        ),
        in_specs=[pl.BlockSpec(memory_space=pltpu.HBM)] * 7,
        out_specs=tuple(in_vmem(5)),
        scratch_shapes=[
            pltpu.VMEM((2, pattern.shape[0]), jnp.int32),
            pltpu.VMEM((1, NSHELL), F32),
            pltpu.VMEM(shell_index.shape, jnp.int32),
            pltpu.VMEM((2 * NBAND, *shell_index.shape), F32),
            pltpu.SemaphoreType.DMA((6,)),
        ],
        compiler_params=params(),
        name="front",
    )(*in_hbm(members, control, tables, columns, pattern.T, loc_spectrum.reshape(1, NSHELL), shell_index))


def on_device(members, control, loc_spectrum, pattern, shell_index):
    tables, columns = constant_tables()
    members = members.reshape(512, 128)
    control = control.reshape(512, 128)
    swap_cores = [(0, 1), (1, 0)]
    got_members = lax.ppermute(members, "core", swap_cores)
    got_control = lax.ppermute(control, "core", swap_cores)
    own, tables, columns, straight, mirrored = call_front(
        members, control, tables, columns, pattern, loc_spectrum, shell_index
    )
    spectra = call_rows_forward(own, got_members, got_control, tables, columns)
    spectra = lax.all_to_all(spectra.reshape(64, 32, 128), FIRST, split_axis=0, concat_axis=0, tiled=True)
    filtered = call_cols_filter(spectra, straight, mirrored, tables, columns)
    filtered = lax.all_to_all(filtered, SECOND, split_axis=0, concat_axis=0, tiled=True)
    keep, send = call_rows_inverse(filtered, tables, columns)
    got = lax.ppermute(send, "core", swap_cores)
    near = jnp.stack([keep[0], got[0]])
    far = jnp.stack([keep[1], got[1]])

    def exchange(value, step):
        return lax.ppermute(value, ("grp", "ylo"), [(i, i ^ step) for i in range(4)])

    by_grp, by_both, by_row = exchange(near, 2), exchange(far, 3), exchange(far, 1)
    return call_assemble(near, by_row, by_grp, by_both)


def solution(mesh):
    fine = Mesh(mesh.devices.reshape((2,) * len(AXES)), AXES)
    rows, cols = AXES[1:3], AXES[3:]
    placed = (P("grp", rows, cols), P("grp", rows, cols), P(), P(), P())
    return jax.shard_map(on_device, mesh=fine, in_specs=placed, out_specs=P(rows, cols), check_vma=False)
```

```python
import math

import jax
import jax.numpy as jnp
import ml_dtypes
import numpy as np
from jax import lax
from jax.experimental import pallas as pl
from jax.experimental.pallas import tpu as pltpu
from jax.sharding import Mesh
from jax.sharding import PartitionSpec as P

NBAND = 2
NSHELL = 12
F32 = jnp.float32
BF16 = jnp.bfloat16
C1, C2, C3 = math.cos(math.pi / 8), math.cos(math.pi / 4), math.cos(3 * math.pi / 8)
LIMIT = 48 * 1024 * 1024
GROUP = 16
SCALE = 1.0 / (2048.0 * 2048.0)


def split_table(table):
    high = table.astype(ml_dtypes.bfloat16)
    low = (table - high.astype(np.float64)).astype(ml_dtypes.bfloat16)
    return high, low


def rows_tables():
    j = np.arange(128)
    t = np.arange(64)
    forward, inverse = [], []

    def interleave(real_part, imag_part):
        stacked = np.stack([real_part.reshape(4, 16, 128), imag_part.reshape(4, 16, 128)], axis=1)
        return stacked.reshape(128, 128)

    for s in (0, 8):
        theta = 2 * np.pi * (((s + 16 * t)[:, None] * j[None, :]) % 2048) / 2048
        cos, sin = np.cos(theta), -np.sin(theta)
        weight = np.full((64, 1), 2.0)
        if s == 0:
            sin[0] = 1.0 - 2.0 * (j % 2)
            weight[0] = 1.0
        forward.append(interleave(cos, sin))
        inverse.append(SCALE * interleave(weight * cos, weight * sin).T)
    return np.stack(forward), np.stack(inverse)


def cols_tables():
    j = np.arange(128)
    theta = 2 * np.pi * ((j[:, None] * j[None, :]) % 128) / 128
    cos, sin = np.cos(theta), np.sin(theta)
    forward = np.block([[cos, -sin], [sin, cos]])
    inverse = np.block([[cos, sin], [-sin, cos]])
    angle = 2 * np.pi * (np.arange(16)[:, None] * j[None, :]) / 2048
    twiddle = np.stack([np.cos(angle), -np.sin(angle)], axis=1).astype(np.float32)
    column = np.concatenate([np.cos(angle[:8]), np.sin(angle[:8])], axis=0).T
    return forward, inverse, twiddle, column


AXES = ("grp", "ylo", "core", "x1", "x0", "z1", "z0")
FIRST = ("x0", "x1", "core", "z1", "ylo", "z0")
SECOND = ("core", "z1", "z0", "x1", "x0", "grp", "ylo")


def place_of(order, at):
    place = 0
    for axis in order:
        place = place * 2 + at[axis]
    return place


def block_at(block):
    return {"x1": block >> 3, "x0": (block >> 2) & 1, "z1": (block >> 1) & 1, "z0": block & 1}


def of_group(grp, chunk):
    at = {"grp": grp}
    for axis in reversed(FIRST):
        at[axis] = chunk & 1
        chunk >>= 1
    return place_of(SECOND, at)


def split_value(value):
    high = value.astype(BF16)
    return high, (value - high.astype(F32)).astype(BF16)


def mxu(a, b):
    return jnp.dot(a, b, preferred_element_type=F32)


def table_times(both, value):
    v_high, v_low = split_value(value)
    rows = both.shape[0] // 2
    high, low = both[:rows], both[rows:]
    return mxu(jnp.concatenate([high, high, low], axis=1), jnp.concatenate([v_high, v_low, v_high], axis=0))


def times_table(value, both):
    v_high, v_low = split_value(value)
    high, low = both[:256], both[256:]
    return mxu(jnp.concatenate([v_high, v_low, v_high], axis=1), jnp.concatenate([high, high, low], axis=0))


def fft4(a, b, c, d, sign):
    s0r, s0i = a[0] + c[0], a[1] + c[1]
    s1r, s1i = a[0] - c[0], a[1] - c[1]
    s2r, s2i = b[0] + d[0], b[1] + d[1]
    s3r, s3i = b[0] - d[0], b[1] - d[1]
    rr, ri = -sign * s3i, sign * s3r
    return (
        (s0r + s2r, s0i + s2i),
        (s1r + rr, s1i + ri),
        (s0r - s2r, s0i - s2i),
        (s1r - rr, s1i - ri),
    )


def turn(z, k, sign):
    re, im = z
    k = (k * sign) % 16
    if k == 0:
        return z
    if k == 4:
        return (-im, re)
    if k == 2:
        return ((re - im) * C2, (re + im) * C2)
    if k == 14:
        return ((re + im) * C2, (im - re) * C2)
    if k == 6:
        return ((re + im) * -C2, (re - im) * C2)
    if k == 10:
        return ((im - re) * C2, (re + im) * -C2)
    cos, sin = math.cos(2 * math.pi * k / 16), math.sin(2 * math.pi * k / 16)
    return (re * cos - im * sin, re * sin + im * cos)


def fft16(z, sign):
    out = [None] * 16
    inner = [fft4(z[p], z[p + 4], z[p + 8], z[p + 12], sign) for p in range(4)]
    for k in range(4):
        outer = fft4(*[turn(inner[p][k], p * k, sign) for p in range(4)], sign)
        for q in range(4):
            out[k + 4 * q] = outer[q]
    return out


def diagonals(values, lane):
    for d in (1, 2, 4):
        chosen = (lane & (16 * d)) != 0
        values = [jnp.where(chosen, values[(i + d) % 8], values[i]) for i in range(8)]
    return values


def rows_forward(own, got_members, got_control, tables, columns, out, z_full, z_half):
    first = lax.axis_index("core") == 0
    flip = jnp.where(lax.axis_index("ylo") == 0, 1.0, -1.0).astype(F32)
    for slab in range(16):
        x = []
        for m in range(8):
            at = pl.ds((m % 4) * 128 + slab * 8, 8)
            if m < 4:
                x.append(jnp.where(first, own[at, :], got_control[at, :]))
            else:
                x.append(jnp.where(first, got_members[at, :], own[at, :]))
        e = [x[m] + x[m + 4] for m in range(4)]
        d = [x[m] - x[m + 4] for m in range(4)]
        e02, e13 = e[0] + e[2], e[1] + e[3]
        minus, plus = (d[1] - d[3]) * C2, (d[1] + d[3]) * C2
        a = [None] + [(x[m] - x[8 - m]) * flip for m in range(1, 4)]
        b = [None] + [(x[m] + x[8 - m]) * flip for m in range(1, 4)]
        x0, x4 = x[0] * flip, x[4] * flip
        even, odd = x0 + a[2] * C2, x0 - a[2] * C2
        p1, p3 = a[1] * C1 + a[3] * C3, a[1] * C3 - a[3] * C1
        i_even, i_odd = x4 + b[2] * C2, b[2] * C2 - x4
        q1, q3 = b[1] * C3 + b[3] * C1, b[1] * C1 - b[3] * C3
        rows = pl.ds(slab * 8, 8)
        shifted = pl.ds(128 + slab * 8, 8)
        z_half[0, rows, :] = e02 + e13
        z_half[1, rows, :] = e02 - e13
        values = {
            1: (even + p1, -(i_even + q1)),
            2: (d[0] + minus, -(d[2] + plus)),
            3: (odd + p3, -(i_odd + q3)),
            4: (e[0] - e[2], e[3] - e[1]),
            5: (odd - p3, i_odd - q3),
            6: (d[0] - minus, d[2] - plus),
            7: (even - p1, i_even - q1),
        }
        turns = columns[rows, 0:16]
        for s, (re, im) in values.items():
            cos, sin = turns[:, s : s + 1], turns[:, 8 + s : 9 + s]
            lanes = pl.ds(128 * (s - 1), 128)
            z_full[rows, lanes] = re * cos + im * sin
            z_full[shifted, lanes] = im * cos - re * sin
    for members in ((0,), (1, 2), (3, 4), (5, 6)):
        lanes = pl.ds(128 * members[0], 128 * len(members))
        result = table_times(tables[0:512, :], z_full[:, lanes])
        for k, s in enumerate(members):
            at = 256 * s
            lanes = slice(128 * k, 128 * k + 128)
            for u in range(8):
                out[pl.ds(at + 32 * u, 16), :] = result[16 * u : 16 * u + 16, lanes]
                out[pl.ds(at + 32 * u + 16, 16), :] = result[128 + 16 * u : 144 + 16 * u, lanes]
    for s in range(2):
        out[pl.ds(1792 + 128 * s, 128), :] = table_times(tables[1024:1280, 128 * s : 128 * s + 128], z_half[s])


def front(members, control, tables, columns, pattern, loc, shell_index, own, tables_v, columns_v, straight, mirrored,
          pairs_v, loc_v, shells_v, filters_v, sems):
    core = lax.axis_index("core")
    first = core == 0
    field = pltpu.make_async_copy(members, own, sems.at[0])
    small = [
        pltpu.make_async_copy(pattern, pairs_v, sems.at[3]),
        pltpu.make_async_copy(loc, loc_v, sems.at[4]),
        pltpu.make_async_copy(shell_index, shells_v, sems.at[5]),
    ]
    large = [
        pltpu.make_async_copy(tables, tables_v, sems.at[1]),
        pltpu.make_async_copy(columns, columns_v, sems.at[2]),
    ]
    for copy in small:
        copy.start()

    @pl.when(first)
    def _():
        field.start()

    @pl.when(jnp.logical_not(first))
    def _():
        pltpu.make_async_copy(control, own, sems.at[0]).start()

    for copy in large:
        copy.start()
    for copy in small:
        copy.wait()
    chunk = place_of(FIRST, {axis: lax.axis_index(axis) for axis in FIRST})
    general = chunk < 56
    s = jnp.where(general, (chunk >> 3) + 1, jnp.where(chunk < 60, 0, 8))
    u = jnp.where(general, chunk & 7, (chunk - 56) & 3)
    special = chunk == 56
    from_shell, to_shell = pairs_v[0:1, :], pairs_v[1:2, :]
    hits = to_shell == lax.broadcasted_iota(jnp.int32, (NSHELL, to_shell.shape[1]), 0)
    second = from_shell * NBAND >= NSHELL
    shells = shells_v[...]
    in_second = shells * NBAND >= NSHELL
    filters = [jnp.where(in_second, 0.0, 1.0).astype(F32), jnp.where(in_second, 1.0, 0.0).astype(F32)]
    for band in range(NBAND):
        chosen = second if band else jnp.logical_not(second)
        counts = jnp.sum(jnp.where(jnp.logical_and(hits, chosen), 1.0, 0.0).astype(F32), axis=1, keepdims=True)
        gain = jnp.zeros(shells.shape, F32)
        for shell in range(NSHELL):
            gain = jnp.where(shells == shell, counts[shell : shell + 1, :] * loc_v[:, shell : shell + 1], gain)
        filters.append(gain)
    for f in range(2 * NBAND):
        filters_v[f] = filters[f]
    i = lax.broadcasted_iota(jnp.int32, (16, 16), 0)
    picked = []
    for f in range(2 * NBAND):

        def tile_row(tile):
            return filters_v[f, pl.ds(tile, 1), :]

        here = jnp.where(i < 8, tile_row(2 * u), tile_row(2 * u + 1))
        negated = jnp.where(i < jnp.where(s == 0, 9, 8), tile_row(15 - 2 * u), tile_row(14 - 2 * u))
        negated = jnp.where(jnp.logical_and(i == 0, s == 0), tile_row((16 - 2 * u) & 15), negated)
        picked += [here, negated, jnp.broadcast_to(tile_row(8), (8, 16))]
    picked = jnp.concatenate(picked, axis=0)
    high, rest = split_value(picked)
    middle = (picked - high.astype(F32) - rest.astype(F32)).astype(BF16)
    tile = lax.broadcasted_iota(jnp.int32, (48, 128), 0) & 15
    lane = lax.broadcasted_iota(jnp.int32, (48, 128), 1)
    spread = [tile == (lane >> 3), tile == (((128 - lane) & 127) >> 3), tile == 15 - (lane >> 3)]
    widen = jnp.concatenate([jnp.where(mask, 1.0, 0.0).astype(BF16) for mask in spread], axis=1)
    wide = mxu(jnp.concatenate([high, rest, middle], axis=1), widen)
    first_row = jnp.logical_and(special, lax.broadcasted_iota(jnp.int32, (8, 128), 0) == 0)
    for f in range(2 * NBAND):
        for kind in range(2):
            at = slice(128 + 128 * kind, 256 + 128 * kind)
            top = 40 * f
            gain = 0.5 * (wide[top : top + 16, :128] + wide[top + 16 : top + 32, at])
            other = 0.5 * (wide[top + 32 : top + 40, :128] + wide[top + 32 : top + 40, at])
            straight[kind, f, 0:8] = jnp.where(first_row, 0.5 * (gain[0:8] + other), gain[0:8])
            straight[kind, f, 8:16] = gain[8:16]
            mirrored[kind, f] = jnp.where(first_row, 0.5 * (gain[0:8] - other), 0.0)
    field.wait()
    for copy in large:
        copy.wait()


def cols_filter(received, straight, mirrored, tables, columns, out, z, y, v):
    tw = [(columns[128 + s : 129 + s, :], columns[144 + s : 145 + s, :]) for s in range(16)]

    def put(s, field, at, zr, zi):
        wr, wi = tw[s]
        z[s, field, at, 0:128] = zr * wr - zi * wi
        z[s, field, at, 128:256] = zr * wi + zi * wr

    lane = lax.broadcasted_iota(jnp.int32, (8, 128), 1)
    grp = lax.axis_index("grp")
    shifts = [(16 * (e + grp)) & 127 for e in range(8)]

    def forward(field, half):
        re_at, im_at = pl.ds(8 * half, 8), pl.ds(16 + 8 * half, 8)
        values = []
        for c in range(16):
            one, two = [place_of(FIRST, {"ylo": ylo, "core": field, **block_at(c)}) for ylo in range(2)]
            values.append(
                (received[one, re_at, :] + received[two, re_at, :], received[one, im_at, :] + received[two, im_at, :])
            )
        values = fft16(values, -1)
        for s in range(16):
            put(s, field, re_at, *values[s])
            if half == 0:
                mr, mi = values[(16 - s) % 16]
                put(s, field, pl.ds(16, 8), mr, -mi)

    def spectral(field, group):
        steps = range(16 * group, 16 * group + 16)
        spectrum = times_table(z[pl.ds(steps[0], 16), field].reshape(16 * 24, 256), tables[512:1024, :])
        spectrum = spectrum.reshape(16, 24, 256)
        for f in (2 * field, 2 * field + 1):
            filtered = []
            for step in range(16):
                kind = 0 if steps[step] == 0 else 1
                tile = spectrum[step]
                gain = straight[kind, f]
                mirror = mirrored[kind, f]
                gain = jnp.concatenate([gain, gain], axis=1)
                mirror = jnp.concatenate([mirror, mirror], axis=1)
                top = gain[0:8] * tile[0:8] + mirror * tile[16:24]
                filtered.append(jnp.concatenate([top, gain[8:16] * tile[8:16]], axis=0))
            back = times_table(jnp.concatenate(filtered, axis=0), tables[0:512, :])
            y[pl.ds(steps[0], 16), f] = back.reshape(16, 16, 256)

    def inverse(f, half):
        at = pl.ds(8 * half, 8)
        values = []
        for s in range(16):
            re, im = y[s, f, at, 0:128], y[s, f, at, 128:256]
            wr, wi = tw[s]
            values.append((re * wr + im * wi, im * wr - re * wi))
        values = fft16(values, 1)
        for c in range(16):
            v[f, c, 0, at] = values[c][0]
            v[f, c, 1, at] = values[c][1]

    def send(half, c):
        at = pl.ds(8 * half, 8)
        turned = [pltpu.roll(v[e >> 1, c, e & 1, at], shifts[e], 1) for e in range(8)]
        for i, moved in enumerate(diagonals(turned, lane)):
            q = (-i - grp) & 7
            target = {"grp": q >> 2, "ylo": (q >> 1) & 1, "core": q & 1, **block_at(c)}
            out[place_of(SECOND, target), at, :] = moved

    forward(0, 0)
    forward(0, 1)
    for group in range(16 // GROUP):
        spectral(0, group)
    forward(1, 0)
    forward(1, 1)
    for group in range(16 // GROUP):
        spectral(1, group)
    for f, half in ((0, 0), (1, 0), (0, 1), (1, 1), (2, 0), (3, 0)):
        inverse(f, half)
    for c in range(16):
        send(0, c)
    inverse(2, 1)
    inverse(3, 1)
    for c in range(16):
        send(1, c)


def rows_inverse(received, tables, columns, out, z_full, z_half):
    row = lax.axis_index("ylo") * 2 + lax.axis_index("core")
    mine = lax.axis_index("grp") * 4 + row
    even = ((lax.broadcasted_iota(jnp.int32, (16, 128), 1) - 16 * mine) & 16) == 0

    def chunk(d):
        one, two = received[of_group(0, d)], received[of_group(1, d)]
        return jnp.where(even, one, two), pltpu.roll(jnp.where(even, two, one), 112, 1)

    for members in ((0,), (1, 2), (3, 4), (5, 6)):
        spectra = []
        for s in members:
            parts = [chunk(8 * s + u) for u in range(8)]
            spectra.append(jnp.concatenate([p[0] for p in parts] + [p[1] for p in parts], axis=0))
        result = table_times(tables[512:1024, :], jnp.concatenate(spectra, axis=1))
        for k, s in enumerate(members):
            z_full[s] = result[:, 128 * k : 128 * k + 128]
    for s in range(2):
        parts = [chunk(56 + 4 * s + u) for u in range(4)]
        z_half[s] = table_times(tables[1280:1536, 128 * s : 128 * s + 128], jnp.concatenate([p[k] for p in parts for k in range(2)], axis=0))
    lane = lax.broadcasted_iota(jnp.int32, (8, 128), 1) - 16 * mine
    low64, low32, low16 = (lane & 64) == 0, (lane & 32) == 0, (lane & 16) == 0

    def fold(one, two, low, shift):
        other = jnp.where(low, two, one)
        return jnp.where(low, one, two) + jnp.where(low, pltpu.roll(other, 128 - shift, 1), pltpu.roll(other, shift, 1))

    for slab in range(8):
        x = [fields_of(slab + 8 * h, z_full, z_half, columns) for h in range(2)]
        for dest in range(4):
            u = []
            for m in range(4 * dest, 4 * dest + 4):
                one, two = x[0][m], x[1][m]
                u.append(jnp.where(low64, one, two) * pltpu.roll(jnp.where(low64, two, one), 64, 1))
            packed = fold(fold(u[0], u[2], low32, 32), fold(u[1], u[3], low32, 32), low16, 16)
            slot = dest ^ row
            out[((slot & 1) << 1) | (slot >> 1), pl.ds(slab * 8, 8), :] = packed


def fields_of(slab, z_full, z_half, columns):
    rows, shifted = pl.ds(slab * 8, 8), pl.ds(128 + slab * 8, 8)
    y0, y8 = z_half[0, rows, :], z_half[1, rows, :]
    turns = columns[rows, 16:32]
    a, b = [None], [None]
    for s in range(1, 8):
        cos, sin = turns[:, s : s + 1], turns[:, 8 + s : 9 + s]
        re, im = z_full[s - 1, rows, :], z_full[s - 1, shifted, :]
        a.append(re * cos - im * sin)
        b.append(re * sin + im * cos)
    plus, minus = y0 + y8, y0 - y8
    a26, turned = a[2] + a[6], (a[2] - a[6]) * C2
    c_even = [plus + a26 + a[4], minus + turned, plus - a[4], minus - turned, plus - a26 + a[4]]
    p, q, r, t = a[1] - a[7], a[3] - a[5], a[1] + a[7], a[3] + a[5]
    c_odd = [r + t, p * C1 + q * C3, (r - t) * C2, p * C3 - q * C1, None]
    b17, b35, b26 = b[1] + b[7], b[3] + b[5], (b[2] + b[6]) * C2
    d17, d35 = b[1] - b[7], b[3] - b[5]
    s_odd = [None, b17 * C3 + b35 * C1, (d17 + d35) * C2, b17 * C1 - b35 * C3, d17 - d35]
    s_even = [None, b26 + b[4], b[2] - b[6], b26 - b[4], None]
    x = [None] * 16
    x[0], x[8] = c_even[0] + c_odd[0], c_even[0] - c_odd[0]
    x[4], x[12] = c_even[4] - s_odd[4], c_even[4] + s_odd[4]
    for m in range(1, 4):
        c_near, c_far = c_even[m] + c_odd[m], c_even[m] - c_odd[m]
        s_near, s_far = s_odd[m] + s_even[m], s_odd[m] - s_even[m]
        x[m], x[16 - m] = c_near - s_near, c_near + s_near
        x[8 - m], x[8 + m] = c_far - s_far, c_far + s_far
    return x


def assemble(own, by_row, by_grp, by_both, out, pieces, whole, sems):
    mine = (lax.axis_index("grp") * 2 + lax.axis_index("ylo")) * 2 + lax.axis_index("core")
    for k, ref in enumerate((own, by_row, by_grp, by_both)):
        pieces[pl.ds(2 * k, 2)] = ref[...]
    lane = lax.broadcasted_iota(jnp.int32, (8, 128), 1)
    copies = []
    for part in range(2):
        for slab in range(4 * part, 4 * part + 4):
            rows = pl.ds(slab * 8, 8)
            for i, moved in enumerate(diagonals([pieces[q ^ mine, rows, :] for q in range(8)], lane)):
                e = -i % 8
                whole[e & 3, e >> 2, rows, :] = pltpu.roll(moved, 16 * i, 1) if i else moved
        rows = pl.ds(32 * part, 32)
        copy = pltpu.make_async_copy(whole.at[:, :, rows, :], out.at[:, :, rows, :], sems.at[part])
        copy.start()
        copies.append(copy)
    for copy in copies:
        copy.wait()


def in_vmem(count):
    return [pl.BlockSpec(memory_space=pltpu.VMEM)] * count


def in_hbm(*arrays):
    return [pltpu.with_memory_space_constraint(jnp.asarray(x), pltpu.HBM) for x in arrays]


def params():
    return pltpu.CompilerParams(vmem_limit_bytes=LIMIT)


def shape(*dims):
    return jax.ShapeDtypeStruct(dims, F32)


def constant_tables():
    half_f, half_i = [np.concatenate(split_table(t), axis=1) for t in rows_tables()]
    fwd, inv, twiddle, column = cols_tables()
    halves = [np.concatenate([h[0], h[1]], axis=1) for h in (half_f, half_i)]
    tables = np.concatenate([*split_table(inv), *split_table(fwd), *halves], axis=0)
    columns = np.zeros((160, 128), np.float32)
    columns[:128, 0:16] = column
    columns[:128, 16:32] = 2 * SCALE * column
    columns[128:144] = twiddle[:, 0]
    columns[144:160] = twiddle[:, 1]
    return tables, columns


def call_rows_forward(own, got_members, got_control, tables, columns):
    return pl.pallas_call(
        rows_forward,
        out_shape=shape(2048, 128),
        in_specs=in_vmem(5),
        out_specs=in_vmem(1)[0],
        scratch_shapes=[pltpu.VMEM((256, 896), F32), pltpu.VMEM((2, 128, 128), F32)],
        compiler_params=params(),
        name="rows_forward",
    )(own, got_members, got_control, tables, columns)


def call_cols_filter(spectra, straight, mirrored, tables, columns):
    return pl.pallas_call(
        cols_filter,
        out_shape=shape(128, 16, 128),
        in_specs=in_vmem(5),
        out_specs=in_vmem(1)[0],
        scratch_shapes=[
            pltpu.VMEM((16, 2, 24, 256), F32),
            pltpu.VMEM((16, 4, 16, 256), F32),
            pltpu.VMEM((4, 16, 2, 16, 128), F32),
        ],
        compiler_params=params(),
        name="cols_filter",
    )(spectra, straight, mirrored, tables, columns)


def call_rows_inverse(filtered, tables, columns):
    return pl.pallas_call(
        rows_inverse,
        out_shape=shape(4, 64, 128),
        in_specs=in_vmem(3),
        out_specs=in_vmem(1)[0],
        scratch_shapes=[pltpu.VMEM((7, 256, 128), F32), pltpu.VMEM((2, 128, 128), F32)],
        compiler_params=params(),
        name="rows_inverse",
    )(filtered, tables, columns)


def call_assemble(near, by_row, by_grp, by_both):
    return pl.pallas_call(
        assemble,
        out_shape=shape(4, 2, 64, 128),
        in_specs=in_vmem(4),
        out_specs=pl.BlockSpec(memory_space=pltpu.HBM),
        scratch_shapes=[
            pltpu.VMEM((8, 64, 128), F32),
            pltpu.VMEM((4, 2, 64, 128), F32),
            pltpu.SemaphoreType.DMA((2,)),
        ],
        compiler_params=params(),
        name="assemble",
    )(near, by_row, by_grp, by_both).reshape(512, 128)


def call_front(members, control, tables, columns, pattern, loc_spectrum, shell_index):
    return pl.pallas_call(
        front,
        out_shape=(
            shape(512, 128),
            jax.ShapeDtypeStruct(tables.shape, BF16),
            shape(*columns.shape),
            shape(2, 4, 16, 128),
            shape(2, 4, 8, 128),
        ),
        in_specs=[pl.BlockSpec(memory_space=pltpu.HBM)] * 7,
        out_specs=tuple(in_vmem(5)),
        scratch_shapes=[
            pltpu.VMEM((2, pattern.shape[0]), jnp.int32),
            pltpu.VMEM((1, NSHELL), F32),
            pltpu.VMEM(shell_index.shape, jnp.int32),
            pltpu.VMEM((2 * NBAND, *shell_index.shape), F32),
            pltpu.SemaphoreType.DMA((6,)),
        ],
        compiler_params=params(),
        name="front",
    )(*in_hbm(members, control, tables, columns, pattern.T, loc_spectrum.reshape(1, NSHELL), shell_index))


def on_device(members, control, loc_spectrum, pattern, shell_index):
    tables, columns = constant_tables()
    members = members.reshape(512, 128)
    control = control.reshape(512, 128)
    swap_cores = [(0, 1), (1, 0)]
    got_members = lax.ppermute(members, "core", swap_cores)
    got_control = lax.ppermute(control, "core", swap_cores)
    own, tables, columns, straight, mirrored = call_front(
        members, control, tables, columns, pattern, loc_spectrum, shell_index
    )
    spectra = call_rows_forward(own, got_members, got_control, tables, columns)
    spectra = lax.all_to_all(spectra.reshape(64, 32, 128), FIRST, split_axis=0, concat_axis=0, tiled=True)
    filtered = call_cols_filter(spectra, straight, mirrored, tables, columns)
    filtered = lax.all_to_all(filtered, SECOND, split_axis=0, concat_axis=0, tiled=True)
    products = call_rows_inverse(filtered, tables, columns)
    got = lax.ppermute(products[2:4], "core", swap_cores)
    near = jnp.stack([products[0], got[0]])
    far = jnp.stack([products[1], got[1]])

    def exchange(value, step):
        return lax.ppermute(value, ("grp", "ylo"), [(i, i ^ step) for i in range(4)])

    by_grp, by_both, by_row = exchange(near, 2), exchange(far, 3), exchange(far, 1)
    return call_assemble(near, by_row, by_grp, by_both)


def solution(mesh):
    fine = Mesh(mesh.devices.reshape((2,) * len(AXES)), AXES)
    rows, cols = AXES[1:3], AXES[3:]
    placed = (P("grp", rows, cols), P("grp", rows, cols), P(), P(), P())
    return jax.shard_map(on_device, mesh=fine, in_specs=placed, out_specs=P(rows, cols), check_vma=False)
```

```python
import math

import jax
import jax.numpy as jnp
import ml_dtypes
import numpy as np
from jax import lax
from jax.experimental import pallas as pl
from jax.experimental.pallas import tpu as pltpu
from jax.sharding import Mesh
from jax.sharding import PartitionSpec as P

NBAND = 2
NSHELL = 12
F32 = jnp.float32
BF16 = jnp.bfloat16
C1, C2, C3 = math.cos(math.pi / 8), math.cos(math.pi / 4), math.cos(3 * math.pi / 8)
LIMIT = 48 * 1024 * 1024
GROUP = 16
SCALE = 1.0 / (2048.0 * 2048.0)


def split_table(table):
    high = table.astype(ml_dtypes.bfloat16)
    low = (table - high.astype(np.float64)).astype(ml_dtypes.bfloat16)
    return high, low


def rows_tables():
    j = np.arange(128)
    t = np.arange(64)
    forward, inverse = [], []

    def interleave(real_part, imag_part):
        stacked = np.stack([real_part.reshape(4, 16, 128), imag_part.reshape(4, 16, 128)], axis=1)
        return stacked.reshape(128, 128)

    for s in (0, 8):
        theta = 2 * np.pi * (((s + 16 * t)[:, None] * j[None, :]) % 2048) / 2048
        cos, sin = np.cos(theta), -np.sin(theta)
        weight = np.full((64, 1), 2.0)
        if s == 0:
            sin[0] = 1.0 - 2.0 * (j % 2)
            weight[0] = 1.0
        forward.append(interleave(cos, sin))
        inverse.append(SCALE * interleave(weight * cos, weight * sin).T)
    return np.stack(forward), np.stack(inverse)


def cols_tables():
    j = np.arange(128)
    theta = 2 * np.pi * ((j[:, None] * j[None, :]) % 128) / 128
    cos, sin = np.cos(theta), np.sin(theta)
    forward = np.block([[cos, -sin], [sin, cos]])
    inverse = np.block([[cos, sin], [-sin, cos]])
    angle = 2 * np.pi * (np.arange(16)[:, None] * j[None, :]) / 2048
    twiddle = np.stack([np.cos(angle), -np.sin(angle)], axis=1).astype(np.float32)
    column = np.concatenate([np.cos(angle[:8]), np.sin(angle[:8])], axis=0).T
    return forward, inverse, twiddle, column


AXES = ("grp", "ylo", "core", "x1", "x0", "z1", "z0")
FIRST = ("x1", "x0", "core", "z1", "ylo", "z0")
SECOND = ("core", "z1", "z0", "x1", "x0", "grp", "ylo")


def place_of(order, at):
    place = 0
    for axis in order:
        place = place * 2 + at[axis]
    return place


def block_at(block):
    return {"x1": block >> 3, "x0": (block >> 2) & 1, "z1": (block >> 1) & 1, "z0": block & 1}


def of_group(grp, chunk):
    at = {"grp": grp}
    for axis in reversed(FIRST):
        at[axis] = chunk & 1
        chunk >>= 1
    return place_of(SECOND, at)


def split_value(value):
    high = value.astype(BF16)
    return high, (value - high.astype(F32)).astype(BF16)


def mxu(a, b):
    return jnp.dot(a, b, preferred_element_type=F32)


def table_times(both, value):
    v_high, v_low = split_value(value)
    rows = both.shape[0] // 2
    high, low = both[:rows], both[rows:]
    return mxu(jnp.concatenate([high, high, low], axis=1), jnp.concatenate([v_high, v_low, v_high], axis=0))


def times_table(value, both):
    v_high, v_low = split_value(value)
    high, low = both[:256], both[256:]
    return mxu(jnp.concatenate([v_high, v_low, v_high], axis=1), jnp.concatenate([high, high, low], axis=0))


def fft4(a, b, c, d, sign):
    s0r, s0i = a[0] + c[0], a[1] + c[1]
    s1r, s1i = a[0] - c[0], a[1] - c[1]
    s2r, s2i = b[0] + d[0], b[1] + d[1]
    s3r, s3i = b[0] - d[0], b[1] - d[1]
    rr, ri = -sign * s3i, sign * s3r
    return (
        (s0r + s2r, s0i + s2i),
        (s1r + rr, s1i + ri),
        (s0r - s2r, s0i - s2i),
        (s1r - rr, s1i - ri),
    )


def turn(z, k, sign):
    re, im = z
    k = (k * sign) % 16
    if k == 0:
        return z
    if k == 4:
        return (-im, re)
    if k == 2:
        return ((re - im) * C2, (re + im) * C2)
    if k == 14:
        return ((re + im) * C2, (im - re) * C2)
    if k == 6:
        return ((re + im) * -C2, (re - im) * C2)
    if k == 10:
        return ((im - re) * C2, (re + im) * -C2)
    cos, sin = math.cos(2 * math.pi * k / 16), math.sin(2 * math.pi * k / 16)
    return (re * cos - im * sin, re * sin + im * cos)


def fft16(z, sign):
    out = [None] * 16
    inner = [fft4(z[p], z[p + 4], z[p + 8], z[p + 12], sign) for p in range(4)]
    for k in range(4):
        outer = fft4(*[turn(inner[p][k], p * k, sign) for p in range(4)], sign)
        for q in range(4):
            out[k + 4 * q] = outer[q]
    return out


def diagonals(values, lane):
    for d in (1, 2, 4):
        chosen = (lane & (16 * d)) != 0
        values = [jnp.where(chosen, values[(i + d) % 8], values[i]) for i in range(8)]
    return values


def rows_forward(own, got_members, got_control, tables, columns, out, z_full, z_half):
    first = lax.axis_index("core") == 0
    flip = jnp.where(lax.axis_index("ylo") == 0, 1.0, -1.0).astype(F32)
    for slab in range(16):
        x = []
        for m in range(8):
            at = pl.ds((m % 4) * 128 + slab * 8, 8)
            if m < 4:
                x.append(jnp.where(first, own[at, :], got_control[at, :]))
            else:
                x.append(jnp.where(first, got_members[at, :], own[at, :]))
        e = [x[m] + x[m + 4] for m in range(4)]
        d = [x[m] - x[m + 4] for m in range(4)]
        e02, e13 = e[0] + e[2], e[1] + e[3]
        minus, plus = (d[1] - d[3]) * C2, (d[1] + d[3]) * C2
        a = [None] + [(x[m] - x[8 - m]) * flip for m in range(1, 4)]
        b = [None] + [(x[m] + x[8 - m]) * flip for m in range(1, 4)]
        x0, x4 = x[0] * flip, x[4] * flip
        even, odd = x0 + a[2] * C2, x0 - a[2] * C2
        p1, p3 = a[1] * C1 + a[3] * C3, a[1] * C3 - a[3] * C1
        i_even, i_odd = x4 + b[2] * C2, b[2] * C2 - x4
        q1, q3 = b[1] * C3 + b[3] * C1, b[1] * C1 - b[3] * C3
        rows = pl.ds(slab * 8, 8)
        shifted = pl.ds(128 + slab * 8, 8)
        z_half[0, rows, :] = e02 + e13
        z_half[1, rows, :] = e02 - e13
        values = {
            1: (even + p1, -(i_even + q1)),
            2: (d[0] + minus, -(d[2] + plus)),
            3: (odd + p3, -(i_odd + q3)),
            4: (e[0] - e[2], e[3] - e[1]),
            5: (odd - p3, i_odd - q3),
            6: (d[0] - minus, d[2] - plus),
            7: (even - p1, i_even - q1),
        }
        turns = columns[rows, 0:16]
        for s, (re, im) in values.items():
            cos, sin = turns[:, s : s + 1], turns[:, 8 + s : 9 + s]
            lanes = pl.ds(128 * (s - 1), 128)
            z_full[rows, lanes] = re * cos + im * sin
            z_full[shifted, lanes] = im * cos - re * sin
    for members in ((0,), (1, 2), (3, 4), (5, 6)):
        lanes = pl.ds(128 * members[0], 128 * len(members))
        result = table_times(tables[0:512, :], z_full[:, lanes])
        for k, s in enumerate(members):
            at = 256 * s
            lanes = slice(128 * k, 128 * k + 128)
            for u in range(8):
                out[pl.ds(at + 32 * u, 16), :] = result[16 * u : 16 * u + 16, lanes]
                out[pl.ds(at + 32 * u + 16, 16), :] = result[128 + 16 * u : 144 + 16 * u, lanes]
    for s in range(2):
        out[pl.ds(1792 + 128 * s, 128), :] = table_times(tables[1024:1280, 128 * s : 128 * s + 128], z_half[s])


def front(members, control, tables, columns, pattern, loc, shell_index, own, tables_v, columns_v, straight, mirrored,
          pairs_v, loc_v, shells_v, filters_v, sems):
    core = lax.axis_index("core")
    first = core == 0
    field = pltpu.make_async_copy(members, own, sems.at[0])
    small = [
        pltpu.make_async_copy(pattern, pairs_v, sems.at[3]),
        pltpu.make_async_copy(loc, loc_v, sems.at[4]),
        pltpu.make_async_copy(shell_index, shells_v, sems.at[5]),
    ]
    large = [
        pltpu.make_async_copy(tables, tables_v, sems.at[1]),
        pltpu.make_async_copy(columns, columns_v, sems.at[2]),
    ]
    for copy in small:
        copy.start()

    @pl.when(first)
    def _():
        field.start()

    @pl.when(jnp.logical_not(first))
    def _():
        pltpu.make_async_copy(control, own, sems.at[0]).start()

    for copy in large:
        copy.start()
    for copy in small:
        copy.wait()
    chunk = place_of(FIRST, {axis: lax.axis_index(axis) for axis in FIRST})
    general = chunk < 56
    s = jnp.where(general, (chunk >> 3) + 1, jnp.where(chunk < 60, 0, 8))
    u = jnp.where(general, chunk & 7, (chunk - 56) & 3)
    special = chunk == 56
    from_shell, to_shell = pairs_v[0:1, :], pairs_v[1:2, :]
    hits = to_shell == lax.broadcasted_iota(jnp.int32, (NSHELL, to_shell.shape[1]), 0)
    second = from_shell * NBAND >= NSHELL
    shells = shells_v[...]
    in_second = shells * NBAND >= NSHELL
    filters = [jnp.where(in_second, 0.0, 1.0).astype(F32), jnp.where(in_second, 1.0, 0.0).astype(F32)]
    for band in range(NBAND):
        chosen = second if band else jnp.logical_not(second)
        counts = jnp.sum(jnp.where(jnp.logical_and(hits, chosen), 1.0, 0.0).astype(F32), axis=1, keepdims=True)
        gain = jnp.zeros(shells.shape, F32)
        for shell in range(NSHELL):
            gain = jnp.where(shells == shell, counts[shell : shell + 1, :] * loc_v[:, shell : shell + 1], gain)
        filters.append(gain)
    for f in range(2 * NBAND):
        filters_v[f] = filters[f]
    i = lax.broadcasted_iota(jnp.int32, (16, 16), 0)
    picked = []
    for f in range(2 * NBAND):

        def tile_row(tile):
            return filters_v[f, pl.ds(tile, 1), :]

        here = jnp.where(i < 8, tile_row(2 * u), tile_row(2 * u + 1))
        negated = jnp.where(i < jnp.where(s == 0, 9, 8), tile_row(15 - 2 * u), tile_row(14 - 2 * u))
        negated = jnp.where(jnp.logical_and(i == 0, s == 0), tile_row((16 - 2 * u) & 15), negated)
        picked += [here, negated, jnp.broadcast_to(tile_row(8), (8, 16))]
    picked = jnp.concatenate(picked, axis=0)
    high, rest = split_value(picked)
    middle = (picked - high.astype(F32) - rest.astype(F32)).astype(BF16)
    tile = lax.broadcasted_iota(jnp.int32, (48, 128), 0) & 15
    lane = lax.broadcasted_iota(jnp.int32, (48, 128), 1)
    spread = [tile == (lane >> 3), tile == (((128 - lane) & 127) >> 3), tile == 15 - (lane >> 3)]
    widen = jnp.concatenate([jnp.where(mask, 1.0, 0.0).astype(BF16) for mask in spread], axis=1)
    wide = mxu(jnp.concatenate([high, rest, middle], axis=1), widen)
    first_row = jnp.logical_and(special, lax.broadcasted_iota(jnp.int32, (8, 128), 0) == 0)
    for f in range(2 * NBAND):
        for kind in range(2):
            at = slice(128 + 128 * kind, 256 + 128 * kind)
            top = 40 * f
            gain = 0.5 * (wide[top : top + 16, :128] + wide[top + 16 : top + 32, at])
            other = 0.5 * (wide[top + 32 : top + 40, :128] + wide[top + 32 : top + 40, at])
            straight[kind, f, 0:8] = jnp.where(first_row, 0.5 * (gain[0:8] + other), gain[0:8])
            straight[kind, f, 8:16] = gain[8:16]
            mirrored[kind, f] = jnp.where(first_row, 0.5 * (gain[0:8] - other), 0.0)
    field.wait()
    for copy in large:
        copy.wait()


def cols_filter(received, straight, mirrored, tables, columns, out, z, y, v):
    tw = [(columns[128 + s : 129 + s, :], columns[144 + s : 145 + s, :]) for s in range(16)]

    def put(s, field, at, zr, zi):
        wr, wi = tw[s]
        z[s, field, at, 0:128] = zr * wr - zi * wi
        z[s, field, at, 128:256] = zr * wi + zi * wr

    lane = lax.broadcasted_iota(jnp.int32, (8, 128), 1)
    grp = lax.axis_index("grp")
    shifts = [(16 * (e + grp)) & 127 for e in range(8)]

    def forward(field, half):
        re_at, im_at = pl.ds(8 * half, 8), pl.ds(16 + 8 * half, 8)
        values = []
        for c in range(16):
            one, two = [place_of(FIRST, {"ylo": ylo, "core": field, **block_at(c)}) for ylo in range(2)]
            values.append(
                (received[one, re_at, :] + received[two, re_at, :], received[one, im_at, :] + received[two, im_at, :])
            )
        values = fft16(values, -1)
        for s in range(16):
            put(s, field, re_at, *values[s])
            if half == 0:
                mr, mi = values[(16 - s) % 16]
                put(s, field, pl.ds(16, 8), mr, -mi)

    def spectral(field, group):
        steps = range(16 * group, 16 * group + 16)
        spectrum = times_table(z[pl.ds(steps[0], 16), field].reshape(16 * 24, 256), tables[512:1024, :])
        spectrum = spectrum.reshape(16, 24, 256)
        for f in (2 * field, 2 * field + 1):
            filtered = []
            for step in range(16):
                kind = 0 if steps[step] == 0 else 1
                tile = spectrum[step]
                gain = straight[kind, f]
                mirror = mirrored[kind, f]
                gain = jnp.concatenate([gain, gain], axis=1)
                mirror = jnp.concatenate([mirror, mirror], axis=1)
                top = gain[0:8] * tile[0:8] + mirror * tile[16:24]
                filtered.append(jnp.concatenate([top, gain[8:16] * tile[8:16]], axis=0))
            back = times_table(jnp.concatenate(filtered, axis=0), tables[0:512, :])
            y[pl.ds(steps[0], 16), f] = back.reshape(16, 16, 256)

    def inverse(f, half):
        at = pl.ds(8 * half, 8)
        values = []
        for s in range(16):
            re, im = y[s, f, at, 0:128], y[s, f, at, 128:256]
            wr, wi = tw[s]
            values.append((re * wr + im * wi, im * wr - re * wi))
        values = fft16(values, 1)
        for c in range(16):
            v[f, c, 0, at] = values[c][0]
            v[f, c, 1, at] = values[c][1]

    def send(half, c):
        at = pl.ds(8 * half, 8)
        turned = [pltpu.roll(v[e >> 1, c, e & 1, at], shifts[e], 1) for e in range(8)]
        for i, moved in enumerate(diagonals(turned, lane)):
            q = (-i - grp) & 7
            target = {"grp": q >> 2, "ylo": (q >> 1) & 1, "core": q & 1, **block_at(c)}
            out[place_of(SECOND, target), at, :] = moved

    forward(0, 0)
    forward(0, 1)
    for group in range(16 // GROUP):
        spectral(0, group)
    forward(1, 0)
    forward(1, 1)
    for group in range(16 // GROUP):
        spectral(1, group)
    for f, half in ((0, 0), (1, 0), (0, 1), (1, 1), (2, 0), (3, 0)):
        inverse(f, half)
    for c in range(16):
        send(0, c)
    inverse(2, 1)
    inverse(3, 1)
    for c in range(16):
        send(1, c)


def rows_inverse(received, tables, columns, out, z_full, z_half):
    row = lax.axis_index("ylo") * 2 + lax.axis_index("core")
    mine = lax.axis_index("grp") * 4 + row
    even = ((lax.broadcasted_iota(jnp.int32, (16, 128), 1) - 16 * mine) & 16) == 0

    def chunk(d):
        one, two = received[of_group(0, d)], received[of_group(1, d)]
        return jnp.where(even, one, two), pltpu.roll(jnp.where(even, two, one), 112, 1)

    for members in ((0,), (1, 2), (3, 4), (5, 6)):
        spectra = []
        for s in members:
            parts = [chunk(8 * s + u) for u in range(8)]
            spectra.append(jnp.concatenate([p[0] for p in parts] + [p[1] for p in parts], axis=0))
        result = table_times(tables[512:1024, :], jnp.concatenate(spectra, axis=1))
        for k, s in enumerate(members):
            z_full[s] = result[:, 128 * k : 128 * k + 128]
    for s in range(2):
        parts = [chunk(56 + 4 * s + u) for u in range(4)]
        z_half[s] = table_times(tables[1280:1536, 128 * s : 128 * s + 128], jnp.concatenate([p[k] for p in parts for k in range(2)], axis=0))
    lane = lax.broadcasted_iota(jnp.int32, (8, 128), 1) - 16 * mine
    low64, low32, low16 = (lane & 64) == 0, (lane & 32) == 0, (lane & 16) == 0

    def fold(one, two, low, shift):
        other = jnp.where(low, two, one)
        return jnp.where(low, one, two) + jnp.where(low, pltpu.roll(other, 128 - shift, 1), pltpu.roll(other, shift, 1))

    for slab in range(8):
        x = [fields_of(slab + 8 * h, z_full, z_half, columns) for h in range(2)]
        for dest in range(4):
            u = []
            for m in range(4 * dest, 4 * dest + 4):
                one, two = x[0][m], x[1][m]
                u.append(jnp.where(low64, one, two) * pltpu.roll(jnp.where(low64, two, one), 64, 1))
            packed = fold(fold(u[0], u[2], low32, 32), fold(u[1], u[3], low32, 32), low16, 16)
            slot = dest ^ row
            out[((slot & 1) << 1) | (slot >> 1), pl.ds(slab * 8, 8), :] = packed


def fields_of(slab, z_full, z_half, columns):
    rows, shifted = pl.ds(slab * 8, 8), pl.ds(128 + slab * 8, 8)
    y0, y8 = z_half[0, rows, :], z_half[1, rows, :]
    turns = columns[rows, 16:32]
    a, b = [None], [None]
    for s in range(1, 8):
        cos, sin = turns[:, s : s + 1], turns[:, 8 + s : 9 + s]
        re, im = z_full[s - 1, rows, :], z_full[s - 1, shifted, :]
        a.append(re * cos - im * sin)
        b.append(re * sin + im * cos)
    plus, minus = y0 + y8, y0 - y8
    a26, turned = a[2] + a[6], (a[2] - a[6]) * C2
    c_even = [plus + a26 + a[4], minus + turned, plus - a[4], minus - turned, plus - a26 + a[4]]
    p, q, r, t = a[1] - a[7], a[3] - a[5], a[1] + a[7], a[3] + a[5]
    c_odd = [r + t, p * C1 + q * C3, (r - t) * C2, p * C3 - q * C1, None]
    b17, b35, b26 = b[1] + b[7], b[3] + b[5], (b[2] + b[6]) * C2
    d17, d35 = b[1] - b[7], b[3] - b[5]
    s_odd = [None, b17 * C3 + b35 * C1, (d17 + d35) * C2, b17 * C1 - b35 * C3, d17 - d35]
    s_even = [None, b26 + b[4], b[2] - b[6], b26 - b[4], None]
    x = [None] * 16
    x[0], x[8] = c_even[0] + c_odd[0], c_even[0] - c_odd[0]
    x[4], x[12] = c_even[4] - s_odd[4], c_even[4] + s_odd[4]
    for m in range(1, 4):
        c_near, c_far = c_even[m] + c_odd[m], c_even[m] - c_odd[m]
        s_near, s_far = s_odd[m] + s_even[m], s_odd[m] - s_even[m]
        x[m], x[16 - m] = c_near - s_near, c_near + s_near
        x[8 - m], x[8 + m] = c_far - s_far, c_far + s_far
    return x


def assemble(own, by_row, by_grp, by_both, out, pieces, whole, sems):
    mine = (lax.axis_index("grp") * 2 + lax.axis_index("ylo")) * 2 + lax.axis_index("core")
    for k, ref in enumerate((own, by_row, by_grp, by_both)):
        pieces[pl.ds(2 * k, 2)] = ref[...]
    lane = lax.broadcasted_iota(jnp.int32, (8, 128), 1)
    copies = []
    for part in range(4):
        for slab in range(2 * part, 2 * part + 2):
            rows = pl.ds(slab * 8, 8)
            for i, moved in enumerate(diagonals([pieces[q ^ mine, rows, :] for q in range(8)], lane)):
                e = -i % 8
                whole[e & 3, e >> 2, rows, :] = pltpu.roll(moved, 16 * i, 1) if i else moved
        rows = pl.ds(16 * part, 16)
        copy = pltpu.make_async_copy(whole.at[:, :, rows, :], out.at[:, :, rows, :], sems.at[part])
        copy.start()
        copies.append(copy)
    for copy in copies:
        copy.wait()


def in_vmem(count):
    return [pl.BlockSpec(memory_space=pltpu.VMEM)] * count


def in_hbm(*arrays):
    return [pltpu.with_memory_space_constraint(jnp.asarray(x), pltpu.HBM) for x in arrays]


def params():
    return pltpu.CompilerParams(vmem_limit_bytes=LIMIT)


def shape(*dims):
    return jax.ShapeDtypeStruct(dims, F32)


def constant_tables():
    half_f, half_i = [np.concatenate(split_table(t), axis=1) for t in rows_tables()]
    fwd, inv, twiddle, column = cols_tables()
    halves = [np.concatenate([h[0], h[1]], axis=1) for h in (half_f, half_i)]
    tables = np.concatenate([*split_table(inv), *split_table(fwd), *halves], axis=0)
    columns = np.zeros((160, 128), np.float32)
    columns[:128, 0:16] = column
    columns[:128, 16:32] = 2 * SCALE * column
    columns[128:144] = twiddle[:, 0]
    columns[144:160] = twiddle[:, 1]
    return tables, columns


def call_rows_forward(own, got_members, got_control, tables, columns):
    return pl.pallas_call(
        rows_forward,
        out_shape=shape(2048, 128),
        in_specs=in_vmem(5),
        out_specs=in_vmem(1)[0],
        scratch_shapes=[pltpu.VMEM((256, 896), F32), pltpu.VMEM((2, 128, 128), F32)],
        compiler_params=params(),
        name="rows_forward",
    )(own, got_members, got_control, tables, columns)


def call_cols_filter(spectra, straight, mirrored, tables, columns):
    return pl.pallas_call(
        cols_filter,
        out_shape=shape(128, 16, 128),
        in_specs=in_vmem(5),
        out_specs=in_vmem(1)[0],
        scratch_shapes=[
            pltpu.VMEM((16, 2, 24, 256), F32),
            pltpu.VMEM((16, 4, 16, 256), F32),
            pltpu.VMEM((4, 16, 2, 16, 128), F32),
        ],
        compiler_params=params(),
        name="cols_filter",
    )(spectra, straight, mirrored, tables, columns)


def call_rows_inverse(filtered, tables, columns):
    return pl.pallas_call(
        rows_inverse,
        out_shape=shape(4, 64, 128),
        in_specs=in_vmem(3),
        out_specs=in_vmem(1)[0],
        scratch_shapes=[pltpu.VMEM((7, 256, 128), F32), pltpu.VMEM((2, 128, 128), F32)],
        compiler_params=params(),
        name="rows_inverse",
    )(filtered, tables, columns)


def call_assemble(near, by_row, by_grp, by_both):
    return pl.pallas_call(
        assemble,
        out_shape=shape(4, 2, 64, 128),
        in_specs=in_vmem(4),
        out_specs=pl.BlockSpec(memory_space=pltpu.HBM),
        scratch_shapes=[
            pltpu.VMEM((8, 64, 128), F32),
            pltpu.VMEM((4, 2, 64, 128), F32),
            pltpu.SemaphoreType.DMA((4,)),
        ],
        compiler_params=params(),
        name="assemble",
    )(near, by_row, by_grp, by_both).reshape(512, 128)


def call_front(members, control, tables, columns, pattern, loc_spectrum, shell_index):
    return pl.pallas_call(
        front,
        out_shape=(
            shape(512, 128),
            jax.ShapeDtypeStruct(tables.shape, BF16),
            shape(*columns.shape),
            shape(2, 4, 16, 128),
            shape(2, 4, 8, 128),
        ),
        in_specs=[pl.BlockSpec(memory_space=pltpu.HBM)] * 7,
        out_specs=tuple(in_vmem(5)),
        scratch_shapes=[
            pltpu.VMEM((2, pattern.shape[0]), jnp.int32),
            pltpu.VMEM((1, NSHELL), F32),
            pltpu.VMEM(shell_index.shape, jnp.int32),
            pltpu.VMEM((2 * NBAND, *shell_index.shape), F32),
            pltpu.SemaphoreType.DMA((6,)),
        ],
        compiler_params=params(),
        name="front",
    )(*in_hbm(members, control, tables, columns, pattern.T, loc_spectrum.reshape(1, NSHELL), shell_index))


def on_device(members, control, loc_spectrum, pattern, shell_index):
    tables, columns = constant_tables()
    members = members.reshape(512, 128)
    control = control.reshape(512, 128)
    swap_cores = [(0, 1), (1, 0)]
    got_members = lax.ppermute(members, "core", swap_cores)
    got_control = lax.ppermute(control, "core", swap_cores)
    own, tables, columns, straight, mirrored = call_front(
        members, control, tables, columns, pattern, loc_spectrum, shell_index
    )
    spectra = call_rows_forward(own, got_members, got_control, tables, columns)
    spectra = lax.all_to_all(spectra.reshape(64, 32, 128), FIRST, split_axis=0, concat_axis=0, tiled=True)
    filtered = call_cols_filter(spectra, straight, mirrored, tables, columns)
    filtered = lax.all_to_all(filtered, SECOND, split_axis=0, concat_axis=0, tiled=True)
    products = call_rows_inverse(filtered, tables, columns)
    got = lax.ppermute(products[2:4], "core", swap_cores)
    near = jnp.stack([products[0], got[0]])
    far = jnp.stack([products[1], got[1]])

    def exchange(value, step):
        return lax.ppermute(value, ("grp", "ylo"), [(i, i ^ step) for i in range(4)])

    by_grp, by_both, by_row = exchange(near, 2), exchange(far, 3), exchange(far, 1)
    return call_assemble(near, by_row, by_grp, by_both)


def solution(mesh):
    fine = Mesh(mesh.devices.reshape((2,) * len(AXES)), AXES)
    rows, cols = AXES[1:3], AXES[3:]
    placed = (P("grp", rows, cols), P("grp", rows, cols), P(), P(), P())
    return jax.shard_map(on_device, mesh=fine, in_specs=placed, out_specs=P(rows, cols), check_vma=False)
```
